32 devices in a mesh: wide: 8 (over z, y), narrow: 4 (over x, core).
Axes of the slice: x: 2, y: 2, z: 4, core: 2. Of those that a mesh axis runs over, the one named last changes fastest.
Arguments:
- hidden_in: bfloat16 [128, 16384], P('narrow', 'wide'), may hold values from -6 to 6
- attn_gain: float32 [16384], P('wide'), may hold values from 0.1 to 1.9
- w_query: bfloat16 [16384, 16384], P('wide', 'narrow'), may hold values from -0.046875 to 0.046875
- w_key: bfloat16 [16384, 1024], P('wide', 'narrow'), may hold values from -0.046875 to 0.046875
- w_value: bfloat16 [16384, 1024], P('wide', 'narrow'), may hold values from -0.046875 to 0.046875
- w_out: bfloat16 [16384, 16384], P('narrow', 'wide'), may hold values from -0.046875 to 0.046875
- ffn_gain: float32 [16384], P('wide'), may hold values from 0.1 to 1.9
- w_gate: bfloat16 [16384, 8192], P('wide', 'narrow'), may hold values from -0.046875 to 0.046875
- w_up: bfloat16 [16384, 8192], P('wide', 'narrow'), may hold values from -0.046875 to 0.046875
- w_down: bfloat16 [8192, 16384], P('narrow', 'wide'), may hold values from -0.0625 to 0.0625
- key_cache: bfloat16 [128, 512, 1024], P(('wide', 'narrow')), may hold values from -192 to 192
- value_cache: bfloat16 [128, 512, 1024], P(('wide', 'narrow')), may hold values from -6 to 6
- cache_len: int32 [128], P(('wide', 'narrow')), may hold values from 1 to 512, as said below
- bank_row: int32 [128], replicated, may hold values from 0 to 127, each once
Outputs:
- layer_out: bfloat16 [128, 16384], P('narrow', 'wide')
The draws below stay inside these ranges and needn't reach their ends.
Inputs may be any that keep to these rules, and one draw needn't show every extreme that they name: cache_len[b] counts the valid leading positions of bank row b; some row is full.
All inputs are finite; a program needn't handle non-finite values.
Results may differ from the reference program's by a relative error of at most 0.006.
The reference program's roundings to bfloat16 on the way (of `normed`, `probs`, `context`, `resid`, `normed_two` and `hidden_act`) count: a program that leaves them out, or rounds other values in their place, can miss the bound.
Values may be sent and summed in bfloat16 or wider, within the bound.
No kernel may reach another device: no remote copies, remote signals or barrier semaphores. Data moves between devices by JAX's collectives and lax.ppermute only.
A program may use at most 192 MiB of HBM per device.

```python
import math
import jax
import jax.numpy as jnp
from jax import lax

D = 16384
KV_HEADS = 8
HEAD_DIM = 128
FF_SLAB = 8192
CACHE_LEN = 512
ROWS = 128


def draw_key_cache(key, part):
    key = jax.random.fold_in(key, 11)
    full_shape = (ROWS, CACHE_LEN, KV_HEADS * HEAD_DIM)
    noise = jax.random.normal(key, full_shape, jnp.float32)
    return jnp.clip(noise, -4.0, 4.0).astype(jnp.bfloat16)


def draw_cache_len(key, part):
    key = jax.random.fold_in(key, 23)
    ceiling = jax.random.randint(key, (ROWS,), 2, CACHE_LEN + 2)
    offsets = jax.random.randint(jax.random.fold_in(key, 1), (ROWS,), 1, ceiling)
    lengths = CACHE_LEN + 1 - offsets
    return lengths.at[0].set(CACHE_LEN).astype(jnp.int32)


def levels(key, shape, split, smallest, largest):
    def one(dim, shards_of):
        draws = jax.random.uniform(jax.random.fold_in(jax.random.fold_in(key, 6), dim), (shards_of,), jnp.float32, smallest / len(split), largest / len(split))
        return jnp.repeat(jnp.exp(draws), shape[dim] // shards_of).reshape((-1,) + (1,) * (len(shape) - dim - 1))

    gain = one(*split[0])
    for cut in split[1:]:
        gain = gain * one(*cut)
    return gain


def centred(stream_key, dims, deviation, limit, split=(), kind=jnp.bfloat16):
    array = deviation * jax.random.normal(stream_key, dims, jnp.float32)
    if split:
        array = array * levels(stream_key, dims, split, -0.22, 0.18)
    return jnp.clip(array, -limit, limit).astype(kind)


def setup_inputs(seed: int = 0) -> dict:
    streams_of = jax.random.split(jax.random.key(seed), 15)
    hidden_in = centred(streams_of[0], (ROWS, D), 1.0, 6.0, ((0, 4), (1, 8)))
    attn_gain = jnp.clip(1.0 + 0.18 * jax.random.normal(streams_of[1], (D,), jnp.float32), 0.1, 1.9)
    w_query = centred(streams_of[2], (D, D), D ** -0.5, 0.046875, ((0, 8), (1, 4)))
    w_key = centred(streams_of[3], (D, KV_HEADS * HEAD_DIM), D ** -0.5, 0.046875, ((0, 8), (1, 4)))
    w_value = centred(streams_of[4], (D, KV_HEADS * HEAD_DIM), D ** -0.5, 0.046875, ((0, 8), (1, 4)))
    w_out = centred(streams_of[5], (D, D), D ** -0.5, 0.046875, ((0, 4), (1, 8)))
    ffn_gain = jnp.clip(1.0 + 0.18 * jax.random.normal(streams_of[6], (D,), jnp.float32), 0.1, 1.9)
    w_gate = centred(streams_of[7], (D, FF_SLAB), D ** -0.5, 0.046875, ((0, 8), (1, 4)))
    w_up = centred(streams_of[8], (D, FF_SLAB), D ** -0.5, 0.046875, ((0, 8), (1, 4)))
    w_down = centred(streams_of[9], (FF_SLAB, D), FF_SLAB ** -0.5, 0.0625, ((0, 4), (1, 8)))
    key_cache = draw_key_cache(jax.random.fold_in(streams_of[14], 71), 0)
    value_cache = centred(streams_of[11], (ROWS, CACHE_LEN, KV_HEADS * HEAD_DIM), 1.0, 6.0, ((0, 32),))
    cache_len = draw_cache_len(jax.random.fold_in(streams_of[14], 71), 0)
    bank_row = jax.random.permutation(streams_of[13], ROWS).astype(jnp.int32)
    return dict(hidden_in=hidden_in, attn_gain=attn_gain, w_query=w_query, w_key=w_key, w_value=w_value, w_out=w_out, ffn_gain=ffn_gain, w_gate=w_gate, w_up=w_up, w_down=w_down, key_cache=key_cache, value_cache=value_cache, cache_len=cache_len, bank_row=bank_row)


NORM_EPSILON = 1e-05
ROPE_BASE = 500000.0

def rms_rows(values_in, gain_row):
    values = values_in.astype(jnp.float32)
    mean_sq = lax.optimization_barrier(jnp.mean(values * values, axis=1, keepdims=True))
    scaled = values * lax.rsqrt(mean_sq + NORM_EPSILON)
    return (scaled * gain_row.astype(jnp.float32)[None, :]).astype(jnp.bfloat16)

def rotate(head_rows, lengths):
    head_size = head_rows.shape[-1]
    half_size = head_size // 2
    inverse_freq = jnp.exp(jnp.arange(half_size, dtype=jnp.float32) * (-2.0 * math.log(ROPE_BASE) / head_size))
    angles = lengths.astype(jnp.float32)[:, None] * inverse_freq[None, :]
    cos_part = jnp.cos(angles)[:, None, :]
    sin_part = jnp.sin(angles)[:, None, :]
    front_half = head_rows[..., :half_size].astype(jnp.float32)
    back_half = head_rows[..., half_size:].astype(jnp.float32)
    turned = jnp.concatenate([front_half * cos_part - back_half * sin_part, back_half * cos_part + front_half * sin_part], axis=-1)
    return turned.astype(jnp.bfloat16)

def attend_block(row_block):
    queries, fresh_key, fresh_value, key_cache, value_cache, lengths = row_block
    row_count, length, kv_width = key_cache.shape
    groups = kv_width // HEAD_DIM
    group_size = queries.shape[1] // kv_width
    score_scale = 1.0 / math.sqrt(HEAD_DIM)
    query_heads = queries.astype(jnp.float32).reshape(row_count, groups, group_size, HEAD_DIM)
    cache_keys = key_cache.astype(jnp.float32).reshape(row_count, length, groups, HEAD_DIM)
    cache_values = value_cache.astype(jnp.float32).reshape(row_count, length, groups, HEAD_DIM)
    own_key = fresh_key.astype(jnp.float32).reshape(row_count, groups, HEAD_DIM)
    own_value = fresh_value.astype(jnp.float32).reshape(row_count, groups, HEAD_DIM)
    scores = jnp.einsum('rgqd,rlgd->rgql', query_heads, cache_keys) * score_scale
    own_score = jnp.einsum('rgqd,rgd->rgq', query_heads, own_key) * score_scale
    valid_pos = jnp.arange(length, dtype=jnp.int32)[None, :] < lengths[:, None]
    scores = jnp.where(valid_pos[:, None, None, :], scores, -jnp.inf)
    row_max = jnp.maximum(lax.optimization_barrier(jnp.max(scores, axis=3)), own_score)
    weights = jnp.exp(scores - row_max[..., None])
    own_weight = jnp.exp(own_score - row_max)
    weight_sum = lax.optimization_barrier(jnp.sum(weights, axis=3)) + own_weight
    probs = (weights / weight_sum[..., None]).astype(jnp.bfloat16)
    own_prob = (own_weight / weight_sum).astype(jnp.bfloat16)
    context = jnp.einsum('rgql,rlgd->rgqd', probs.astype(jnp.float32), cache_values)
    context = context + own_prob.astype(jnp.float32)[..., None] * own_value[:, :, None, :]
    return context.reshape(row_count, groups * group_size * HEAD_DIM).astype(jnp.bfloat16)

def reference(hidden_in, attn_gain, w_query, w_key, w_value, w_out, ffn_gain, w_gate, w_up, w_down, key_cache, value_cache, cache_len, bank_row):
    row_total = hidden_in.shape[0]
    normed = rms_rows(hidden_in, attn_gain)
    queries = jnp.dot(normed, w_query, preferred_element_type=jnp.float32).astype(jnp.bfloat16)
    key_new = jnp.dot(normed, w_key, preferred_element_type=jnp.float32).astype(jnp.bfloat16)
    value_new = jnp.dot(normed, w_value, preferred_element_type=jnp.float32).astype(jnp.bfloat16)
    served_by = jnp.zeros((row_total,), jnp.int32).at[bank_row].set(jnp.arange(row_total, dtype=jnp.int32))
    query_rot = rotate(queries[served_by].reshape(row_total, -1, HEAD_DIM), cache_len).reshape(row_total, -1)
    key_rot = rotate(key_new[served_by].reshape(row_total, -1, HEAD_DIM), cache_len).reshape(row_total, -1)
    value_bank = value_new[served_by]
    block_rows = 32
    block_count = row_total // block_rows
    members = (query_rot, key_rot, value_bank, key_cache, value_cache, cache_len)
    blocked = tuple((member.reshape((block_count, block_rows) + member.shape[1:]) for member in members))
    context = lax.map(attend_block, blocked).reshape(row_total, -1)
    attn_out = jnp.dot(context[bank_row], w_out, preferred_element_type=jnp.float32)
    resid = (hidden_in.astype(jnp.float32) + attn_out).astype(jnp.bfloat16)
    normed_two = rms_rows(resid, ffn_gain)
    gate_sum = jnp.dot(normed_two, w_gate, preferred_element_type=jnp.float32)
    up_sum = jnp.dot(normed_two, w_up, preferred_element_type=jnp.float32)
    hidden_act = (jax.nn.silu(gate_sum) * up_sum).astype(jnp.bfloat16)
    down_sum = jnp.dot(hidden_act, w_down, preferred_element_type=jnp.float32)
    return (resid.astype(jnp.float32) + down_sum).astype(jnp.bfloat16)
```

```python
import math

import jax
import jax.numpy as jnp
from jax import lax
from jax.experimental import pallas as pl
from jax.experimental.pallas import tpu as pltpu
from jax.sharding import PartitionSpec as P

HEAD_DIM = 128


NORM_EPSILON = 1e-05
ROPE_BASE = 500000.0


def product(left, right):
    return jnp.dot(left, right, preferred_element_type=jnp.float32)


def normalize(values_in, gain_row, sum_sq, model_width):
    mean_sq = sum_sq / model_width
    scaled = values_in.astype(jnp.float32) * lax.rsqrt(mean_sq + NORM_EPSILON)[:, None]
    return (scaled * gain_row[None, :]).astype(jnp.bfloat16)


def rotate(head_rows, lengths):
    head_size = head_rows.shape[-1]
    half_size = head_size // 2
    inverse_freq = jnp.exp(
        jnp.arange(half_size, dtype=jnp.float32) * (-2.0 * math.log(ROPE_BASE) / head_size)
    )
    angles = lengths.astype(jnp.float32)[:, None] * inverse_freq[None, :]
    cos_part = jnp.cos(angles)[:, None, :]
    sin_part = jnp.sin(angles)[:, None, :]
    front_half = head_rows[..., :half_size].astype(jnp.float32)
    back_half = head_rows[..., half_size:].astype(jnp.float32)
    turned = jnp.concatenate(
        [
            front_half * cos_part - back_half * sin_part,
            back_half * cos_part + front_half * sin_part,
        ],
        axis=-1,
    )
    return turned.astype(jnp.bfloat16)


def attend(queries, fresh_key, fresh_value, key_cache, value_cache, lengths):
    row_count, length, kv_width = key_cache.shape
    groups = kv_width // HEAD_DIM
    group_size = queries.shape[1] // kv_width
    score_scale = 1.0 / math.sqrt(HEAD_DIM)
    query_heads = queries.reshape(row_count, groups, group_size, HEAD_DIM)
    cache_keys = key_cache.reshape(row_count, length, groups, HEAD_DIM)
    cache_values = value_cache.reshape(row_count, length, groups, HEAD_DIM)
    own_key = fresh_key.reshape(row_count, groups, HEAD_DIM)
    own_value = fresh_value.reshape(row_count, groups, HEAD_DIM)
    scores = (
        jnp.einsum("rgqd,rlgd->rgql", query_heads, cache_keys, preferred_element_type=jnp.float32)
        * score_scale
    )
    own_score = (
        jnp.einsum("rgqd,rgd->rgq", query_heads, own_key, preferred_element_type=jnp.float32)
        * score_scale
    )
    valid_pos = jnp.arange(length, dtype=jnp.int32)[None, :] < lengths[:, None]
    scores = jnp.where(valid_pos[:, None, None, :], scores, -jnp.inf)
    row_max = jnp.maximum(jnp.max(scores, axis=3), own_score)
    weights = jnp.exp(scores - row_max[..., None])
    own_weight = jnp.exp(own_score - row_max)
    weight_sum = jnp.sum(weights, axis=3) + own_weight
    probs = (weights / weight_sum[..., None]).astype(jnp.bfloat16)
    own_prob = (own_weight / weight_sum).astype(jnp.bfloat16)
    context = jnp.einsum("rgql,rlgd->rgqd", probs, cache_values, preferred_element_type=jnp.float32)
    context = (
        context
        + own_prob.astype(jnp.float32)[..., None] * own_value.astype(jnp.float32)[:, :, None, :]
    )
    return context.reshape(row_count, groups * group_size * HEAD_DIM).astype(jnp.bfloat16)


QKV_CHUNKS = 3
FFN_CHUNKS = 4
CONTEXT_CHUNKS = 2
DOWN_CHUNKS = 2
VMEM_LIMIT = 32 * 1024 * 1024


def swap(block, axis, offset):
    count = lax.axis_size(axis)
    return lax.ppermute(block, axis, [(i, i ^ offset) for i in range(count)])


def project(blocks, order, segments, tile, split, total=None):
    rows = order.shape[0]
    depth = blocks[0].shape[1]
    starts = []
    steps = 0
    for _, _, _, tiles in segments:
        starts.append(steps)
        steps += tiles
    width = steps * tile
    part = rows // split

    def body(*refs):
        block_refs = refs[: len(blocks)]
        order_ref = refs[len(blocks)]
        weight_refs = refs[len(blocks) + 1 : len(blocks) + 1 + len(segments)]
        rest = refs[len(blocks) + 1 + len(segments) :]
        if total is not None:
            total_ref, rest = rest[0], rest[1:]
        out_refs, left_ref = rest[:split], rest[split]
        step = pl.program_id(0)

        @pl.when(step == 0)
        def _():
            stacked = jnp.concatenate([ref[...] for ref in block_refs], axis=0)
            left_ref[...] = jnp.dot(
                order_ref[...], stacked, preferred_element_type=jnp.float32
            ).astype(jnp.bfloat16)

        columns = pl.ds(pl.multiple_of(step * tile, tile), tile)
        for start, (_, _, _, tiles), weight_ref in zip(starts, segments, weight_refs):

            @pl.when((step >= start) & (step < start + tiles))
            def _(weight_ref=weight_ref):
                result = jnp.dot(
                    left_ref[...], weight_ref[...], preferred_element_type=jnp.float32
                )
                if total is not None:
                    result = result + total_ref[:, columns]
                for index, out_ref in enumerate(out_refs):
                    out_ref[:, columns] = result[index * part : (index + 1) * part]

    def whole(array):
        return pl.BlockSpec(array.shape, lambda j: (0,) * array.ndim)

    def weight_spec(start, row_block, first, tiles):
        return pl.BlockSpec(
            (depth, tile),
            lambda j: (row_block, first + jnp.clip(j - start, 0, tiles - 1)),
        )

    operands = list(blocks) + [order] + [segment[0] for segment in segments]
    specs = [whole(block) for block in blocks] + [whole(order)]
    specs += [
        weight_spec(start, row_block, first, tiles)
        for start, (_, row_block, first, tiles) in zip(starts, segments)
    ]
    if total is not None:
        operands.append(total)
        specs.append(whole(total))
    out_shape = [jax.ShapeDtypeStruct((part, width), jnp.float32)] * split
    return pl.pallas_call(
        body,
        grid=(steps,),
        in_specs=specs,
        out_specs=[pl.BlockSpec((part, width), lambda j: (0, 0))] * split,
        out_shape=out_shape,
        scratch_shapes=[pltpu.VMEM((rows, depth), jnp.bfloat16)],
        compiler_params=pltpu.CompilerParams(vmem_limit_bytes=VMEM_LIMIT),
        cost_estimate=pl.CostEstimate(
            flops=2 * rows * depth * (width + rows),
            bytes_accessed=2 * depth * width + 4 * rows * width,
            transcendentals=0,
        ),
    )(*operands)


def one_hot(left, right):
    return (left[:, None] == right[None, :]).astype(jnp.bfloat16)


def wide_scatter(parts, low, high):
    half = jnp.float16
    mine = parts[0]
    for i in range(1, low):
        mine = mine + swap(parts[i].astype(half), "wide", i).astype(jnp.float32)
    rows = mine.shape[0] // high
    mine = mine.reshape(high, rows, -1)
    total = mine[0]
    for j in range(1, high):
        total = total + swap(mine[j].astype(half), "wide", low * j).astype(jnp.float32)
    return total


def wide_gather(block, low, high):
    held = [block] + [swap(block, "wide", low * j) for j in range(1, high)]
    result = list(held)
    for i in range(1, low):
        result += [swap(piece, "wide", i) for piece in held]
    return result


def narrow_scatter(parts, far):
    mine = parts[0] + swap(parts[1], "narrow", 1)
    rows = mine.shape[0] // far
    mine = mine.reshape(far, rows, -1)
    total = mine[0]
    for j in range(1, far):
        total = total + swap(mine[j], "narrow", 2 * j)
    return total


def narrow_gather(block, far):
    held = [block] + [swap(block, "narrow", 2 * j) for j in range(1, far)]
    return held + [swap(piece, "narrow", 1) for piece in held]


def shards(
    hidden_in,
    attn_gain,
    w_query,
    w_key,
    w_value,
    w_out,
    ffn_gain,
    w_gate,
    w_up,
    w_down,
    key_cache,
    value_cache,
    cache_len,
    bank_row,
):
    wide_count = lax.axis_size("wide")
    narrow_count = lax.axis_size("narrow")
    me_wide = lax.axis_index("wide")
    me_narrow = lax.axis_index("narrow")
    high = 4
    low = wide_count // high
    far = narrow_count // 2
    model_width = hidden_in.shape[1] * wide_count
    own_rows = hidden_in.shape[0]
    local_rows = cache_len.shape[0]
    all_rows = bank_row.shape[0]
    wide_rows = all_rows // wide_count

    position = jnp.arange(all_rows, dtype=jnp.int32)
    narrow_offset = position // own_rows
    narrow_offset = narrow_offset // far + 2 * (narrow_offset % far)
    hypothesis = (me_narrow ^ narrow_offset) * own_rows + position % own_rows
    wide_offset = position // wide_rows
    wide_offset = wide_offset // high + low * (wide_offset % high)
    wide_block = me_wide ^ wide_offset
    inner = position % wide_rows
    bank = (wide_block * narrow_count + (me_narrow ^ (inner // local_rows))) * local_rows
    bank = bank + inner % local_rows
    hypothesis_bank = bank_row[hypothesis]
    to_bank = one_hot(bank, hypothesis_bank)
    to_hypothesis = one_hot(hypothesis_bank, bank)
    to_wide = one_hot(wide_block * wide_rows + inner, position)
    from_wide = one_hot(position, wide_block * wide_rows + inner)

    def wide_sum(rows_sq):
        for i in (range(1, low),):
            pair = rows_sq + sum(swap(rows_sq, "wide", j) for j in i)
        return pair + sum(swap(pair, "wide", low * j) for j in range(1, high))

    rows_in = hidden_in.astype(jnp.float32)
    first_sq = wide_sum(jnp.sum(rows_in * rows_in, axis=1))
    normed = normalize(hidden_in, attn_gain, first_sq, model_width)
    row_blocks = narrow_gather(normed, far)

    q_cols = w_query.shape[1]
    k_cols = w_key.shape[1]
    tile = k_cols
    q_tiles = q_cols // tile
    tiles = (q_tiles + 2) // QKV_CHUNKS
    pieces = []
    for chunk in range(QKV_CHUNKS):
        first = chunk * tiles
        segments = [(w_query, 0, first, min(tiles, q_tiles - first))]
        if chunk == QKV_CHUNKS - 1:
            segments += [(w_key, 0, 0, 1), (w_value, 0, 0, 1)]
        pieces.append(wide_scatter(project(row_blocks, to_bank, segments, tile, low), low, high))
    summed = jnp.concatenate(pieces, axis=1).astype(jnp.bfloat16)
    summed = summed.reshape(narrow_count, local_rows, -1, HEAD_DIM)
    turned = [summed[0]] + [swap(summed[j], "narrow", j) for j in range(1, narrow_count)]
    ranks = me_narrow ^ jnp.arange(narrow_count, dtype=jnp.int32)
    turned = jnp.stack(turned)[ranks].transpose(1, 0, 2, 3)
    q_heads = q_cols // HEAD_DIM
    k_heads = k_cols // HEAD_DIM
    query_rot = rotate(
        turned[:, :, :q_heads].reshape(local_rows, -1, HEAD_DIM), cache_len
    ).reshape(local_rows, -1)
    key_rot = rotate(
        turned[:, :, q_heads : q_heads + k_heads].reshape(local_rows, -1, HEAD_DIM), cache_len
    ).reshape(local_rows, -1)
    value_new = turned[:, :, q_heads + k_heads :].reshape(local_rows, -1)
    context = attend(query_rot, key_rot, value_new, key_cache, value_cache, cache_len)
    context = context.reshape(local_rows, narrow_count, -1).transpose(1, 0, 2)[ranks]
    by_heads = [context[0]] + [swap(context[j], "narrow", j) for j in range(1, narrow_count)]

    out_tile = 512
    out_tiles = w_out.shape[1] // out_tile
    depth = w_out.shape[0] // CONTEXT_CHUNKS
    total = None
    for chunk in range(CONTEXT_CHUNKS):
        columns = slice(chunk * depth, (chunk + 1) * depth)
        block = jnp.concatenate([piece[:, columns] for piece in by_heads], axis=0)
        last = chunk == CONTEXT_CHUNKS - 1
        total = project(
            wide_gather(block, low, high),
            to_hypothesis,
            [(w_out, chunk, 0, out_tiles)],
            out_tile,
            2 if last else 1,
            total if total is None else total[0],
        )
    attn_out = narrow_scatter(total, far)
    resid = (rows_in + attn_out).astype(jnp.bfloat16)
    resid_wide = resid.astype(jnp.float32)
    second_sq = wide_sum(jnp.sum(resid_wide * resid_wide, axis=1))
    normed_two = normalize(resid, ffn_gain, second_sq, model_width)
    row_blocks = narrow_gather(normed_two, far)

    f_cols = w_gate.shape[1] // FFN_CHUNKS
    acts = []
    for chunk in range(FFN_CHUNKS):
        sums = wide_scatter(
            project(
                row_blocks,
                to_wide,
                [(w_gate, 0, chunk, 1), (w_up, 0, chunk, 1)],
                f_cols,
                low,
            ),
            low,
            high,
        )
        acts.append((jax.nn.silu(sums[:, :f_cols]) * sums[:, f_cols:]).astype(jnp.bfloat16))
    each = FFN_CHUNKS // DOWN_CHUNKS
    down_tile = 512
    down_tiles = w_down.shape[1] // down_tile
    total = None
    for chunk in range(DOWN_CHUNKS):
        block = jnp.concatenate(acts[chunk * each : (chunk + 1) * each], axis=1)
        last = chunk == DOWN_CHUNKS - 1
        total = project(
            wide_gather(block, low, high),
            from_wide,
            [(w_down, chunk, 0, down_tiles)],
            down_tile,
            2 if last else 1,
            total if total is None else total[0],
        )
    ffn_out = narrow_scatter(total, far)
    return (resid_wide + ffn_out).astype(jnp.bfloat16)


def solution(mesh):
    return jax.shard_map(
        shards,
        mesh=mesh,
        in_specs=(
            P("narrow", "wide"),
            P("wide"),
            P("wide", "narrow"),
            P("wide", "narrow"),
            P("wide", "narrow"),
            P("narrow", "wide"),
            P("wide"),
            P("wide", "narrow"),
            P("wide", "narrow"),
            P("narrow", "wide"),
            P(("wide", "narrow"), None, None),
            P(("wide", "narrow"), None, None),
            P(("wide", "narrow")),
            P(),
        ),
        out_specs=P("narrow", "wide"),
        check_vma=False,
    )
```

```python
import math

import jax
import jax.numpy as jnp
from jax import lax
from jax.experimental import pallas as pl
from jax.experimental.pallas import tpu as pltpu
from jax.sharding import PartitionSpec as P

HEAD_DIM = 128


NORM_EPSILON = 1e-05
ROPE_BASE = 500000.0


def product(left, right):
    return jnp.dot(left, right, preferred_element_type=jnp.float32)


def normalize(values_in, gain_row, sum_sq, model_width):
    mean_sq = sum_sq / model_width
    scaled = values_in.astype(jnp.float32) * lax.rsqrt(mean_sq + NORM_EPSILON)[:, None]
    return (scaled * gain_row[None, :]).astype(jnp.bfloat16)


def rotate(head_rows, lengths):
    head_size = head_rows.shape[-1]
    half_size = head_size // 2
    inverse_freq = jnp.exp(
        jnp.arange(half_size, dtype=jnp.float32) * (-2.0 * math.log(ROPE_BASE) / head_size)
    )
    angles = lengths.astype(jnp.float32)[:, None] * inverse_freq[None, :]
    cos_part = jnp.cos(angles)[:, None, :]
    sin_part = jnp.sin(angles)[:, None, :]
    front_half = head_rows[..., :half_size].astype(jnp.float32)
    back_half = head_rows[..., half_size:].astype(jnp.float32)
    turned = jnp.concatenate(
        [
            front_half * cos_part - back_half * sin_part,
            back_half * cos_part + front_half * sin_part,
        ],
        axis=-1,
    )
    return turned.astype(jnp.bfloat16)


def attend(queries, fresh_key, fresh_value, key_cache, value_cache, lengths):
    row_count, length, kv_width = key_cache.shape
    groups = kv_width // HEAD_DIM
    group_size = queries.shape[1] // kv_width
    score_scale = 1.0 / math.sqrt(HEAD_DIM)
    query_heads = queries.reshape(row_count, groups, group_size, HEAD_DIM)
    cache_keys = key_cache.reshape(row_count, length, groups, HEAD_DIM)
    cache_values = value_cache.reshape(row_count, length, groups, HEAD_DIM)
    own_key = fresh_key.reshape(row_count, groups, HEAD_DIM)
    own_value = fresh_value.reshape(row_count, groups, HEAD_DIM)
    scores = (
        jnp.einsum("rgqd,rlgd->rgql", query_heads, cache_keys, preferred_element_type=jnp.float32)
        * score_scale
    )
    own_score = (
        jnp.einsum("rgqd,rgd->rgq", query_heads, own_key, preferred_element_type=jnp.float32)
        * score_scale
    )
    valid_pos = jnp.arange(length, dtype=jnp.int32)[None, :] < lengths[:, None]
    scores = jnp.where(valid_pos[:, None, None, :], scores, -jnp.inf)
    row_max = jnp.maximum(jnp.max(scores, axis=3), own_score)
    weights = jnp.exp(scores - row_max[..., None])
    own_weight = jnp.exp(own_score - row_max)
    weight_sum = jnp.sum(weights, axis=3) + own_weight
    probs = (weights / weight_sum[..., None]).astype(jnp.bfloat16)
    own_prob = (own_weight / weight_sum).astype(jnp.bfloat16)
    context = jnp.einsum("rgql,rlgd->rgqd", probs, cache_values, preferred_element_type=jnp.float32)
    context = (
        context
        + own_prob.astype(jnp.float32)[..., None] * own_value.astype(jnp.float32)[:, :, None, :]
    )
    return context.reshape(row_count, groups * group_size * HEAD_DIM).astype(jnp.bfloat16)


QKV_CHUNKS = 3
FFN_CHUNKS = 2
CONTEXT_CHUNKS = 2
NARROW_KINDS = [jnp.float32] + [jnp.bfloat16] * 8
TILE = 512
STAND_IN = 3
MIB = 1024 * 1024


def swap(block, axis, offset):
    count = lax.axis_size(axis)
    return lax.ppermute(block, axis, [(i, i ^ offset) for i in range(count)])


def strides_of(axis):
    count = lax.axis_size(axis)
    return [1 << bit for bit in range(count.bit_length() - 1)]


def offsets_of(axis):
    order = [0]
    for stride in reversed(strides_of(axis)):
        order = order + [offset ^ stride for offset in order]
    return order


def project(pieces, order, segments, split, room, total=None):
    rows = order.shape[0]
    depth = pieces[0].shape[1]
    tiles = []
    width = 0
    for index, (_, first_row, first, columns) in enumerate(segments):
        for start in range(first, first + columns, TILE):
            tile = min(TILE, first + columns - start)
            tiles.append((index, first_row, start, tile, width))
            width += tile
    part = rows // split
    count = len(pieces)

    def body(*refs):
        piece_refs, order_ref, rest = refs[:count], refs[count], refs[count + 1 :]
        weight_refs, rest = rest[: len(segments)], rest[len(segments) :]
        if total is not None:
            total_ref, rest = rest[0], rest[1:]
        out_refs = rest[:split]
        stacked = jnp.concatenate([ref[...] for ref in piece_refs], axis=0)
        left = jnp.dot(order_ref[...], stacked, preferred_element_type=jnp.float32)
        left = left.astype(jnp.bfloat16)
        for index, first_row, start, tile, base in tiles:
            weight = weight_refs[index][pl.ds(first_row, depth), pl.ds(start, tile)]
            result = jnp.dot(left, weight, preferred_element_type=jnp.float32)
            if total is not None:
                result = result + total_ref[:, base : base + tile]
            for index, out_ref in enumerate(out_refs):
                out_ref[:, base : base + tile] = result[index * part : (index + 1) * part]

    operands = list(pieces) + [order] + [segment[0] for segment in segments]
    in_vmem = pl.BlockSpec(memory_space=pltpu.VMEM)
    specs = [in_vmem] * (count + 1) + [in_vmem] * len(segments)
    if total is not None:
        operands.append(total)
        specs.append(in_vmem)
    return pl.pallas_call(
        body,
        in_specs=specs,
        out_specs=[in_vmem] * split,
        out_shape=[jax.ShapeDtypeStruct((part, width), jnp.float32)] * split,
        compiler_params=pltpu.CompilerParams(vmem_limit_bytes=room * MIB),
        cost_estimate=pl.CostEstimate(
            flops=2 * rows * depth * (width + rows),
            bytes_accessed=2 * depth * width + 4 * rows * width,
            transcendentals=0,
        ),
    )(*operands)


def stand_in(after, microseconds):
    def body(after_ref, zero_ref):
        zero_ref[...] = jnp.zeros_like(zero_ref)

    zero = pl.pallas_call(
        body,
        in_specs=[pl.BlockSpec(memory_space=pl.ANY)],
        out_specs=pl.BlockSpec(memory_space=pltpu.VMEM),
        out_shape=jax.ShapeDtypeStruct((8, 128), jnp.float32),
        compiler_params=pltpu.CompilerParams(vmem_limit_bytes=MIB),
        cost_estimate=pl.CostEstimate(
            flops=int(1.1e9 * microseconds), bytes_accessed=4096, transcendentals=0
        ),
    )(after)
    return zero[0, 0]


def one_hot(left, right):
    return (left[:, None] == right[None, :]).astype(jnp.bfloat16)


def wide_scatter(kept, sent, kind):
    strides = strides_of("wide")
    rows = 2 * kept.shape[0] // lax.axis_size("wide")
    kept = kept + swap(sent.astype(kind), "wide", strides[0]).astype(jnp.float32)
    total = kept[:rows] + stand_in(kept, STAND_IN)
    for place, offset in enumerate(offsets_of("wide")[: kept.shape[0] // rows]):
        if offset:
            block = kept[place * rows : (place + 1) * rows].astype(kind)
            total = total + swap(block, "wide", offset).astype(jnp.float32)
    return total


def narrow_scatter(kept, sent):
    for stride, kind in zip(strides_of("narrow"), NARROW_KINDS):
        if stride > 1:
            half = kept.shape[0] // 2
            kept, sent = kept[:half], kept[half:]
        kept = kept + swap(sent.astype(kind), "narrow", stride).astype(jnp.float32)
    return kept


def gather(block, axis):
    strides = strides_of(axis)[::-1]
    for stride in strides[:-1]:
        block = jnp.concatenate([block, swap(block, axis, stride)], axis=0)
    return [block, swap(block, axis, strides[-1])]


def gather_direct(block, axis):
    offsets = offsets_of(axis)
    held = [block] + [swap(block, axis, o) for o in offsets[1 : len(offsets) // 2]]
    return held + [swap(piece, axis, 1) for piece in held]


def exchange(blocks, axis):
    blocks = list(blocks)
    for stride in strides_of(axis)[::-1]:
        marked = [i for i in range(len(blocks)) if i & stride]
        arrived = swap(jnp.stack([blocks[i] for i in marked]), axis, stride)
        for place, i in enumerate(marked):
            blocks[i] = arrived[place]
    return blocks


def shards(
    hidden_in,
    attn_gain,
    w_query,
    w_key,
    w_value,
    w_out,
    ffn_gain,
    w_gate,
    w_up,
    w_down,
    key_cache,
    value_cache,
    cache_len,
    bank_row,
):
    wide_count = lax.axis_size("wide")
    narrow_count = lax.axis_size("narrow")
    me_wide = lax.axis_index("wide")
    me_narrow = lax.axis_index("narrow")
    model_width = hidden_in.shape[1] * wide_count
    own_rows = hidden_in.shape[0]
    local_rows = cache_len.shape[0]
    all_rows = bank_row.shape[0]
    wide_rows = all_rows // wide_count

    position = jnp.arange(all_rows, dtype=jnp.int32)

    def devices(axis, me):
        offsets = jnp.array(offsets_of(axis), jnp.int32)
        return jnp.repeat(me ^ offsets, all_rows // len(offsets_of(axis)))

    hypothesis = devices("narrow", me_narrow) * own_rows + position % own_rows
    inner = position % wide_rows
    wide_block = devices("wide", me_wide)
    bank = (wide_block * narrow_count + (me_narrow ^ (inner // local_rows))) * local_rows
    bank = bank + inner % local_rows
    hypothesis_bank = bank_row[hypothesis]
    to_bank = one_hot(bank, hypothesis_bank)
    to_hypothesis = one_hot(hypothesis_bank, bank)
    to_wide = one_hot(wide_block * wide_rows + inner, position)
    from_wide = one_hot(position, wide_block * wide_rows + inner)

    def wide_sum(rows_sq):
        for stride in strides_of("wide"):
            arrived = swap(rows_sq, "wide", stride)
            rows_sq = rows_sq + stand_in(rows_sq, STAND_IN) + arrived
        return rows_sq

    rows_in = hidden_in.astype(jnp.float32)
    first_sq = wide_sum(jnp.sum(rows_in * rows_in, axis=1))
    normed = gather(normalize(hidden_in, attn_gain, first_sq, model_width), "narrow")

    q_cols = w_query.shape[1]
    k_cols = w_key.shape[1]
    chunk_cols = (q_cols + 2 * k_cols) // QKV_CHUNKS
    pieces = []
    for chunk in range(QKV_CHUNKS):
        if chunk < QKV_CHUNKS - 1:
            segments = [(w_query, 0, chunk * chunk_cols, chunk_cols)]
        else:
            segments = [(w_query, 0, chunk * chunk_cols, q_cols - chunk * chunk_cols)]
            segments += [(w_key, 0, 0, k_cols), (w_value, 0, 0, k_cols)]
        pieces.append(wide_scatter(*project(normed, to_bank, segments, 2, 24), jnp.float32))
    summed = jnp.concatenate(pieces, axis=1).astype(jnp.bfloat16)
    summed = summed.reshape(narrow_count, local_rows, -1, HEAD_DIM)
    turned = exchange([summed[j] for j in range(narrow_count)], "narrow")
    ranks = me_narrow ^ jnp.arange(narrow_count, dtype=jnp.int32)
    turned = jnp.stack(turned)[ranks].transpose(1, 0, 2, 3)
    q_heads = q_cols // HEAD_DIM
    k_heads = k_cols // HEAD_DIM
    query_rot = rotate(
        turned[:, :, :q_heads].reshape(local_rows, -1, HEAD_DIM), cache_len
    ).reshape(local_rows, -1)
    key_rot = rotate(
        turned[:, :, q_heads : q_heads + k_heads].reshape(local_rows, -1, HEAD_DIM), cache_len
    ).reshape(local_rows, -1)
    value_new = turned[:, :, q_heads + k_heads :].reshape(local_rows, -1)
    context = attend(query_rot, key_rot, value_new, key_cache, value_cache, cache_len)
    context = context.reshape(local_rows, narrow_count, -1).transpose(1, 0, 2)[ranks]
    by_heads = exchange([context[j] for j in range(narrow_count)], "narrow")

    depth = w_out.shape[0] // CONTEXT_CHUNKS
    total = None
    for chunk in range(CONTEXT_CHUNKS):
        columns = slice(chunk * depth, (chunk + 1) * depth)
        block = jnp.concatenate([piece[:, columns] for piece in by_heads], axis=0)
        last = chunk == CONTEXT_CHUNKS - 1
        total = project(
            gather_direct(block, "wide"),
            to_hypothesis,
            [(w_out, chunk * depth, 0, w_out.shape[1])],
            2 if last else 1,
            24,
            total if total is None else total[0],
        )
    attn_out = narrow_scatter(*total)
    resid = (rows_in + attn_out).astype(jnp.bfloat16)
    resid_wide = resid.astype(jnp.float32)
    second_sq = wide_sum(jnp.sum(resid_wide * resid_wide, axis=1))
    normed_two = gather(normalize(resid, ffn_gain, second_sq, model_width), "narrow")

    f_cols = w_gate.shape[1] // FFN_CHUNKS
    total = None
    for chunk in range(FFN_CHUNKS):
        segments = [(w_gate, 0, chunk * f_cols, f_cols), (w_up, 0, chunk * f_cols, f_cols)]
        sums = wide_scatter(*project(normed_two, to_wide, segments, 2, 24), jnp.float16)
        act = (jax.nn.silu(sums[:, :f_cols]) * sums[:, f_cols:]).astype(jnp.bfloat16)
        last = chunk == FFN_CHUNKS - 1
        total = project(
            gather(act, "wide"),
            from_wide,
            [(w_down, chunk * f_cols, 0, w_down.shape[1])],
            2 if last else 1,
            24,
            total if total is None else total[0],
        )
    ffn_out = narrow_scatter(*total)
    return (resid_wide + ffn_out).astype(jnp.bfloat16)


def solution(mesh):
    return jax.shard_map(
        shards,
        mesh=mesh,
        in_specs=(
            P("narrow", "wide"),
            P("wide"),
            P("wide", "narrow"),
            P("wide", "narrow"),
            P("wide", "narrow"),
            P("narrow", "wide"),
            P("wide"),
            P("wide", "narrow"),
            P("wide", "narrow"),
            P("narrow", "wide"),
            P(("wide", "narrow"), None, None),
            P(("wide", "narrow"), None, None),
            P(("wide", "narrow")),
            P(),
        ),
        out_specs=P("narrow", "wide"),
        check_vma=False,
    )
```

```python
import math

import jax
import jax.numpy as jnp
from jax import lax
from jax.experimental import pallas as pl
from jax.experimental.pallas import tpu as pltpu
from jax.sharding import PartitionSpec as P

HEAD_DIM = 128


NORM_EPSILON = 1e-05
ROPE_BASE = 500000.0


def product(left, right):
    return jnp.dot(left, right, preferred_element_type=jnp.float32)


def normalize(values_in, gain_row, sum_sq, model_width):
    mean_sq = sum_sq / model_width
    scaled = values_in.astype(jnp.float32) * lax.rsqrt(mean_sq + NORM_EPSILON)[:, None]
    return (scaled * gain_row[None, :]).astype(jnp.bfloat16)


def rotate(head_rows, lengths):
    head_size = head_rows.shape[-1]
    half_size = head_size // 2
    inverse_freq = jnp.exp(
        jnp.arange(half_size, dtype=jnp.float32) * (-2.0 * math.log(ROPE_BASE) / head_size)
    )
    angles = lengths.astype(jnp.float32)[:, None] * inverse_freq[None, :]
    cos_part = jnp.cos(angles)[:, None, :]
    sin_part = jnp.sin(angles)[:, None, :]
    front_half = head_rows[..., :half_size].astype(jnp.float32)
    back_half = head_rows[..., half_size:].astype(jnp.float32)
    turned = jnp.concatenate(
        [
            front_half * cos_part - back_half * sin_part,
            back_half * cos_part + front_half * sin_part,
        ],
        axis=-1,
    )
    return turned.astype(jnp.bfloat16)


def attend(queries, fresh_key, fresh_value, key_cache, value_cache, lengths):
    row_count, length, kv_width = key_cache.shape
    groups = kv_width // HEAD_DIM
    group_size = queries.shape[1] // kv_width
    score_scale = 1.0 / math.sqrt(HEAD_DIM)
    query_heads = queries.reshape(row_count, groups, group_size, HEAD_DIM)
    cache_keys = key_cache.reshape(row_count, length, groups, HEAD_DIM)
    cache_values = value_cache.reshape(row_count, length, groups, HEAD_DIM)
    own_key = fresh_key.reshape(row_count, groups, HEAD_DIM)
    own_value = fresh_value.reshape(row_count, groups, HEAD_DIM)
    scores = (
        jnp.einsum("rgqd,rlgd->rgql", query_heads, cache_keys, preferred_element_type=jnp.float32)
        * score_scale
    )
    own_score = (
        jnp.einsum("rgqd,rgd->rgq", query_heads, own_key, preferred_element_type=jnp.float32)
        * score_scale
    )
    valid_pos = jnp.arange(length, dtype=jnp.int32)[None, :] < lengths[:, None]
    scores = jnp.where(valid_pos[:, None, None, :], scores, -jnp.inf)
    row_max = jnp.maximum(jnp.max(scores, axis=3), own_score)
    weights = jnp.exp(scores - row_max[..., None])
    own_weight = jnp.exp(own_score - row_max)
    weight_sum = jnp.sum(weights, axis=3) + own_weight
    probs = (weights / weight_sum[..., None]).astype(jnp.bfloat16)
    own_prob = (own_weight / weight_sum).astype(jnp.bfloat16)
    context = jnp.einsum("rgql,rlgd->rgqd", probs, cache_values, preferred_element_type=jnp.float32)
    context = (
        context
        + own_prob.astype(jnp.float32)[..., None] * own_value.astype(jnp.float32)[:, :, None, :]
    )
    return context.reshape(row_count, groups * group_size * HEAD_DIM).astype(jnp.bfloat16)


QKV_CHUNKS = 3
FFN_CHUNKS = 2
CONTEXT_CHUNKS = 2
NARROW_KINDS = [jnp.float32] + [jnp.bfloat16] * 8
TILE = 512
ROOM = 24
STAND_IN = 4
MIB = 1024 * 1024


def swap(block, axis, offset):
    count = lax.axis_size(axis)
    return lax.ppermute(block, axis, [(i, i ^ offset) for i in range(count)])


def strides_of(axis):
    count = lax.axis_size(axis)
    return [1 << bit for bit in range(count.bit_length() - 1)]


def offsets_of(axis):
    order = [0]
    for stride in reversed(strides_of(axis)):
        order = order + [offset ^ stride for offset in order]
    return order


def project(groups, order, turned, segments, split, total=None):
    rows = order.shape[0]
    depth = groups[0][0].shape[1]
    tiles = []
    width = 0
    for index, (_, first_row, first, columns) in enumerate(segments):
        for start in range(first, first + columns, TILE):
            tile = min(TILE, first + columns - start)
            tiles.append((index, first_row, start, tile, width))
            width += tile
    part = rows // split
    pieces = [piece for group in groups for piece in group]
    count = len(pieces)
    each = count // len(groups)

    def body(*refs):
        piece_refs, order_ref, rest = refs[:count], refs[count], refs[count + 1 :]
        weight_refs, rest = rest[: len(segments)], rest[len(segments) :]
        if total is not None:
            total_ref, rest = rest[0], rest[1:]
        out_refs = rest[:split]
        lefts = []
        for group in range(len(groups)):
            group_refs = piece_refs[group * each : (group + 1) * each]
            left = lax.dot_general(
                order_ref[...],
                jnp.concatenate([ref[...] for ref in group_refs], axis=0),
                (((0 if turned else 1,), (0,)), ((), ())),
                preferred_element_type=jnp.float32,
            )
            lefts.append(left.astype(jnp.bfloat16))
        for index, first_row, start, tile, base in tiles:
            result = None
            for group, left in enumerate(lefts):
                weight = weight_refs[index][
                    pl.ds(first_row + group * depth, depth), pl.ds(start, tile)
                ]
                product = jnp.dot(left, weight, preferred_element_type=jnp.float32)
                result = product if result is None else result + product
            if total is not None:
                result = result + total_ref[:, base : base + tile]
            for place, out_ref in enumerate(out_refs):
                out_ref[:, base : base + tile] = result[place * part : (place + 1) * part]

    operands = pieces + [order] + [segment[0] for segment in segments]
    if total is not None:
        operands.append(total)
    in_vmem = pl.BlockSpec(memory_space=pltpu.VMEM)
    return pl.pallas_call(
        body,
        in_specs=[in_vmem] * len(operands),
        out_specs=[in_vmem] * split,
        out_shape=[jax.ShapeDtypeStruct((part, width), jnp.float32)] * split,
        compiler_params=pltpu.CompilerParams(vmem_limit_bytes=ROOM * MIB),
        cost_estimate=pl.CostEstimate(
            flops=2 * rows * len(groups) * depth * (width + rows),
            bytes_accessed=2 * len(groups) * depth * width + 4 * rows * width,
            transcendentals=0,
        ),
    )(*operands)


def stand_in(array):
    def body(array_ref, copy_ref):
        copy_ref[...] = array_ref[...]

    in_vmem = pl.BlockSpec(memory_space=pltpu.VMEM)
    return pl.pallas_call(
        body,
        in_specs=[in_vmem],
        out_specs=in_vmem,
        out_shape=jax.ShapeDtypeStruct(array.shape, array.dtype),
        compiler_params=pltpu.CompilerParams(vmem_limit_bytes=MIB),
        cost_estimate=pl.CostEstimate(
            flops=int(1.1e9 * STAND_IN), bytes_accessed=4096, transcendentals=0
        ),
    )(array)


def wide_scatter(kept, sent, kind):
    strides = strides_of("wide")
    rows = 2 * kept.shape[0] // lax.axis_size("wide")
    kept = kept + swap(sent.astype(kind), "wide", strides[0]).astype(jnp.float32)
    total = kept[:rows]
    for place, offset in enumerate(offsets_of("wide")[: kept.shape[0] // rows]):
        if offset:
            block = kept[place * rows : (place + 1) * rows].astype(kind)
            total = total + swap(block, "wide", offset).astype(jnp.float32)
    return total


def narrow_scatter(kept, sent):
    for stride, kind in zip(strides_of("narrow"), NARROW_KINDS):
        if stride > 1:
            half = kept.shape[0] // 2
            kept, sent = kept[:half], kept[half:]
        kept = kept + swap(sent.astype(kind), "narrow", stride).astype(jnp.float32)
    return kept


def gather(block, axis):
    strides = strides_of(axis)[::-1]
    for stride in strides[:-1]:
        block = jnp.concatenate([block, swap(block, axis, stride)], axis=0)
    return [block, swap(block, axis, strides[-1])]


def gather_direct(block, axis):
    offsets = offsets_of(axis)
    held = [block] + [swap(block, axis, o) for o in offsets[1 : len(offsets) // 2]]
    return [stand_in(block)] + held[1:] + [swap(piece, axis, 1) for piece in held]


def exchange(blocks, axis):
    blocks = list(blocks)
    for stride in strides_of(axis)[::-1]:
        marked = [i for i in range(len(blocks)) if i & stride]
        arrived = swap(jnp.stack([blocks[i] for i in marked]), axis, stride)
        for place, i in enumerate(marked):
            blocks[i] = arrived[place]
    return blocks


def by_rank(blocks, me):
    stride = 1
    while stride < len(blocks):
        other = (me & stride) != 0
        blocks = [jnp.where(other, blocks[i ^ stride], block) for i, block in enumerate(blocks)]
        stride *= 2
    return blocks


def shards(
    hidden_in,
    attn_gain,
    w_query,
    w_key,
    w_value,
    w_out,
    ffn_gain,
    w_gate,
    w_up,
    w_down,
    key_cache,
    value_cache,
    cache_len,
    bank_row,
):
    wide_count = lax.axis_size("wide")
    narrow_count = lax.axis_size("narrow")
    me_wide = lax.axis_index("wide")
    me_narrow = lax.axis_index("narrow")
    model_width = hidden_in.shape[1] * wide_count
    own_rows = hidden_in.shape[0]
    local_rows = cache_len.shape[0]
    all_rows = bank_row.shape[0]
    wide_rows = all_rows // wide_count

    def device(block, axis, me):
        bits = len(strides_of(axis))
        for bit in range(bits):
            me = me ^ (((block >> bit) & 1) << (bits - 1 - bit))
        return me

    def hypothesis(place):
        return device(place // own_rows, "narrow", me_narrow) * own_rows + place % own_rows

    def wide_row(place):
        return device(place // wide_rows, "wide", me_wide) * wide_rows + place % wide_rows

    def bank(place):
        inner = place % wide_rows
        owner = device(place // wide_rows, "wide", me_wide) * narrow_count
        owner = owner + (me_narrow ^ (inner // local_rows))
        return owner * local_rows + inner % local_rows

    down = lax.broadcasted_iota(jnp.int32, (all_rows, all_rows), 0)
    across = lax.broadcasted_iota(jnp.int32, (all_rows, all_rows), 1)
    banks = jnp.broadcast_to(bank_row[None, :], (all_rows, all_rows))
    hypothesis_bank = jnp.sum(
        jnp.where(hypothesis(down) == across, banks, 0), axis=1, keepdims=True
    )
    to_hypothesis = (hypothesis_bank == bank(across)).astype(jnp.bfloat16)
    to_wide = (wide_row(down) == across).astype(jnp.bfloat16)

    def wide_sum(rows_sq):
        for stride in strides_of("wide"):
            rows_sq = stand_in(rows_sq) + swap(rows_sq, "wide", stride)
        return rows_sq

    rows_in = hidden_in.astype(jnp.float32)
    first_sq = wide_sum(jnp.sum(rows_in * rows_in, axis=1))
    normed = gather(normalize(hidden_in, attn_gain, first_sq, model_width), "narrow")

    q_cols = w_query.shape[1]
    k_cols = w_key.shape[1]
    chunk_cols = (q_cols + 2 * k_cols) // QKV_CHUNKS
    pieces = []
    for chunk in range(QKV_CHUNKS):
        if chunk < QKV_CHUNKS - 1:
            segments = [(w_query, 0, chunk * chunk_cols, chunk_cols)]
        else:
            segments = [(w_query, 0, chunk * chunk_cols, q_cols - chunk * chunk_cols)]
            segments += [(w_key, 0, 0, k_cols), (w_value, 0, 0, k_cols)]
        pieces.append(wide_scatter(*project([normed], to_hypothesis, True, segments, 2), jnp.float32))
    summed = jnp.concatenate(pieces, axis=1).astype(jnp.bfloat16)
    summed = summed.reshape(narrow_count, local_rows, -1, HEAD_DIM)
    turned = exchange([summed[j] for j in range(narrow_count)], "narrow")
    turned = jnp.stack(by_rank(turned, me_narrow), axis=1)
    q_heads = q_cols // HEAD_DIM
    k_heads = k_cols // HEAD_DIM
    query_rot = rotate(
        turned[:, :, :q_heads].reshape(local_rows, -1, HEAD_DIM), cache_len
    ).reshape(local_rows, -1)
    key_rot = rotate(
        turned[:, :, q_heads : q_heads + k_heads].reshape(local_rows, -1, HEAD_DIM), cache_len
    ).reshape(local_rows, -1)
    value_new = turned[:, :, q_heads + k_heads :].reshape(local_rows, -1)
    context = attend(query_rot, key_rot, value_new, key_cache, value_cache, cache_len)
    context = context.reshape(local_rows, narrow_count, -1)
    context = by_rank([context[:, j] for j in range(narrow_count)], me_narrow)
    by_heads = exchange(context, "narrow")

    depth = w_out.shape[0] // CONTEXT_CHUNKS
    groups = []
    for chunk in range(CONTEXT_CHUNKS):
        columns = slice(chunk * depth, (chunk + 1) * depth)
        block = jnp.concatenate([piece[:, columns] for piece in by_heads], axis=0)
        groups.append(gather_direct(block, "wide"))
    total = project(groups, to_hypothesis, False, [(w_out, 0, 0, w_out.shape[1])], 2)
    attn_out = narrow_scatter(*total)
    resid = (rows_in + attn_out).astype(jnp.bfloat16)
    resid_wide = resid.astype(jnp.float32)
    second_sq = wide_sum(jnp.sum(resid_wide * resid_wide, axis=1))
    normed_two = gather(normalize(resid, ffn_gain, second_sq, model_width), "narrow")

    f_cols = w_gate.shape[1] // FFN_CHUNKS
    total = None
    for chunk in range(FFN_CHUNKS):
        segments = [(w_gate, 0, chunk * f_cols, f_cols), (w_up, 0, chunk * f_cols, f_cols)]
        sums = wide_scatter(*project([normed_two], to_wide, False, segments, 2), jnp.float16)
        act = (jax.nn.silu(sums[:, :f_cols]) * sums[:, f_cols:]).astype(jnp.bfloat16)
        last = chunk == FFN_CHUNKS - 1
        total = project(
            [gather(act, "wide")],
            to_wide,
            True,
            [(w_down, chunk * f_cols, 0, w_down.shape[1])],
            2 if last else 1,
            total if total is None else total[0],
        )
    ffn_out = narrow_scatter(*total)
    return (resid_wide + ffn_out).astype(jnp.bfloat16)


def solution(mesh):
    return jax.shard_map(
        shards,
        mesh=mesh,
        in_specs=(
            P("narrow", "wide"),
            P("wide"),
            P("wide", "narrow"),
            P("wide", "narrow"),
            P("wide", "narrow"),
            P("narrow", "wide"),
            P("wide"),
            P("wide", "narrow"),
            P("wide", "narrow"),
            P("narrow", "wide"),
            P(("wide", "narrow"), None, None),
            P(("wide", "narrow"), None, None),
            P(("wide", "narrow")),
            P(),
        ),
        out_specs=P("narrow", "wide"),
        check_vma=False,
    )
```

```python
import math

import jax
import jax.numpy as jnp
from jax import lax
from jax.experimental import pallas as pl
from jax.experimental.pallas import tpu as pltpu
from jax.sharding import PartitionSpec as P

HEAD_DIM = 128


NORM_EPSILON = 1e-05
ROPE_BASE = 500000.0


def product(left, right):
    return jnp.dot(left, right, preferred_element_type=jnp.float32)


def normalize(values_in, gain_row, sum_sq, model_width):
    mean_sq = sum_sq / model_width
    scaled = values_in.astype(jnp.float32) * lax.rsqrt(mean_sq + NORM_EPSILON)[:, None]
    return (scaled * gain_row[None, :]).astype(jnp.bfloat16)


def rotate(head_rows, lengths):
    head_size = head_rows.shape[-1]
    half_size = head_size // 2
    inverse_freq = jnp.exp(
        jnp.arange(half_size, dtype=jnp.float32) * (-2.0 * math.log(ROPE_BASE) / head_size)
    )
    angles = lengths.astype(jnp.float32)[:, None] * inverse_freq[None, :]
    cos_part = jnp.cos(angles)[:, None, :]
    sin_part = jnp.sin(angles)[:, None, :]
    front_half = head_rows[..., :half_size].astype(jnp.float32)
    back_half = head_rows[..., half_size:].astype(jnp.float32)
    turned = jnp.concatenate(
        [
            front_half * cos_part - back_half * sin_part,
            back_half * cos_part + front_half * sin_part,
        ],
        axis=-1,
    )
    return turned.astype(jnp.bfloat16)


def attend(queries, fresh_key, fresh_value, key_cache, value_cache, lengths):
    row_count, length, kv_width = key_cache.shape
    groups = kv_width // HEAD_DIM
    group_size = queries.shape[1] // kv_width
    score_scale = 1.0 / math.sqrt(HEAD_DIM)
    query_heads = queries.reshape(row_count, groups, group_size, HEAD_DIM)
    cache_keys = key_cache.reshape(row_count, length, groups, HEAD_DIM)
    cache_values = value_cache.reshape(row_count, length, groups, HEAD_DIM)
    own_key = fresh_key.reshape(row_count, groups, HEAD_DIM)
    own_value = fresh_value.reshape(row_count, groups, HEAD_DIM)
    scores = (
        jnp.einsum("rgqd,rlgd->rgql", query_heads, cache_keys, preferred_element_type=jnp.float32)
        * score_scale
    )
    own_score = (
        jnp.einsum("rgqd,rgd->rgq", query_heads, own_key, preferred_element_type=jnp.float32)
        * score_scale
    )
    valid_pos = jnp.arange(length, dtype=jnp.int32)[None, :] < lengths[:, None]
    scores = jnp.where(valid_pos[:, None, None, :], scores, -jnp.inf)
    row_max = jnp.maximum(jnp.max(scores, axis=3), own_score)
    weights = jnp.exp(scores - row_max[..., None])
    own_weight = jnp.exp(own_score - row_max)
    weight_sum = jnp.sum(weights, axis=3) + own_weight
    probs = (weights / weight_sum[..., None]).astype(jnp.bfloat16)
    own_prob = (own_weight / weight_sum).astype(jnp.bfloat16)
    context = jnp.einsum("rgql,rlgd->rgqd", probs, cache_values, preferred_element_type=jnp.float32)
    context = (
        context
        + own_prob.astype(jnp.float32)[..., None] * own_value.astype(jnp.float32)[:, :, None, :]
    )
    return context.reshape(row_count, groups * group_size * HEAD_DIM).astype(jnp.bfloat16)


QKV_CHUNKS = 4
FFN_CHUNKS = 2
CONTEXT_CHUNKS = 2
NARROW_KINDS = [jnp.float32] + [jnp.bfloat16] * 8
TILE = 512
ROOM = 24
STAND_IN = 4
MIB = 1024 * 1024


def swap(block, axis, offset):
    count = lax.axis_size(axis)
    return lax.ppermute(block, axis, [(i, i ^ offset) for i in range(count)])


def strides_of(axis):
    count = lax.axis_size(axis)
    return [1 << bit for bit in range(count.bit_length() - 1)]


def offsets_of(axis):
    order = [0]
    for stride in reversed(strides_of(axis)):
        order = order + [offset ^ stride for offset in order]
    return order


def project(groups, order, turned, segments, split, total=None):
    rows = order.shape[0]
    depth = groups[0][0].shape[1]
    tiles = []
    width = 0
    for index, (_, first_row, first, columns) in enumerate(segments):
        for start in range(first, first + columns, TILE):
            tile = min(TILE, first + columns - start)
            tiles.append((index, first_row, start, tile, width))
            width += tile
    part = rows // split
    pieces = [piece for group in groups for piece in group]
    count = len(pieces)
    each = count // len(groups)

    def body(*refs):
        piece_refs, order_ref, rest = refs[:count], refs[count], refs[count + 1 :]
        weight_refs, rest = rest[: len(segments)], rest[len(segments) :]
        if total is not None:
            total_ref, rest = rest[0], rest[1:]
        out_refs = rest[:split]
        lefts = []
        for group in range(len(groups)):
            group_refs = piece_refs[group * each : (group + 1) * each]
            left = lax.dot_general(
                order_ref[...],
                jnp.concatenate([ref[...] for ref in group_refs], axis=0),
                (((0 if turned else 1,), (0,)), ((), ())),
                preferred_element_type=jnp.float32,
            )
            lefts.append(left.astype(jnp.bfloat16))
        for index, first_row, start, tile, base in tiles:
            result = None
            for group, left in enumerate(lefts):
                weight = weight_refs[index][
                    pl.ds(first_row + group * depth, depth), pl.ds(start, tile)
                ]
                product = jnp.dot(left, weight, preferred_element_type=jnp.float32)
                result = product if result is None else result + product
            if total is not None:
                result = result + total_ref[:, base : base + tile]
            for place, out_ref in enumerate(out_refs):
                out_ref[:, base : base + tile] = result[place * part : (place + 1) * part]

    operands = pieces + [order] + [segment[0] for segment in segments]
    if total is not None:
        operands.append(total)
    in_vmem = pl.BlockSpec(memory_space=pltpu.VMEM)
    return pl.pallas_call(
        body,
        in_specs=[in_vmem] * len(operands),
        out_specs=[in_vmem] * split,
        out_shape=[jax.ShapeDtypeStruct((part, width), jnp.float32)] * split,
        compiler_params=pltpu.CompilerParams(vmem_limit_bytes=ROOM * MIB),
        cost_estimate=pl.CostEstimate(
            flops=2 * rows * len(groups) * depth * (width + rows),
            bytes_accessed=2 * len(groups) * depth * width + 4 * rows * width,
            transcendentals=0,
        ),
    )(*operands)


def stand_in(array):
    def body(array_ref, copy_ref):
        copy_ref[...] = array_ref[...]

    in_vmem = pl.BlockSpec(memory_space=pltpu.VMEM)
    return pl.pallas_call(
        body,
        in_specs=[in_vmem],
        out_specs=in_vmem,
        out_shape=jax.ShapeDtypeStruct(array.shape, array.dtype),
        compiler_params=pltpu.CompilerParams(vmem_limit_bytes=MIB),
        cost_estimate=pl.CostEstimate(
            flops=int(1.1e9 * STAND_IN), bytes_accessed=4096, transcendentals=0
        ),
    )(array)


def wide_scatter(kept, sent, kind):
    strides = strides_of("wide")
    rows = 2 * kept.shape[0] // lax.axis_size("wide")
    kept = kept + swap(sent.astype(kind), "wide", strides[0]).astype(jnp.float32)
    total = kept[:rows]
    for place, offset in enumerate(offsets_of("wide")[: kept.shape[0] // rows]):
        if offset:
            block = kept[place * rows : (place + 1) * rows].astype(kind)
            total = total + swap(block, "wide", offset).astype(jnp.float32)
    return total


def narrow_scatter(kept, sent):
    for stride, kind in zip(strides_of("narrow"), NARROW_KINDS):
        if stride > 1:
            half = kept.shape[0] // 2
            kept, sent = kept[:half], kept[half:]
        kept = kept + swap(sent.astype(kind), "narrow", stride).astype(jnp.float32)
    return kept


def gather(block, axis, paired=False):
    strides = strides_of(axis)[::-1]
    kept = stand_in if paired else lambda held: held
    for stride in strides[:-1]:
        block = jnp.concatenate([kept(block), swap(block, axis, stride)], axis=0)
    return [kept(block), swap(block, axis, strides[-1])]


def gather_direct(block, axis):
    offsets = offsets_of(axis)
    held = [block] + [swap(block, axis, o) for o in offsets[1 : len(offsets) // 2]]
    return [stand_in(block)] + held[1:] + [swap(piece, axis, 1) for piece in held]


def exchange(blocks, axis):
    blocks = list(blocks)
    for stride in strides_of(axis)[::-1]:
        marked = [i for i in range(len(blocks)) if i & stride]
        arrived = swap(jnp.stack([blocks[i] for i in marked]), axis, stride)
        for place, i in enumerate(marked):
            blocks[i] = arrived[place]
    return blocks


def by_rank(blocks, flags):
    for bit, flag in enumerate(flags):
        other = 1 << bit
        blocks = [jnp.where(flag, blocks[i ^ other], block) for i, block in enumerate(blocks)]
    return blocks


def shards(
    hidden_in,
    attn_gain,
    w_query,
    w_key,
    w_value,
    w_out,
    ffn_gain,
    w_gate,
    w_up,
    w_down,
    key_cache,
    value_cache,
    cache_len,
    bank_row,
):
    wide_count = lax.axis_size("wide")
    narrow_count = lax.axis_size("narrow")
    me_wide = lax.axis_index("wide")
    me_narrow = lax.axis_index("narrow")
    flags = [(me_narrow & stride) != 0 for stride in strides_of("narrow")]
    hidden_in, me_wide, me_narrow, flags = lax.optimization_barrier(
        (hidden_in, me_wide, me_narrow, flags)
    )
    model_width = hidden_in.shape[1] * wide_count
    own_rows = hidden_in.shape[0]
    local_rows = cache_len.shape[0]
    all_rows = bank_row.shape[0]
    wide_rows = all_rows // wide_count

    def device(block, axis, me):
        bits = len(strides_of(axis))
        for bit in range(bits):
            me = me ^ (((block >> bit) & 1) << (bits - 1 - bit))
        return me

    def hypothesis(place):
        return device(place // own_rows, "narrow", me_narrow) * own_rows + place % own_rows

    def wide_row(place):
        return device(place // wide_rows, "wide", me_wide) * wide_rows + place % wide_rows

    def bank(place):
        inner = place % wide_rows
        owner = device(place // wide_rows, "wide", me_wide) * narrow_count
        owner = owner + (me_narrow ^ (inner // local_rows))
        return owner * local_rows + inner % local_rows

    down = lax.broadcasted_iota(jnp.int32, (all_rows, all_rows), 0)
    across = lax.broadcasted_iota(jnp.int32, (all_rows, all_rows), 1)
    banks = jnp.broadcast_to(bank_row[None, :], (all_rows, all_rows))
    hypothesis_bank = jnp.sum(
        jnp.where(hypothesis(down) == across, banks, 0), axis=1, keepdims=True
    )
    to_hypothesis = (hypothesis_bank == bank(across)).astype(jnp.bfloat16)
    to_wide = (wide_row(down) == across).astype(jnp.bfloat16)

    def normalized_rows(values, gain_row):
        wide_values = values.astype(jnp.float32)
        rows_sq = jnp.sum(wide_values * wide_values, axis=1)
        sent = jnp.broadcast_to(rows_sq[None, :], (wide_count * narrow_count, own_rows))
        landed = lax.all_to_all(sent, ("wide", "narrow"), 0, 0, tiled=True)
        pieces = gather(values, "narrow", paired=True)
        sums = jnp.sum(landed.reshape(wide_count, narrow_count, own_rows), axis=0)
        sums = by_rank([sums[j] for j in range(narrow_count)], flags)
        order = offsets_of("narrow")
        half = narrow_count // 2
        result = []
        for piece, offsets in zip(pieces, (order[:half], order[half:])):
            sum_sq = jnp.concatenate([sums[offset] for offset in offsets])
            result.append(normalize(piece, gain_row, sum_sq, model_width))
        return result

    rows_in = hidden_in.astype(jnp.float32)
    normed = normalized_rows(hidden_in, attn_gain)

    q_cols = w_query.shape[1]
    k_cols = w_key.shape[1]
    stacked = [(w_query, q_cols), (w_key, k_cols), (w_value, k_cols)]
    heads = (q_cols + 2 * k_cols) // HEAD_DIM
    edges = [heads * chunk // QKV_CHUNKS for chunk in range(QKV_CHUNKS)] + [heads]
    pieces = []
    for chunk in range(QKV_CHUNKS):
        first, last = edges[chunk] * HEAD_DIM, edges[chunk + 1] * HEAD_DIM
        segments = []
        start = 0
        for weight, columns in stacked:
            low, high = max(first, start), min(last, start + columns)
            if low < high:
                segments.append((weight, 0, low - start, high - low))
            start += columns
        sums = project([normed], to_hypothesis, True, segments, 2)
        pieces.append(wide_scatter(*sums, jnp.float32))
    summed = jnp.concatenate(pieces, axis=1).astype(jnp.bfloat16)
    summed = summed.reshape(narrow_count, local_rows, -1, HEAD_DIM)
    turned = exchange([summed[j] for j in range(narrow_count)], "narrow")
    turned = jnp.stack(by_rank(turned, flags), axis=1)
    q_heads = q_cols // HEAD_DIM
    k_heads = k_cols // HEAD_DIM
    query_rot = rotate(
        turned[:, :, :q_heads].reshape(local_rows, -1, HEAD_DIM), cache_len
    ).reshape(local_rows, -1)
    key_rot = rotate(
        turned[:, :, q_heads : q_heads + k_heads].reshape(local_rows, -1, HEAD_DIM), cache_len
    ).reshape(local_rows, -1)
    value_new = turned[:, :, q_heads + k_heads :].reshape(local_rows, -1)
    context = attend(query_rot, key_rot, value_new, key_cache, value_cache, cache_len)
    context = context.reshape(local_rows, narrow_count, -1)
    context = by_rank([context[:, j] for j in range(narrow_count)], flags)
    by_heads = exchange(context, "narrow")

    depth = w_out.shape[0] // CONTEXT_CHUNKS
    groups = []
    for chunk in range(CONTEXT_CHUNKS):
        columns = slice(chunk * depth, (chunk + 1) * depth)
        block = jnp.concatenate([piece[:, columns] for piece in by_heads], axis=0)
        groups.append(gather_direct(block, "wide"))
    total = project(groups, to_hypothesis, False, [(w_out, 0, 0, w_out.shape[1])], 2)
    attn_out = narrow_scatter(*total)
    resid = (rows_in + attn_out).astype(jnp.bfloat16)
    resid_wide = resid.astype(jnp.float32)
    normed_two = normalized_rows(resid, ffn_gain)

    f_cols = w_gate.shape[1] // FFN_CHUNKS
    total = None
    for chunk in range(FFN_CHUNKS):
        segments = [(w_gate, 0, chunk * f_cols, f_cols), (w_up, 0, chunk * f_cols, f_cols)]
        sums = wide_scatter(*project([normed_two], to_wide, False, segments, 2), jnp.float16)
        act = (jax.nn.silu(sums[:, :f_cols]) * sums[:, f_cols:]).astype(jnp.bfloat16)
        last = chunk == FFN_CHUNKS - 1
        total = project(
            [gather(act, "wide")],
            to_wide,
            True,
            [(w_down, chunk * f_cols, 0, w_down.shape[1])],
            2 if last else 1,
            total if total is None else total[0],
        )
    ffn_out = narrow_scatter(*total)
    return (resid_wide + ffn_out).astype(jnp.bfloat16)


def solution(mesh):
    return jax.shard_map(
        shards,
        mesh=mesh,
        in_specs=(
            P("narrow", "wide"),
            P("wide"),
            P("wide", "narrow"),
            P("wide", "narrow"),
            P("wide", "narrow"),
            P("narrow", "wide"),
            P("wide"),
            P("wide", "narrow"),
            P("wide", "narrow"),
            P("narrow", "wide"),
            P(("wide", "narrow"), None, None),
            P(("wide", "narrow"), None, None),
            P(("wide", "narrow")),
            P(),
        ),
        out_specs=P("narrow", "wide"),
        check_vma=False,
    )
```

```python
import math

import jax
import jax.numpy as jnp
from jax import lax
from jax.experimental import pallas as pl
from jax.experimental.pallas import tpu as pltpu
from jax.sharding import PartitionSpec as P

HEAD_DIM = 128


NORM_EPSILON = 1e-05
ROPE_BASE = 500000.0


def product(left, right):
    return jnp.dot(left, right, preferred_element_type=jnp.float32)


def normalize(values_in, gain_row, sum_sq, model_width):
    mean_sq = sum_sq / model_width
    scaled = values_in.astype(jnp.float32) * lax.rsqrt(mean_sq + NORM_EPSILON)[:, None]
    return (scaled * gain_row[None, :]).astype(jnp.bfloat16)


def rotate(head_rows, lengths):
    head_size = head_rows.shape[-1]
    half_size = head_size // 2
    inverse_freq = jnp.exp(
        jnp.arange(half_size, dtype=jnp.float32) * (-2.0 * math.log(ROPE_BASE) / head_size)
    )
    angles = lengths.astype(jnp.float32)[:, None] * inverse_freq[None, :]
    cos_part = jnp.cos(angles)[:, None, :]
    sin_part = jnp.sin(angles)[:, None, :]
    front_half = head_rows[..., :half_size].astype(jnp.float32)
    back_half = head_rows[..., half_size:].astype(jnp.float32)
    turned = jnp.concatenate(
        [
            front_half * cos_part - back_half * sin_part,
            back_half * cos_part + front_half * sin_part,
        ],
        axis=-1,
    )
    return turned.astype(jnp.bfloat16)


def attend(queries, fresh_key, fresh_value, key_cache, value_cache, lengths):
    row_count, length, kv_width = key_cache.shape
    groups = kv_width // HEAD_DIM
    group_size = queries.shape[1] // kv_width
    score_scale = 1.0 / math.sqrt(HEAD_DIM)
    query_heads = queries.reshape(row_count, groups, group_size, HEAD_DIM)
    cache_keys = key_cache.reshape(row_count, length, groups, HEAD_DIM)
    cache_values = value_cache.reshape(row_count, length, groups, HEAD_DIM)
    own_key = fresh_key.reshape(row_count, groups, HEAD_DIM)
    own_value = fresh_value.reshape(row_count, groups, HEAD_DIM)
    scores = (
        jnp.einsum("rgqd,rlgd->rgql", query_heads, cache_keys, preferred_element_type=jnp.float32)
        * score_scale
    )
    own_score = (
        jnp.einsum("rgqd,rgd->rgq", query_heads, own_key, preferred_element_type=jnp.float32)
        * score_scale
    )
    valid_pos = jnp.arange(length, dtype=jnp.int32)[None, :] < lengths[:, None]
    scores = jnp.where(valid_pos[:, None, None, :], scores, -jnp.inf)
    row_max = jnp.maximum(jnp.max(scores, axis=3), own_score)
    weights = jnp.exp(scores - row_max[..., None])
    own_weight = jnp.exp(own_score - row_max)
    weight_sum = jnp.sum(weights, axis=3) + own_weight
    probs = (weights / weight_sum[..., None]).astype(jnp.bfloat16)
    own_prob = (own_weight / weight_sum).astype(jnp.bfloat16)
    context = jnp.einsum("rgql,rlgd->rgqd", probs, cache_values, preferred_element_type=jnp.float32)
    context = (
        context
        + own_prob.astype(jnp.float32)[..., None] * own_value.astype(jnp.float32)[:, :, None, :]
    )
    return context.reshape(row_count, groups * group_size * HEAD_DIM).astype(jnp.bfloat16)


QKV_CHUNKS = 4
FFN_CHUNKS = 2
CONTEXT_CHUNKS = 2
NARROW_KINDS = [jnp.float32] + [jnp.bfloat16] * 8
TILE = 512
ROOM = 24
DIRECT_ROOM = 50
DIRECT_TILE = 256
IN_FLIGHT = 4
STAND_IN = 4
MIB = 1024 * 1024


def swap(block, axis, offset):
    count = lax.axis_size(axis)
    return lax.ppermute(block, axis, [(i, i ^ offset) for i in range(count)])


def strides_of(axis):
    count = lax.axis_size(axis)
    return [1 << bit for bit in range(count.bit_length() - 1)]


def offsets_of(axis):
    order = [0]
    for stride in reversed(strides_of(axis)):
        order = order + [offset ^ stride for offset in order]
    return order


def project(groups, order, turned, segments, split, total=None, direct=False):
    rows = order.shape[0]
    width_of_tile = DIRECT_TILE if direct else TILE
    depth = groups[0][0].shape[1]
    tiles = []
    width = 0
    for index, (_, first_row, first, columns) in enumerate(segments):
        for start in range(first, first + columns, width_of_tile):
            tile = min(width_of_tile, first + columns - start)
            tiles.append((index, first_row, start, tile, width))
            width += tile
    part = rows // split
    pieces = [piece for group in groups for piece in group]
    count = len(pieces)
    each = count // len(groups)

    def body(*refs):
        piece_refs, order_ref, rest = refs[:count], refs[count], refs[count + 1 :]
        weight_refs, rest = rest[: len(segments)], rest[len(segments) :]
        if total is not None:
            total_ref, rest = rest[0], rest[1:]
        out_refs, rest = rest[:split], rest[split:]
        copies = []
        if direct:
            for place, (index, first_row, start, tile, _) in enumerate(tiles):
                source = weight_refs[index].at[pl.ds(first_row, depth), pl.ds(start, tile)]
                copies.append(pltpu.make_async_copy(source, rest[place], rest[-1].at[place]))
        for copy in copies[:IN_FLIGHT]:
            copy.start()
        lefts = []
        for group in range(len(groups)):
            group_refs = piece_refs[group * each : (group + 1) * each]
            left = lax.dot_general(
                order_ref[...],
                jnp.concatenate([ref[...] for ref in group_refs], axis=0),
                (((0 if turned else 1,), (0,)), ((), ())),
                preferred_element_type=jnp.float32,
            )
            lefts.append(left.astype(jnp.bfloat16))
        for number, (index, first_row, start, tile, base) in enumerate(tiles):
            result = None
            for group, left in enumerate(lefts):
                if direct:
                    copies[number].wait()
                    weight = rest[number][...]
                    if number + IN_FLIGHT < len(tiles):
                        copies[number + IN_FLIGHT].start()
                else:
                    weight = weight_refs[index][
                        pl.ds(first_row + group * depth, depth), pl.ds(start, tile)
                    ]
                product = jnp.dot(left, weight, preferred_element_type=jnp.float32)
                result = product if result is None else result + product
            if total is not None:
                result = result + total_ref[:, base : base + tile]
            for place, out_ref in enumerate(out_refs):
                out_ref[:, base : base + tile] = result[place * part : (place + 1) * part]

    operands = pieces + [order] + [segment[0] for segment in segments]
    if total is not None:
        operands.append(total)
    in_vmem = pl.BlockSpec(memory_space=pltpu.VMEM)
    specs = [in_vmem] * len(operands)
    scratch = []
    if direct:
        for place in range(count + 1, count + 1 + len(segments)):
            specs[place] = pl.BlockSpec(memory_space=pltpu.HBM)
        scratch = [pltpu.VMEM((depth, tile[3]), jnp.bfloat16) for tile in tiles]
        scratch.append(pltpu.SemaphoreType.DMA((len(tiles),)))
    return pl.pallas_call(
        body,
        in_specs=specs,
        out_specs=[in_vmem] * split,
        scratch_shapes=scratch,
        out_shape=[jax.ShapeDtypeStruct((part, width), jnp.float32)] * split,
        compiler_params=pltpu.CompilerParams(vmem_limit_bytes=(DIRECT_ROOM if direct else ROOM) * MIB),
        cost_estimate=pl.CostEstimate(
            flops=2 * rows * len(groups) * depth * (width + rows),
            bytes_accessed=2 * len(groups) * depth * width + 4 * rows * width,
            transcendentals=0,
        ),
    )(*operands)


def stand_in(array):
    def body(array_ref, copy_ref):
        copy_ref[...] = array_ref[...]

    in_vmem = pl.BlockSpec(memory_space=pltpu.VMEM)
    return pl.pallas_call(
        body,
        in_specs=[in_vmem],
        out_specs=in_vmem,
        out_shape=jax.ShapeDtypeStruct(array.shape, array.dtype),
        compiler_params=pltpu.CompilerParams(vmem_limit_bytes=MIB),
        cost_estimate=pl.CostEstimate(
            flops=int(1.1e9 * STAND_IN), bytes_accessed=4096, transcendentals=0
        ),
    )(array)


def wide_scatter(kept, sent, kind):
    strides = strides_of("wide")
    rows = 2 * kept.shape[0] // lax.axis_size("wide")
    kept = kept + swap(sent.astype(kind), "wide", strides[0]).astype(jnp.float32)
    total = kept[:rows]
    for place, offset in enumerate(offsets_of("wide")[: kept.shape[0] // rows]):
        if offset:
            block = kept[place * rows : (place + 1) * rows].astype(kind)
            total = total + swap(block, "wide", offset).astype(jnp.float32)
    return total


def narrow_scatter(kept, sent):
    for stride, kind in zip(strides_of("narrow"), NARROW_KINDS):
        if stride > 1:
            half = kept.shape[0] // 2
            kept, sent = kept[:half], kept[half:]
        kept = kept + swap(sent.astype(kind), "narrow", stride).astype(jnp.float32)
    return kept


def gather(block, axis):
    strides = strides_of(axis)[::-1]
    for stride in strides[:-1]:
        block = jnp.concatenate([block, swap(block, axis, stride)], axis=0)
    return [block, swap(block, axis, strides[-1])]


def gather_direct(block, axis):
    offsets = offsets_of(axis)
    held = [block] + [swap(block, axis, o) for o in offsets[1 : len(offsets) // 2]]
    return [stand_in(block)] + held[1:] + [swap(piece, axis, 1) for piece in held]


def exchange(blocks, axis):
    blocks = list(blocks)
    for stride in strides_of(axis)[::-1]:
        marked = [i for i in range(len(blocks)) if i & stride]
        arrived = swap(jnp.stack([blocks[i] for i in marked]), axis, stride)
        for place, i in enumerate(marked):
            blocks[i] = arrived[place]
    return blocks


def by_rank(blocks, flags):
    for bit, flag in enumerate(flags):
        other = 1 << bit
        blocks = [jnp.where(flag, blocks[i ^ other], block) for i, block in enumerate(blocks)]
    return blocks


def shards(
    hidden_in,
    attn_gain,
    w_query,
    w_key,
    w_value,
    w_out,
    ffn_gain,
    w_gate,
    w_up,
    w_down,
    key_cache,
    value_cache,
    cache_len,
    bank_row,
):
    wide_count = lax.axis_size("wide")
    narrow_count = lax.axis_size("narrow")
    me_wide = lax.axis_index("wide")
    me_narrow = lax.axis_index("narrow")
    flags = [(me_narrow & stride) != 0 for stride in strides_of("narrow")]
    hidden_in, me_wide, me_narrow, flags = lax.optimization_barrier(
        (hidden_in, me_wide, me_narrow, flags)
    )
    model_width = hidden_in.shape[1] * wide_count
    own_rows = hidden_in.shape[0]
    local_rows = cache_len.shape[0]
    all_rows = bank_row.shape[0]
    wide_rows = all_rows // wide_count

    def device(block, axis, me):
        bits = len(strides_of(axis))
        for bit in range(bits):
            me = me ^ (((block >> bit) & 1) << (bits - 1 - bit))
        return me

    def hypothesis(place):
        return device(place // own_rows, "narrow", me_narrow) * own_rows + place % own_rows

    def wide_row(place):
        return device(place // wide_rows, "wide", me_wide) * wide_rows + place % wide_rows

    def bank(place):
        inner = place % wide_rows
        owner = device(place // wide_rows, "wide", me_wide) * narrow_count
        owner = owner + (me_narrow ^ (inner // local_rows))
        return owner * local_rows + inner % local_rows

    down = lax.broadcasted_iota(jnp.int32, (all_rows, all_rows), 0)
    across = lax.broadcasted_iota(jnp.int32, (all_rows, all_rows), 1)
    banks = jnp.broadcast_to(bank_row[None, :], (all_rows, all_rows))
    hypothesis_bank = jnp.sum(
        jnp.where(hypothesis(down) == across, banks, 0), axis=1, keepdims=True
    )
    to_hypothesis = (hypothesis_bank == bank(across)).astype(jnp.bfloat16)
    to_wide = (wide_row(down) == across).astype(jnp.bfloat16)

    def normalized_rows(values, gain_row):
        wide_values = values.astype(jnp.float32)
        rows_sq = jnp.sum(wide_values * wide_values, axis=1)
        sent = jnp.broadcast_to(rows_sq[None, :], (wide_count * narrow_count, own_rows))
        landed = lax.all_to_all(sent, ("wide", "narrow"), 0, 0, tiled=True)
        pieces = gather(values, "narrow")
        sums = jnp.sum(landed.reshape(wide_count, narrow_count, own_rows), axis=0)
        sums = by_rank([sums[j] for j in range(narrow_count)], flags)
        order = offsets_of("narrow")
        half = narrow_count // 2
        result = []
        for piece, offsets in zip(pieces, (order[:half], order[half:])):
            sum_sq = jnp.concatenate([sums[offset] for offset in offsets])
            result.append(normalize(piece, gain_row, sum_sq, model_width))
        return result

    rows_in = hidden_in.astype(jnp.float32)
    normed = normalized_rows(hidden_in, attn_gain)

    q_cols = w_query.shape[1]
    k_cols = w_key.shape[1]
    stacked = [(w_query, q_cols), (w_key, k_cols), (w_value, k_cols)]
    heads = (q_cols + 2 * k_cols) // HEAD_DIM
    edges = [heads * chunk // QKV_CHUNKS for chunk in range(QKV_CHUNKS)] + [heads]
    pieces = []
    ordered = to_hypothesis
    for chunk in range(QKV_CHUNKS):
        first, last = edges[chunk] * HEAD_DIM, edges[chunk + 1] * HEAD_DIM
        segments = []
        start = 0
        for weight, columns in stacked:
            low, high = max(first, start), min(last, start + columns)
            if low < high:
                segments.append((weight, 0, low - start, high - low))
            start += columns
        sums = project([normed], ordered, True, segments, 2, direct=True)
        sums, ordered = lax.optimization_barrier((sums, ordered))
        pieces.append(wide_scatter(*sums, jnp.float32))
    summed = jnp.concatenate(pieces, axis=1).astype(jnp.bfloat16)
    summed = summed.reshape(narrow_count, local_rows, -1, HEAD_DIM)
    turned = exchange([summed[j] for j in range(narrow_count)], "narrow")
    turned = jnp.stack(by_rank(turned, flags), axis=1)
    q_heads = q_cols // HEAD_DIM
    k_heads = k_cols // HEAD_DIM
    query_rot = rotate(
        turned[:, :, :q_heads].reshape(local_rows, -1, HEAD_DIM), cache_len
    ).reshape(local_rows, -1)
    key_rot = rotate(
        turned[:, :, q_heads : q_heads + k_heads].reshape(local_rows, -1, HEAD_DIM), cache_len
    ).reshape(local_rows, -1)
    value_new = turned[:, :, q_heads + k_heads :].reshape(local_rows, -1)
    context = attend(query_rot, key_rot, value_new, key_cache, value_cache, cache_len)
    context = context.reshape(local_rows, narrow_count, -1)
    context = by_rank([context[:, j] for j in range(narrow_count)], flags)
    by_heads = exchange(context, "narrow")

    depth = w_out.shape[0] // CONTEXT_CHUNKS
    groups = []
    for chunk in range(CONTEXT_CHUNKS):
        columns = slice(chunk * depth, (chunk + 1) * depth)
        block = jnp.concatenate([piece[:, columns] for piece in by_heads], axis=0)
        groups.append(gather_direct(block, "wide"))
    total = project(groups, to_hypothesis, False, [(w_out, 0, 0, w_out.shape[1])], 2)
    attn_out = narrow_scatter(*total)
    resid = (rows_in + attn_out).astype(jnp.bfloat16)
    resid_wide = resid.astype(jnp.float32)
    normed_two = normalized_rows(resid, ffn_gain)

    f_cols = w_gate.shape[1] // FFN_CHUNKS
    total = None
    for chunk in range(FFN_CHUNKS):
        segments = [(w_gate, 0, chunk * f_cols, f_cols), (w_up, 0, chunk * f_cols, f_cols)]
        sums = wide_scatter(*project([normed_two], to_wide, False, segments, 2, direct=True), jnp.float16)
        act = (jax.nn.silu(sums[:, :f_cols]) * sums[:, f_cols:]).astype(jnp.bfloat16)
        last = chunk == FFN_CHUNKS - 1
        total = project(
            [gather(act, "wide")],
            to_wide,
            True,
            [(w_down, chunk * f_cols, 0, w_down.shape[1])],
            2 if last else 1,
            total if total is None else total[0],
            direct=True,
        )
    ffn_out = narrow_scatter(*total)
    return (resid_wide + ffn_out).astype(jnp.bfloat16)


def solution(mesh):
    return jax.shard_map(
        shards,
        mesh=mesh,
        in_specs=(
            P("narrow", "wide"),
            P("wide"),
            P("wide", "narrow"),
            P("wide", "narrow"),
            P("wide", "narrow"),
            P("narrow", "wide"),
            P("wide"),
            P("wide", "narrow"),
            P("wide", "narrow"),
            P("narrow", "wide"),
            P(("wide", "narrow"), None, None),
            P(("wide", "narrow"), None, None),
            P(("wide", "narrow")),
            P(),
        ),
        out_specs=P("narrow", "wide"),
        check_vma=False,
    )
```

```python
import math

import jax
import jax.numpy as jnp
from jax import lax
from jax.experimental import pallas as pl
from jax.experimental.pallas import tpu as pltpu
from jax.sharding import PartitionSpec as P

HEAD_DIM = 128


NORM_EPSILON = 1e-05
ROPE_BASE = 500000.0


def product(left, right):
    return jnp.dot(left, right, preferred_element_type=jnp.float32)


def normalize(values_in, gain_row, sum_sq, model_width):
    mean_sq = sum_sq / model_width
    scaled = values_in.astype(jnp.float32) * lax.rsqrt(mean_sq + NORM_EPSILON)[:, None]
    return (scaled * gain_row[None, :]).astype(jnp.bfloat16)


def rotate(head_rows, lengths):
    head_size = head_rows.shape[-1]
    half_size = head_size // 2
    inverse_freq = jnp.exp(
        jnp.arange(half_size, dtype=jnp.float32) * (-2.0 * math.log(ROPE_BASE) / head_size)
    )
    angles = lengths.astype(jnp.float32)[:, None] * inverse_freq[None, :]
    cos_part = jnp.cos(angles)[:, None, :]
    sin_part = jnp.sin(angles)[:, None, :]
    front_half = head_rows[..., :half_size].astype(jnp.float32)
    back_half = head_rows[..., half_size:].astype(jnp.float32)
    turned = jnp.concatenate(
        [
            front_half * cos_part - back_half * sin_part,
            back_half * cos_part + front_half * sin_part,
        ],
        axis=-1,
    )
    return turned.astype(jnp.bfloat16)


def attend(queries, fresh_key, fresh_value, key_cache, value_cache, lengths):
    row_count, length, kv_width = key_cache.shape
    groups = kv_width // HEAD_DIM
    group_size = queries.shape[1] // kv_width
    score_scale = 1.0 / math.sqrt(HEAD_DIM)
    query_heads = queries.reshape(row_count, groups, group_size, HEAD_DIM)
    cache_keys = key_cache.reshape(row_count, length, groups, HEAD_DIM)
    cache_values = value_cache.reshape(row_count, length, groups, HEAD_DIM)
    own_key = fresh_key.reshape(row_count, groups, HEAD_DIM)
    own_value = fresh_value.reshape(row_count, groups, HEAD_DIM)
    scores = (
        jnp.einsum("rgqd,rlgd->rgql", query_heads, cache_keys, preferred_element_type=jnp.float32)
        * score_scale
    )
    own_score = (
        jnp.einsum("rgqd,rgd->rgq", query_heads, own_key, preferred_element_type=jnp.float32)
        * score_scale
    )
    valid_pos = jnp.arange(length, dtype=jnp.int32)[None, :] < lengths[:, None]
    scores = jnp.where(valid_pos[:, None, None, :], scores, -jnp.inf)
    row_max = jnp.maximum(jnp.max(scores, axis=3), own_score)
    weights = jnp.exp(scores - row_max[..., None])
    own_weight = jnp.exp(own_score - row_max)
    weight_sum = jnp.sum(weights, axis=3) + own_weight
    probs = (weights / weight_sum[..., None]).astype(jnp.bfloat16)
    own_prob = (own_weight / weight_sum).astype(jnp.bfloat16)
    context = jnp.einsum("rgql,rlgd->rgqd", probs, cache_values, preferred_element_type=jnp.float32)
    context = (
        context
        + own_prob.astype(jnp.float32)[..., None] * own_value.astype(jnp.float32)[:, :, None, :]
    )
    return context.reshape(row_count, groups * group_size * HEAD_DIM).astype(jnp.bfloat16)


QKV_CHUNKS = 3
FFN_CHUNKS = 2
CONTEXT_CHUNKS = 2
NARROW_KINDS = [jnp.float32] + [jnp.bfloat16] * 8
TILE = 512
ROOM = 24
DIRECT_ROOM = 50
IN_FLIGHT = 9
LANES = 128
TOP_CODE = 32700.0
LOG_STEPS = 64.0
STAND_IN = 4
MIB = 1024 * 1024


def swap(block, axis, offset):
    count = lax.axis_size(axis)
    return lax.ppermute(block, axis, [(i, i ^ offset) for i in range(count)])


def strides_of(axis):
    count = lax.axis_size(axis)
    return [1 << bit for bit in range(count.bit_length() - 1)]


def offsets_of(axis):
    order = [0]
    for stride in reversed(strides_of(axis)):
        order = order + [offset ^ stride for offset in order]
    return order


def encoded(values):
    top = jnp.max(jnp.abs(values), axis=1, keepdims=True)
    steps = jnp.floor(jnp.log2(jnp.maximum(top, 1e-30)) * LOG_STEPS + 1.5)
    return jnp.round(values * (TOP_CODE * jnp.exp2(steps * (-1.0 / LOG_STEPS)))), steps


def write_codes(code_ref, place, values, steps_tile):
    codes, steps = encoded(values)
    code_ref[:, place * LANES : (place + 1) * LANES] = codes.astype(jnp.int32).astype(jnp.int16)
    lanes = lax.broadcasted_iota(jnp.int32, (values.shape[0], LANES), 1)
    return jnp.where(lanes == place, steps, steps_tile)


def read_codes(code_ref, place):
    codes = code_ref[:, place * LANES : (place + 1) * LANES]
    steps = code_ref[:, code_ref.shape[1] - LANES :].astype(jnp.int32).astype(jnp.float32)
    scale = jnp.exp2(steps[:, place : place + 1] * (1.0 / LOG_STEPS)) * (1.0 / TOP_CODE)
    return codes.astype(jnp.int32).astype(jnp.float32) * scale


def project(
    groups, order, turned, segments, split, total=None, direct=False, coded=False
):
    rows = order.shape[0]
    depth = groups[0][0].shape[1]
    tiles = []
    width = 0
    for index, (_, first_row, first, columns) in enumerate(segments):
        for start in range(first, first + columns, TILE):
            tile = min(TILE, first + columns - start)
            tiles.append((index, first_row, start, tile, width))
            width += tile
    part = rows // split
    pieces = [piece for group in groups for piece in group]
    count = len(pieces)
    each = count // len(groups)

    def body(*refs):
        piece_refs, order_ref, rest = refs[:count], refs[count], refs[count + 1 :]
        weight_refs, rest = rest[: len(segments)], rest[len(segments) :]
        if total is not None:
            total_ref, rest = rest[0], rest[1:]
        out_refs, rest = rest[:split], rest[split:]
        copies = []
        if direct:
            for place, (index, first_row, start, tile, _) in enumerate(tiles):
                source = weight_refs[index].at[pl.ds(first_row, depth), pl.ds(start, tile)]
                copies.append(pltpu.make_async_copy(source, rest[place], rest[-1].at[place]))
        for copy in copies[:IN_FLIGHT]:
            copy.start()
        lefts = []
        for group in range(len(groups)):
            group_refs = piece_refs[group * each : (group + 1) * each]
            left = lax.dot_general(
                order_ref[...],
                jnp.concatenate([ref[...] for ref in group_refs], axis=0),
                (((0 if turned else 1,), (0,)), ((), ())),
                preferred_element_type=jnp.float32,
            )
            lefts.append(left.astype(jnp.bfloat16))
        steps_tile = jnp.zeros((part, LANES), jnp.float32)
        for number, (index, first_row, start, tile, base) in enumerate(tiles):
            result = None
            for group, left in enumerate(lefts):
                if direct:
                    copies[number].wait()
                    weight = rest[number][...]
                    if number + IN_FLIGHT < len(tiles):
                        copies[number + IN_FLIGHT].start()
                else:
                    weight = weight_refs[index][
                        pl.ds(first_row + group * depth, depth), pl.ds(start, tile)
                    ]
                product = jnp.dot(left, weight, preferred_element_type=jnp.float32)
                result = product if result is None else result + product
            if total is not None:
                result = result + total_ref[:, base : base + tile]
            for place, out_ref in enumerate(out_refs[: 1 if coded else split]):
                out_ref[:, base : base + tile] = result[place * part : (place + 1) * part]
            if coded:
                for column in range(0, tile, LANES):
                    values = result[part:, column : column + LANES]
                    place = (base + column) // LANES
                    steps_tile = write_codes(out_refs[1], place, values, steps_tile)
        if coded:
            out_refs[1][:, width:] = steps_tile.astype(jnp.int32).astype(jnp.int16)

    operands = pieces + [order] + [segment[0] for segment in segments]
    if total is not None:
        operands.append(total)
    in_vmem = pl.BlockSpec(memory_space=pltpu.VMEM)
    specs = [in_vmem] * len(operands)
    out_shape = [jax.ShapeDtypeStruct((part, width), jnp.float32)] * split
    if coded:
        out_shape[1] = jax.ShapeDtypeStruct((part, width + LANES), jnp.int16)
    scratch = []
    if direct:
        for place in range(count + 1, count + 1 + len(segments)):
            specs[place] = pl.BlockSpec(memory_space=pltpu.HBM)
        scratch = [pltpu.VMEM((depth, tile[3]), jnp.bfloat16) for tile in tiles]
        scratch.append(pltpu.SemaphoreType.DMA((len(tiles),)))
    return pl.pallas_call(
        body,
        in_specs=specs,
        out_specs=[in_vmem] * split,
        scratch_shapes=scratch,
        out_shape=out_shape,
        compiler_params=pltpu.CompilerParams(vmem_limit_bytes=(DIRECT_ROOM if direct else ROOM) * MIB),
        cost_estimate=pl.CostEstimate(
            flops=2 * rows * len(groups) * depth * (width + rows),
            bytes_accessed=2 * len(groups) * depth * width + 4 * rows * width,
            transcendentals=0,
        ),
    )(*operands)


def stand_in(array):
    def body(array_ref, copy_ref):
        copy_ref[...] = array_ref[...]

    in_vmem = pl.BlockSpec(memory_space=pltpu.VMEM)
    return pl.pallas_call(
        body,
        in_specs=[in_vmem],
        out_specs=in_vmem,
        out_shape=jax.ShapeDtypeStruct(array.shape, array.dtype),
        compiler_params=pltpu.CompilerParams(vmem_limit_bytes=MIB),
        cost_estimate=pl.CostEstimate(
            flops=int(1.1e9 * STAND_IN), bytes_accessed=4096, transcendentals=0
        ),
    )(array)


def fold(kept, arrived, blocks):
    rows = kept.shape[0] // blocks
    width = kept.shape[1]

    def body(kept_ref, arrived_ref, own_ref, *code_refs):
        tiles = [jnp.zeros((rows, LANES), jnp.float32)] * (blocks - 1)
        for place in range(width // LANES):
            columns = slice(place * LANES, (place + 1) * LANES)
            sums = kept_ref[:, columns] + read_codes(arrived_ref, place)
            own_ref[:, columns] = sums[:rows]
            for index, code_ref in enumerate(code_refs):
                values = sums[(index + 1) * rows : (index + 2) * rows]
                tiles[index] = write_codes(code_ref, place, values, tiles[index])
        for tile, code_ref in zip(tiles, code_refs):
            code_ref[:, width:] = tile.astype(jnp.int32).astype(jnp.int16)

    codes = jax.ShapeDtypeStruct((rows, width + LANES), jnp.int16)
    return pl.pallas_call(
        body,
        out_shape=[jax.ShapeDtypeStruct((rows, width), jnp.float32)] + [codes] * (blocks - 1),
        compiler_params=pltpu.CompilerParams(vmem_limit_bytes=8 * MIB),
    )(kept, arrived)


def add_codes(own, arrived):
    def body(own_ref, *refs):
        for place in range(own.shape[1] // LANES):
            columns = slice(place * LANES, (place + 1) * LANES)
            sums = own_ref[:, columns]
            for code_ref in refs[:-1]:
                sums = sums + read_codes(code_ref, place)
            refs[-1][:, columns] = sums.astype(jnp.bfloat16)

    return pl.pallas_call(
        body,
        out_shape=jax.ShapeDtypeStruct(own.shape, jnp.bfloat16),
        compiler_params=pltpu.CompilerParams(vmem_limit_bytes=8 * MIB),
    )(own, *arrived)


def coded_scatter(kept, sent):
    blocks = lax.axis_size("wide") // 2
    own, *codes = fold(kept, swap(sent, "wide", 1), blocks)
    offsets = offsets_of("wide")[1:blocks]
    return add_codes(own, [swap(code, "wide", o) for code, o in zip(codes, offsets)])


def wide_scatter(kept, sent):
    rows = 2 * kept.shape[0] // lax.axis_size("wide")
    kept = kept + swap(sent.astype(jnp.float16), "wide", 1).astype(jnp.float32)
    total = kept[:rows]
    for place, offset in enumerate(offsets_of("wide")[: kept.shape[0] // rows]):
        if offset:
            block = kept[place * rows : (place + 1) * rows].astype(jnp.float16)
            total = total + swap(block, "wide", offset).astype(jnp.float32)
    return total


def narrow_scatter(kept, sent):
    for stride, kind in zip(strides_of("narrow"), NARROW_KINDS):
        if stride > 1:
            half = kept.shape[0] // 2
            kept, sent = kept[:half], kept[half:]
        kept = kept + swap(sent.astype(kind), "narrow", stride).astype(jnp.float32)
    return kept


def gather(block, axis):
    strides = strides_of(axis)[::-1]
    for stride in strides[:-1]:
        block = jnp.concatenate([block, swap(block, axis, stride)], axis=0)
    return [block, swap(block, axis, strides[-1])]


def gather_direct(block, axis):
    offsets = offsets_of(axis)
    held = [block] + [swap(block, axis, o) for o in offsets[1 : len(offsets) // 2]]
    return [stand_in(block)] + held[1:] + [swap(piece, axis, 1) for piece in held]


def exchange(blocks, axis):
    blocks = list(blocks)
    for stride in strides_of(axis)[::-1]:
        marked = [i for i in range(len(blocks)) if i & stride]
        arrived = swap(jnp.stack([blocks[i] for i in marked]), axis, stride)
        for place, i in enumerate(marked):
            blocks[i] = arrived[place]
    return blocks


def by_rank(blocks, flags):
    for bit, flag in enumerate(flags):
        other = 1 << bit
        blocks = [jnp.where(flag, blocks[i ^ other], block) for i, block in enumerate(blocks)]
    return blocks


def shards(
    hidden_in,
    attn_gain,
    w_query,
    w_key,
    w_value,
    w_out,
    ffn_gain,
    w_gate,
    w_up,
    w_down,
    key_cache,
    value_cache,
    cache_len,
    bank_row,
):
    wide_count = lax.axis_size("wide")
    narrow_count = lax.axis_size("narrow")
    me_wide = lax.axis_index("wide")
    me_narrow = lax.axis_index("narrow")
    flags = [(me_narrow & stride) != 0 for stride in strides_of("narrow")]
    hidden_in, me_wide, me_narrow, flags = lax.optimization_barrier(
        (hidden_in, me_wide, me_narrow, flags)
    )
    model_width = hidden_in.shape[1] * wide_count
    own_rows = hidden_in.shape[0]
    local_rows = cache_len.shape[0]
    all_rows = bank_row.shape[0]
    wide_rows = all_rows // wide_count

    def device(block, axis, me):
        bits = len(strides_of(axis))
        for bit in range(bits):
            me = me ^ (((block >> bit) & 1) << (bits - 1 - bit))
        return me

    def hypothesis(place):
        return device(place // own_rows, "narrow", me_narrow) * own_rows + place % own_rows

    def wide_row(place):
        return device(place // wide_rows, "wide", me_wide) * wide_rows + place % wide_rows

    def bank(place):
        inner = place % wide_rows
        owner = device(place // wide_rows, "wide", me_wide) * narrow_count
        owner = owner + (me_narrow ^ (inner // local_rows))
        return owner * local_rows + inner % local_rows

    down = lax.broadcasted_iota(jnp.int32, (all_rows, all_rows), 0)
    across = lax.broadcasted_iota(jnp.int32, (all_rows, all_rows), 1)
    banks = jnp.broadcast_to(bank_row[None, :], (all_rows, all_rows))
    hypothesis_bank = jnp.sum(
        jnp.where(hypothesis(down) == across, banks, 0), axis=1, keepdims=True
    )
    to_hypothesis = (hypothesis_bank == bank(across)).astype(jnp.bfloat16)
    to_wide = (wide_row(down) == across).astype(jnp.bfloat16)

    def normalized_rows(values, gain_row):
        wide_values = values.astype(jnp.float32)
        rows_sq = jnp.sum(wide_values * wide_values, axis=1)
        sent = jnp.broadcast_to(rows_sq[None, :], (wide_count * narrow_count, own_rows))
        landed = lax.all_to_all(sent, ("wide", "narrow"), 0, 0, tiled=True)
        pieces = gather(values, "narrow")
        sums = jnp.sum(landed.reshape(wide_count, narrow_count, own_rows), axis=0)
        sums = by_rank([sums[j] for j in range(narrow_count)], flags)
        order = offsets_of("narrow")
        half = narrow_count // 2
        result = []
        for piece, offsets in zip(pieces, (order[:half], order[half:])):
            sum_sq = jnp.concatenate([sums[offset] for offset in offsets])
            result.append(normalize(piece, gain_row, sum_sq, model_width))
        return result

    rows_in = hidden_in.astype(jnp.float32)
    normed = normalized_rows(hidden_in, attn_gain)

    q_cols = w_query.shape[1]
    k_cols = w_key.shape[1]
    stacked = [(w_query, q_cols), (w_key, k_cols), (w_value, k_cols)]
    heads = (q_cols + 2 * k_cols) // HEAD_DIM
    edges = [heads * chunk // QKV_CHUNKS for chunk in range(QKV_CHUNKS)] + [heads]
    pieces = []
    ordered = to_hypothesis
    for chunk in range(QKV_CHUNKS):
        first, last = edges[chunk] * HEAD_DIM, edges[chunk + 1] * HEAD_DIM
        segments = []
        start = 0
        for weight, columns in stacked:
            low, high = max(first, start), min(last, start + columns)
            if low < high:
                segments.append((weight, 0, low - start, high - low))
            start += columns
        sums = project([normed], ordered, True, segments, 2, direct=True, coded=True)
        sums, ordered = lax.optimization_barrier((sums, ordered))
        pieces.append(coded_scatter(*sums))
    summed = jnp.concatenate(pieces, axis=1)
    summed = summed.reshape(narrow_count, local_rows, -1, HEAD_DIM)
    turned = exchange([summed[j] for j in range(narrow_count)], "narrow")
    turned = jnp.stack(by_rank(turned, flags), axis=1)
    q_heads = q_cols // HEAD_DIM
    k_heads = k_cols // HEAD_DIM
    query_rot = rotate(
        turned[:, :, :q_heads].reshape(local_rows, -1, HEAD_DIM), cache_len
    ).reshape(local_rows, -1)
    key_rot = rotate(
        turned[:, :, q_heads : q_heads + k_heads].reshape(local_rows, -1, HEAD_DIM), cache_len
    ).reshape(local_rows, -1)
    value_new = turned[:, :, q_heads + k_heads :].reshape(local_rows, -1)
    context = attend(query_rot, key_rot, value_new, key_cache, value_cache, cache_len)
    context = context.reshape(local_rows, narrow_count, -1)
    context = by_rank([context[:, j] for j in range(narrow_count)], flags)
    by_heads = exchange(context, "narrow")

    depth = w_out.shape[0] // CONTEXT_CHUNKS
    groups = []
    for chunk in range(CONTEXT_CHUNKS):
        columns = slice(chunk * depth, (chunk + 1) * depth)
        block = jnp.concatenate([piece[:, columns] for piece in by_heads], axis=0)
        groups.append(gather_direct(block, "wide"))
    total = project(groups, to_hypothesis, False, [(w_out, 0, 0, w_out.shape[1])], 2)
    attn_out = narrow_scatter(*total)
    resid = (rows_in + attn_out).astype(jnp.bfloat16)
    resid_wide = resid.astype(jnp.float32)
    normed_two = normalized_rows(resid, ffn_gain)

    f_cols = w_gate.shape[1] // FFN_CHUNKS
    total = None
    for chunk in range(FFN_CHUNKS):
        segments = [(w_gate, 0, chunk * f_cols, f_cols), (w_up, 0, chunk * f_cols, f_cols)]
        sums = wide_scatter(*project([normed_two], to_wide, False, segments, 2, direct=True))
        act = (jax.nn.silu(sums[:, :f_cols]) * sums[:, f_cols:]).astype(jnp.bfloat16)
        last = chunk == FFN_CHUNKS - 1
        total = project(
            [gather(act, "wide")],
            to_wide,
            True,
            [(w_down, chunk * f_cols, 0, w_down.shape[1])],
            2 if last else 1,
            total if total is None else total[0],
            direct=True,
        )
    ffn_out = narrow_scatter(*total)
    return (resid_wide + ffn_out).astype(jnp.bfloat16)


def solution(mesh):
    return jax.shard_map(
        shards,
        mesh=mesh,
        in_specs=(
            P("narrow", "wide"),
            P("wide"),
            P("wide", "narrow"),
            P("wide", "narrow"),
            P("wide", "narrow"),
            P("narrow", "wide"),
            P("wide"),
            P("wide", "narrow"),
            P("wide", "narrow"),
            P("narrow", "wide"),
            P(("wide", "narrow"), None, None),
            P(("wide", "narrow"), None, None),
            P(("wide", "narrow")),
            P(),
        ),
        out_specs=P("narrow", "wide"),
        check_vma=False,
    )
```

```python
import math

import jax
import jax.numpy as jnp
from jax import lax
from jax.experimental import pallas as pl
from jax.experimental.pallas import tpu as pltpu
from jax.sharding import PartitionSpec as P

HEAD_DIM = 128


NORM_EPSILON = 1e-05
ROPE_BASE = 500000.0


def product(left, right):
    return jnp.dot(left, right, preferred_element_type=jnp.float32)


def normalize(values_in, gain_row, sum_sq, model_width):
    mean_sq = sum_sq / model_width
    scaled = values_in.astype(jnp.float32) * lax.rsqrt(mean_sq + NORM_EPSILON)[:, None]
    return (scaled * gain_row[None, :]).astype(jnp.bfloat16)


def rotate(head_rows, lengths):
    head_size = head_rows.shape[-1]
    half_size = head_size // 2
    inverse_freq = jnp.exp(
        jnp.arange(half_size, dtype=jnp.float32) * (-2.0 * math.log(ROPE_BASE) / head_size)
    )
    angles = lengths.astype(jnp.float32)[:, None] * inverse_freq[None, :]
    cos_part = jnp.cos(angles)[:, None, :]
    sin_part = jnp.sin(angles)[:, None, :]
    front_half = head_rows[..., :half_size].astype(jnp.float32)
    back_half = head_rows[..., half_size:].astype(jnp.float32)
    turned = jnp.concatenate(
        [
            front_half * cos_part - back_half * sin_part,
            back_half * cos_part + front_half * sin_part,
        ],
        axis=-1,
    )
    return turned.astype(jnp.bfloat16)


def attend(queries, fresh_key, fresh_value, key_cache, value_cache, lengths):
    row_count, length, kv_width = key_cache.shape
    groups = kv_width // HEAD_DIM
    group_size = queries.shape[1] // kv_width
    score_scale = 1.0 / math.sqrt(HEAD_DIM)
    query_heads = queries.reshape(row_count, groups, group_size, HEAD_DIM)
    cache_keys = key_cache.reshape(row_count, length, groups, HEAD_DIM)
    cache_values = value_cache.reshape(row_count, length, groups, HEAD_DIM)
    own_key = fresh_key.reshape(row_count, groups, HEAD_DIM)
    own_value = fresh_value.reshape(row_count, groups, HEAD_DIM)
    scores = (
        jnp.einsum("rgqd,rlgd->rgql", query_heads, cache_keys, preferred_element_type=jnp.float32)
        * score_scale
    )
    own_score = (
        jnp.einsum("rgqd,rgd->rgq", query_heads, own_key, preferred_element_type=jnp.float32)
        * score_scale
    )
    valid_pos = jnp.arange(length, dtype=jnp.int32)[None, :] < lengths[:, None]
    scores = jnp.where(valid_pos[:, None, None, :], scores, -jnp.inf)
    row_max = jnp.maximum(jnp.max(scores, axis=3), own_score)
    weights = jnp.exp(scores - row_max[..., None])
    own_weight = jnp.exp(own_score - row_max)
    weight_sum = jnp.sum(weights, axis=3) + own_weight
    probs = (weights / weight_sum[..., None]).astype(jnp.bfloat16)
    own_prob = (own_weight / weight_sum).astype(jnp.bfloat16)
    context = jnp.einsum("rgql,rlgd->rgqd", probs, cache_values, preferred_element_type=jnp.float32)
    context = (
        context
        + own_prob.astype(jnp.float32)[..., None] * own_value.astype(jnp.float32)[:, :, None, :]
    )
    return context.reshape(row_count, groups * group_size * HEAD_DIM).astype(jnp.bfloat16)


QKV_CHUNKS = 3
FFN_SPLIT = 0.625
CONTEXT_CHUNKS = 2
NARROW_KINDS = [jnp.float32] + [jnp.bfloat16] * 8
TILE = 512
ROOM = 24
DIRECT_ROOM = 50
IN_FLIGHT = 9
LANES = 128
TOP_CODE = 32700.0
LOG_STEPS = 64.0
STAND_IN = 4
MIB = 1024 * 1024


def swap(block, axis, offset):
    count = lax.axis_size(axis)
    return lax.ppermute(block, axis, [(i, i ^ offset) for i in range(count)])


def strides_of(axis):
    count = lax.axis_size(axis)
    return [1 << bit for bit in range(count.bit_length() - 1)]


def offsets_of(axis):
    order = [0]
    for stride in reversed(strides_of(axis)):
        order = order + [offset ^ stride for offset in order]
    return order


def encoded(values):
    top = jnp.max(jnp.abs(values), axis=1, keepdims=True)
    steps = jnp.floor(jnp.log2(jnp.maximum(top, 1e-30)) * LOG_STEPS + 1.5)
    return jnp.round(values * (TOP_CODE * jnp.exp2(steps * (-1.0 / LOG_STEPS)))), steps


def write_codes(code_ref, place, values, steps_tile):
    codes, steps = encoded(values)
    code_ref[:, place * LANES : (place + 1) * LANES] = codes.astype(jnp.int32).astype(jnp.int16)
    lanes = lax.broadcasted_iota(jnp.int32, (values.shape[0], LANES), 1)
    return jnp.where(lanes == place, steps, steps_tile)


def read_codes(code_ref, place):
    codes = code_ref[:, place * LANES : (place + 1) * LANES]
    steps = code_ref[:, code_ref.shape[1] - LANES :].astype(jnp.int32).astype(jnp.float32)
    scale = jnp.exp2(steps[:, place : place + 1] * (1.0 / LOG_STEPS)) * (1.0 / TOP_CODE)
    return codes.astype(jnp.int32).astype(jnp.float32) * scale


def project(
    groups, order, turned, segments, split, total=None, direct=False, coded=False
):
    rows = order.shape[0]
    depth = groups[0][0].shape[1]
    tiles = []
    width = 0
    for index, (_, first_row, first, columns) in enumerate(segments):
        for start in range(first, first + columns, TILE):
            tile = min(TILE, first + columns - start)
            tiles.append((index, first_row, start, tile, width))
            width += tile
    part = rows // split
    pieces = [piece for group in groups for piece in group]
    count = len(pieces)
    each = count // len(groups)

    def body(*refs):
        piece_refs, order_ref, rest = refs[:count], refs[count], refs[count + 1 :]
        weight_refs, rest = rest[: len(segments)], rest[len(segments) :]
        if total is not None:
            total_ref, rest = rest[0], rest[1:]
        out_refs, rest = rest[:split], rest[split:]
        copies = []
        if direct:
            for place, (index, first_row, start, tile, _) in enumerate(tiles):
                source = weight_refs[index].at[pl.ds(first_row, depth), pl.ds(start, tile)]
                copies.append(pltpu.make_async_copy(source, rest[place], rest[-1].at[place]))
        for copy in copies[:IN_FLIGHT]:
            copy.start()
        lefts = []
        for group in range(len(groups)):
            group_refs = piece_refs[group * each : (group + 1) * each]
            left = lax.dot_general(
                order_ref[...],
                jnp.concatenate([ref[...] for ref in group_refs], axis=0),
                (((0 if turned else 1,), (0,)), ((), ())),
                preferred_element_type=jnp.float32,
            )
            lefts.append(left.astype(jnp.bfloat16))
        steps_tile = jnp.zeros((part, LANES), jnp.float32)
        for number, (index, first_row, start, tile, base) in enumerate(tiles):
            result = None
            for group, left in enumerate(lefts):
                if direct:
                    copies[number].wait()
                    weight = rest[number][...]
                    if number + IN_FLIGHT < len(tiles):
                        copies[number + IN_FLIGHT].start()
                else:
                    weight = weight_refs[index][
                        pl.ds(first_row + group * depth, depth), pl.ds(start, tile)
                    ]
                product = jnp.dot(left, weight, preferred_element_type=jnp.float32)
                result = product if result is None else result + product
            if total is not None:
                result = result + total_ref[:, base : base + tile]
            for place, out_ref in enumerate(out_refs[: 1 if coded else split]):
                out_ref[:, base : base + tile] = result[place * part : (place + 1) * part]
            if coded:
                for column in range(0, tile, LANES):
                    values = result[part:, column : column + LANES]
                    place = (base + column) // LANES
                    steps_tile = write_codes(out_refs[1], place, values, steps_tile)
        if coded:
            out_refs[1][:, width:] = steps_tile.astype(jnp.int32).astype(jnp.int16)

    operands = pieces + [order] + [segment[0] for segment in segments]
    if total is not None:
        operands.append(total)
    in_vmem = pl.BlockSpec(memory_space=pltpu.VMEM)
    specs = [in_vmem] * len(operands)
    out_shape = [jax.ShapeDtypeStruct((part, width), jnp.float32)] * split
    if coded:
        out_shape[1] = jax.ShapeDtypeStruct((part, width + LANES), jnp.int16)
    scratch = []
    if direct:
        for place in range(count + 1, count + 1 + len(segments)):
            specs[place] = pl.BlockSpec(memory_space=pltpu.HBM)
        scratch = [pltpu.VMEM((depth, tile[3]), jnp.bfloat16) for tile in tiles]
        scratch.append(pltpu.SemaphoreType.DMA((len(tiles),)))
    return pl.pallas_call(
        body,
        in_specs=specs,
        out_specs=[in_vmem] * split,
        scratch_shapes=scratch,
        out_shape=out_shape,
        compiler_params=pltpu.CompilerParams(vmem_limit_bytes=(DIRECT_ROOM if direct else ROOM) * MIB),
        cost_estimate=pl.CostEstimate(
            flops=2 * rows * len(groups) * depth * (width + rows),
            bytes_accessed=2 * len(groups) * depth * width + 4 * rows * width,
            transcendentals=0,
        ),
    )(*operands)


def stand_in(array):
    def body(array_ref, copy_ref):
        copy_ref[...] = array_ref[...]

    in_vmem = pl.BlockSpec(memory_space=pltpu.VMEM)
    return pl.pallas_call(
        body,
        in_specs=[in_vmem],
        out_specs=in_vmem,
        out_shape=jax.ShapeDtypeStruct(array.shape, array.dtype),
        compiler_params=pltpu.CompilerParams(vmem_limit_bytes=MIB),
        cost_estimate=pl.CostEstimate(
            flops=int(1.1e9 * STAND_IN), bytes_accessed=4096, transcendentals=0
        ),
    )(array)


def fold(kept, arrived, blocks):
    rows = kept.shape[0] // blocks
    width = kept.shape[1]

    def body(kept_ref, arrived_ref, own_ref, *code_refs):
        tiles = [jnp.zeros((rows, LANES), jnp.float32)] * (blocks - 1)
        for place in range(width // LANES):
            columns = slice(place * LANES, (place + 1) * LANES)
            sums = kept_ref[:, columns] + read_codes(arrived_ref, place)
            own_ref[:, columns] = sums[:rows]
            for index, code_ref in enumerate(code_refs):
                values = sums[(index + 1) * rows : (index + 2) * rows]
                tiles[index] = write_codes(code_ref, place, values, tiles[index])
        for tile, code_ref in zip(tiles, code_refs):
            code_ref[:, width:] = tile.astype(jnp.int32).astype(jnp.int16)

    codes = jax.ShapeDtypeStruct((rows, width + LANES), jnp.int16)
    return pl.pallas_call(
        body,
        out_shape=[jax.ShapeDtypeStruct((rows, width), jnp.float32)] + [codes] * (blocks - 1),
        compiler_params=pltpu.CompilerParams(vmem_limit_bytes=8 * MIB),
    )(kept, arrived)


def add_codes(own, arrived):
    def body(own_ref, *refs):
        for place in range(own.shape[1] // LANES):
            columns = slice(place * LANES, (place + 1) * LANES)
            sums = own_ref[:, columns]
            for code_ref in refs[:-1]:
                sums = sums + read_codes(code_ref, place)
            refs[-1][:, columns] = sums.astype(jnp.bfloat16)

    return pl.pallas_call(
        body,
        out_shape=jax.ShapeDtypeStruct(own.shape, jnp.bfloat16),
        compiler_params=pltpu.CompilerParams(vmem_limit_bytes=8 * MIB),
    )(own, *arrived)


def coded_scatter(kept, arrived):
    blocks = lax.axis_size("wide") // 2
    own, *codes = fold(kept, arrived, blocks)
    offsets = offsets_of("wide")[1:blocks]
    return add_codes(own, [swap(code, "wide", o) for code, o in zip(codes, offsets)])


def wide_scatter(kept, sent):
    rows = 2 * kept.shape[0] // lax.axis_size("wide")
    kept = kept + swap(sent.astype(jnp.float16), "wide", 1).astype(jnp.float32)
    total = kept[:rows]
    for place, offset in enumerate(offsets_of("wide")[: kept.shape[0] // rows]):
        if offset:
            block = kept[place * rows : (place + 1) * rows].astype(jnp.float16)
            total = total + swap(block, "wide", offset).astype(jnp.float32)
    return total


def narrow_scatter(kept, sent):
    for stride, kind in zip(strides_of("narrow"), NARROW_KINDS):
        if stride > 1:
            half = kept.shape[0] // 2
            kept, sent = kept[:half], kept[half:]
        kept = kept + swap(sent.astype(kind), "narrow", stride).astype(jnp.float32)
    return kept


def gather(block, axis, paired=False):
    strides = strides_of(axis)[::-1]
    for stride in strides[:-1]:
        held = stand_in(block) if paired else block
        block = jnp.concatenate([held, swap(block, axis, stride)], axis=0)
    return [block, swap(block, axis, strides[-1])]


def gather_direct(block, axis):
    offsets = offsets_of(axis)
    held = [block] + [swap(block, axis, o) for o in offsets[1 : len(offsets) // 2]]
    return [stand_in(block)] + held[1:] + [swap(piece, axis, 1) for piece in held]


def exchange(blocks, axis):
    blocks = list(blocks)
    for stride in strides_of(axis)[::-1]:
        marked = [i for i in range(len(blocks)) if i & stride]
        arrived = swap(jnp.stack([blocks[i] for i in marked]), axis, stride)
        for place, i in enumerate(marked):
            blocks[i] = arrived[place]
    return blocks


def by_rank(blocks, flags):
    for bit, flag in enumerate(flags):
        other = 1 << bit
        blocks = [jnp.where(flag, blocks[i ^ other], block) for i, block in enumerate(blocks)]
    return blocks


def shards(
    hidden_in,
    attn_gain,
    w_query,
    w_key,
    w_value,
    w_out,
    ffn_gain,
    w_gate,
    w_up,
    w_down,
    key_cache,
    value_cache,
    cache_len,
    bank_row,
):
    wide_count = lax.axis_size("wide")
    narrow_count = lax.axis_size("narrow")
    me_wide = lax.axis_index("wide")
    me_narrow = lax.axis_index("narrow")
    flags = [(me_narrow & stride) != 0 for stride in strides_of("narrow")]
    hidden_in, me_wide, me_narrow, flags = lax.optimization_barrier(
        (hidden_in, me_wide, me_narrow, flags)
    )
    model_width = hidden_in.shape[1] * wide_count
    own_rows = hidden_in.shape[0]
    local_rows = cache_len.shape[0]
    all_rows = bank_row.shape[0]
    wide_rows = all_rows // wide_count

    def device(block, axis, me):
        bits = len(strides_of(axis))
        for bit in range(bits):
            me = me ^ (((block >> bit) & 1) << (bits - 1 - bit))
        return me

    def hypothesis(place):
        return device(place // own_rows, "narrow", me_narrow) * own_rows + place % own_rows

    def wide_row(place):
        return device(place // wide_rows, "wide", me_wide) * wide_rows + place % wide_rows

    def bank(place):
        inner = place % wide_rows
        owner = device(place // wide_rows, "wide", me_wide) * narrow_count
        owner = owner + (me_narrow ^ (inner // local_rows))
        return owner * local_rows + inner % local_rows

    down = lax.broadcasted_iota(jnp.int32, (all_rows, all_rows), 0)
    across = lax.broadcasted_iota(jnp.int32, (all_rows, all_rows), 1)
    banks = jnp.broadcast_to(bank_row[None, :], (all_rows, all_rows))
    hypothesis_bank = jnp.sum(
        jnp.where(hypothesis(down) == across, banks, 0), axis=1, keepdims=True
    )
    to_hypothesis = (hypothesis_bank == bank(across)).astype(jnp.bfloat16)
    to_wide = (wide_row(down) == across).astype(jnp.bfloat16)

    def normalized_rows(values, gain_row):
        wide_values = values.astype(jnp.float32)
        rows_sq = jnp.sum(wide_values * wide_values, axis=1)
        sent = jnp.broadcast_to(rows_sq[None, :], (wide_count * narrow_count, own_rows))
        landed = lax.all_to_all(sent, ("wide", "narrow"), 0, 0, tiled=True)
        pieces = gather(values, "narrow")
        sums = jnp.sum(landed.reshape(wide_count, narrow_count, own_rows), axis=0)
        sums = by_rank([sums[j] for j in range(narrow_count)], flags)
        order = offsets_of("narrow")
        half = narrow_count // 2
        result = []
        for piece, offsets in zip(pieces, (order[:half], order[half:])):
            sum_sq = jnp.concatenate([sums[offset] for offset in offsets])
            result.append(normalize(piece, gain_row, sum_sq, model_width))
        return result

    rows_in = hidden_in.astype(jnp.float32)
    normed = normalized_rows(hidden_in, attn_gain)

    q_cols = w_query.shape[1]
    k_cols = w_key.shape[1]
    stacked = [(w_query, q_cols), (w_key, k_cols), (w_value, k_cols)]
    heads = (q_cols + 2 * k_cols) // HEAD_DIM
    edges = [heads * chunk // QKV_CHUNKS for chunk in range(QKV_CHUNKS)] + [heads]
    pieces = []
    arrivals = []
    ordered = to_hypothesis
    for chunk in range(QKV_CHUNKS):
        first, last = edges[chunk] * HEAD_DIM, edges[chunk + 1] * HEAD_DIM
        segments = []
        start = 0
        for weight, columns in stacked:
            low, high = max(first, start), min(last, start + columns)
            if low < high:
                segments.append((weight, 0, low - start, high - low))
            start += columns
        if chunk >= 2:
            ordered, arrivals[chunk - 2] = lax.optimization_barrier((ordered, arrivals[chunk - 2]))
        (kept, sent), ordered = lax.optimization_barrier(
            (project([normed], ordered, True, segments, 2, direct=True, coded=True), ordered)
        )
        pieces.append(kept)
        arrivals.append(swap(sent, "wide", 1))
    pieces = [coded_scatter(kept, arrived) for kept, arrived in zip(pieces, arrivals)]
    summed = jnp.concatenate(pieces, axis=1)
    summed = summed.reshape(narrow_count, local_rows, -1, HEAD_DIM)
    turned = exchange([summed[j] for j in range(narrow_count)], "narrow")
    turned = jnp.stack(by_rank(turned, flags), axis=1)
    q_heads = q_cols // HEAD_DIM
    k_heads = k_cols // HEAD_DIM
    query_rot = rotate(
        turned[:, :, :q_heads].reshape(local_rows, -1, HEAD_DIM), cache_len
    ).reshape(local_rows, -1)
    key_rot = rotate(
        turned[:, :, q_heads : q_heads + k_heads].reshape(local_rows, -1, HEAD_DIM), cache_len
    ).reshape(local_rows, -1)
    value_new = turned[:, :, q_heads + k_heads :].reshape(local_rows, -1)
    context = attend(query_rot, key_rot, value_new, key_cache, value_cache, cache_len)
    context = context.reshape(local_rows, narrow_count, -1)
    context = by_rank([context[:, j] for j in range(narrow_count)], flags)
    by_heads = exchange(context, "narrow")

    depth = w_out.shape[0] // CONTEXT_CHUNKS
    groups = []
    for chunk in range(CONTEXT_CHUNKS):
        columns = slice(chunk * depth, (chunk + 1) * depth)
        block = jnp.concatenate([piece[:, columns] for piece in by_heads], axis=0)
        groups.append(gather_direct(block, "wide"))
    total = project(groups, to_hypothesis, False, [(w_out, 0, 0, w_out.shape[1])], 2)
    attn_out = narrow_scatter(*total)
    resid = (rows_in + attn_out).astype(jnp.bfloat16)
    resid_wide = resid.astype(jnp.float32)
    normed_two = normalized_rows(resid, ffn_gain)

    f_total = w_gate.shape[1]
    f_edge = int(f_total * FFN_SPLIT) // LANES * LANES
    total = None
    for first, last in ((0, f_edge), (f_edge, f_total)):
        f_cols = last - first
        segments = [(w_gate, 0, first, f_cols), (w_up, 0, first, f_cols)]
        sums, normed_two = lax.optimization_barrier(
            (project([normed_two], to_wide, False, segments, 2, direct=True), normed_two)
        )
        sums = wide_scatter(*sums)
        act = (jax.nn.silu(sums[:, :f_cols]) * sums[:, f_cols:]).astype(jnp.bfloat16)
        total = project(
            [gather(act, "wide", paired=True)],
            to_wide,
            True,
            [(w_down, first, 0, w_down.shape[1])],
            2 if last == f_total else 1,
            total if total is None else total[0],
        )
    ffn_out = narrow_scatter(*total)
    return (resid_wide + ffn_out).astype(jnp.bfloat16)


def solution(mesh):
    return jax.shard_map(
        shards,
        mesh=mesh,
        in_specs=(
            P("narrow", "wide"),
            P("wide"),
            P("wide", "narrow"),
            P("wide", "narrow"),
            P("wide", "narrow"),
            P("narrow", "wide"),
            P("wide"),
            P("wide", "narrow"),
            P("wide", "narrow"),
            P("narrow", "wide"),
            P(("wide", "narrow"), None, None),
            P(("wide", "narrow"), None, None),
            P(("wide", "narrow")),
            P(),
        ),
        out_specs=P("narrow", "wide"),
        check_vma=False,
    )
```

```python
import math

import jax
import jax.numpy as jnp
from jax import lax
from jax.experimental import pallas as pl
from jax.experimental.pallas import tpu as pltpu
from jax.sharding import PartitionSpec as P

HEAD_DIM = 128


NORM_EPSILON = 1e-05
ROPE_BASE = 500000.0


def product(left, right):
    return jnp.dot(left, right, preferred_element_type=jnp.float32)


def normalize(values_in, gain_row, sum_sq, model_width):
    mean_sq = sum_sq / model_width
    scaled = values_in.astype(jnp.float32) * lax.rsqrt(mean_sq + NORM_EPSILON)[:, None]
    return (scaled * gain_row[None, :]).astype(jnp.bfloat16)


QKV_CHUNKS = 3
FFN_SPLIT = 0.5
CONTEXT_CHUNKS = 2
NARROW_KINDS = [jnp.float32] + [jnp.bfloat16] * 8
TILE = 512
ROOM = 24
DIRECT_ROOM = 50
IN_FLIGHT = 9
LANES = 128
TOP_CODE = 32700.0
LOG_STEPS = 64.0
STAND_IN = 4
MIB = 1024 * 1024


def swap(block, axis, offset):
    count = lax.axis_size(axis)
    return lax.ppermute(block, axis, [(i, i ^ offset) for i in range(count)])


def strides_of(axis):
    count = lax.axis_size(axis)
    return [1 << bit for bit in range(count.bit_length() - 1)]


def offsets_of(axis):
    order = [0]
    for stride in reversed(strides_of(axis)):
        order = order + [offset ^ stride for offset in order]
    return order


def attend(queries, fresh, key_cache, value_cache, lengths, me):
    count, row_count, heads, _ = queries.shape
    groups = fresh.shape[2] // 2
    group_size = heads // groups
    length = key_cache.shape[1]
    half_size = HEAD_DIM // 2
    score_scale = 1.0 / math.sqrt(HEAD_DIM)
    inverse_freq = jnp.exp(
        jnp.arange(half_size, dtype=jnp.float32) * (-2.0 * math.log(ROPE_BASE) / HEAD_DIM)
    )
    angles = lengths.astype(jnp.float32)[:, None] * inverse_freq[None, :]
    cosines = jnp.concatenate([jnp.cos(angles)] * 2, axis=1)
    sines = jnp.concatenate([-jnp.sin(angles), jnp.sin(angles)], axis=1)

    def body(me_ref, length_ref, query_ref, fresh_ref, cos_ref, sin_ref, key_ref, value_ref, out_ref):
        places = lax.broadcasted_iota(jnp.int32, (group_size, length), 1)
        for row in range(row_count):
            cos_row, sin_row = cos_ref[row : row + 1, :], sin_ref[row : row + 1, :]
            valid = places < length_ref[row]

            def turn(values):
                turned = values * cos_row + pltpu.roll(values, half_size, 1) * sin_row
                return turned.astype(jnp.bfloat16)

            for offset in range(count):
                fresh_rows = fresh_ref[offset, row]
                own_keys = turn(jnp.concatenate([fresh_rows] * (8 // (2 * groups)), axis=0))
                for group in range(groups):
                    heads_of = slice(group * group_size, (group + 1) * group_size)
                    query = turn(query_ref[offset, row, heads_of, :].astype(jnp.float32))
                    first = ((me_ref[0] ^ offset) * groups + group) * HEAD_DIM
                    columns = pl.ds(pl.multiple_of(first, HEAD_DIM), HEAD_DIM)
                    scores = lax.dot_general(
                        query,
                        key_ref[row, :, columns],
                        (((1,), (1,)), ((), ())),
                        preferred_element_type=jnp.float32,
                    )
                    scores = jnp.where(valid, scores * score_scale, -jnp.inf)
                    own_key = own_keys[group : group + 1].astype(jnp.float32)
                    own_score = jnp.sum(query.astype(jnp.float32) * own_key, axis=1, keepdims=True)
                    own_score = own_score * score_scale
                    row_max = jnp.maximum(jnp.max(scores, axis=1, keepdims=True), own_score)
                    weights = jnp.exp(scores - row_max)
                    own_weight = jnp.exp(own_score - row_max)
                    weight_sum = jnp.sum(weights, axis=1, keepdims=True) + own_weight
                    probs = (weights / weight_sum).astype(jnp.bfloat16)
                    own_prob = (own_weight / weight_sum).astype(jnp.bfloat16).astype(jnp.float32)
                    context = jnp.dot(
                        probs, value_ref[row, :, columns], preferred_element_type=jnp.float32
                    )
                    own_value = fresh_rows[groups + group : groups + group + 1]
                    context = context + own_prob * own_value
                    out_ref[offset, row, heads_of, :] = context.astype(jnp.bfloat16)

    in_vmem = pl.BlockSpec(memory_space=pltpu.VMEM)
    in_smem = pl.BlockSpec(memory_space=pltpu.SMEM)
    return pl.pallas_call(
        body,
        in_specs=[in_smem, in_smem] + [in_vmem] * 6,
        out_specs=in_vmem,
        out_shape=jax.ShapeDtypeStruct(queries.shape, jnp.bfloat16),
        compiler_params=pltpu.CompilerParams(vmem_limit_bytes=ROOM * MIB),
        cost_estimate=pl.CostEstimate(
            flops=4 * queries.size * length,
            bytes_accessed=4 * key_cache.size,
            transcendentals=queries.size * length // HEAD_DIM,
        ),
    )(me[None], lengths, queries, fresh, cosines, sines, key_cache, value_cache)


def encoded(values):
    top = jnp.max(jnp.abs(values), axis=1, keepdims=True)
    steps = jnp.floor(jnp.log2(jnp.maximum(top, 1e-30)) * LOG_STEPS + 1.5)
    return jnp.round(values * (TOP_CODE * jnp.exp2(steps * (-1.0 / LOG_STEPS)))), steps


def write_codes(code_ref, place, values, steps_tile):
    codes, steps = encoded(values)
    code_ref[:, place * LANES : (place + 1) * LANES] = codes.astype(jnp.int32).astype(jnp.int16)
    lanes = lax.broadcasted_iota(jnp.int32, (values.shape[0], LANES), 1)
    return jnp.where(lanes == place, steps, steps_tile)


def read_codes(code_ref, place):
    codes = code_ref[:, place * LANES : (place + 1) * LANES]
    steps = code_ref[:, code_ref.shape[1] - LANES :].astype(jnp.int32).astype(jnp.float32)
    scale = jnp.exp2(steps[:, place : place + 1] * (1.0 / LOG_STEPS)) * (1.0 / TOP_CODE)
    return codes.astype(jnp.int32).astype(jnp.float32) * scale


def project(
    groups, order, turned, segments, split, total=None, direct=False, coded=False
):
    rows = order.shape[0]
    depth = groups[0][0].shape[1]
    tiles = []
    width = 0
    for index, (_, first_row, first, columns) in enumerate(segments):
        for start in range(first, first + columns, TILE):
            tile = min(TILE, first + columns - start)
            tiles.append((index, first_row, start, tile, width))
            width += tile
    part = rows // split
    pieces = [piece for group in groups for piece in group]
    count = len(pieces)
    each = count // len(groups)

    def body(*refs):
        piece_refs, order_ref, rest = refs[:count], refs[count], refs[count + 1 :]
        weight_refs, rest = rest[: len(segments)], rest[len(segments) :]
        if total is not None:
            total_ref, rest = rest[0], rest[1:]
        out_refs, rest = rest[:split], rest[split:]
        copies = []
        if direct:
            for place, (index, first_row, start, tile, _) in enumerate(tiles):
                source = weight_refs[index].at[pl.ds(first_row, depth), pl.ds(start, tile)]
                copies.append(pltpu.make_async_copy(source, rest[place], rest[-1].at[place]))
        for copy in copies[:IN_FLIGHT]:
            copy.start()
        lefts = []
        for group in range(len(groups)):
            group_refs = piece_refs[group * each : (group + 1) * each]
            left = lax.dot_general(
                order_ref[...],
                jnp.concatenate([ref[...] for ref in group_refs], axis=0),
                (((0 if turned else 1,), (0,)), ((), ())),
                preferred_element_type=jnp.float32,
            )
            lefts.append(left.astype(jnp.bfloat16))
        steps_tile = jnp.zeros((part, LANES), jnp.float32)
        for number, (index, first_row, start, tile, base) in enumerate(tiles):
            result = None
            for group, left in enumerate(lefts):
                if direct:
                    copies[number].wait()
                    weight = rest[number][...]
                    if number + IN_FLIGHT < len(tiles):
                        copies[number + IN_FLIGHT].start()
                else:
                    weight = weight_refs[index][
                        pl.ds(first_row + group * depth, depth), pl.ds(start, tile)
                    ]
                product = jnp.dot(left, weight, preferred_element_type=jnp.float32)
                result = product if result is None else result + product
            if total is not None:
                result = result + total_ref[:, base : base + tile]
            for place, out_ref in enumerate(out_refs[: 1 if coded else split]):
                out_ref[:, base : base + tile] = result[place * part : (place + 1) * part]
            if coded:
                for column in range(0, tile, LANES):
                    values = result[part:, column : column + LANES]
                    place = (base + column) // LANES
                    steps_tile = write_codes(out_refs[1], place, values, steps_tile)
        if coded:
            out_refs[1][:, width:] = steps_tile.astype(jnp.int32).astype(jnp.int16)

    operands = pieces + [order] + [segment[0] for segment in segments]
    if total is not None:
        operands.append(total)
    in_vmem = pl.BlockSpec(memory_space=pltpu.VMEM)
    specs = [in_vmem] * len(operands)
    out_shape = [jax.ShapeDtypeStruct((part, width), jnp.float32)] * split
    if coded:
        out_shape[1] = jax.ShapeDtypeStruct((part, width + LANES), jnp.int16)
    scratch = []
    if direct:
        for place in range(count + 1, count + 1 + len(segments)):
            specs[place] = pl.BlockSpec(memory_space=pltpu.HBM)
        scratch = [pltpu.VMEM((depth, tile[3]), jnp.bfloat16) for tile in tiles]
        scratch.append(pltpu.SemaphoreType.DMA((len(tiles),)))
    return pl.pallas_call(
        body,
        in_specs=specs,
        out_specs=[in_vmem] * split,
        scratch_shapes=scratch,
        out_shape=out_shape,
        compiler_params=pltpu.CompilerParams(vmem_limit_bytes=(DIRECT_ROOM if direct else ROOM) * MIB),
        cost_estimate=pl.CostEstimate(
            flops=2 * rows * len(groups) * depth * (width + rows),
            bytes_accessed=2 * len(groups) * depth * width + 4 * rows * width,
            transcendentals=0,
        ),
    )(*operands)


def stand_in(array):
    def body(array_ref, copy_ref):
        copy_ref[...] = array_ref[...]

    in_vmem = pl.BlockSpec(memory_space=pltpu.VMEM)
    return pl.pallas_call(
        body,
        in_specs=[in_vmem],
        out_specs=in_vmem,
        out_shape=jax.ShapeDtypeStruct(array.shape, array.dtype),
        compiler_params=pltpu.CompilerParams(vmem_limit_bytes=MIB),
        cost_estimate=pl.CostEstimate(
            flops=int(1.1e9 * STAND_IN), bytes_accessed=4096, transcendentals=0
        ),
    )(array)


def fold(kept, arrived, blocks):
    rows = kept.shape[0] // blocks
    width = kept.shape[1]

    def body(kept_ref, arrived_ref, own_ref, *code_refs):
        tiles = [jnp.zeros((rows, LANES), jnp.float32)] * (blocks - 1)
        for place in range(width // LANES):
            columns = slice(place * LANES, (place + 1) * LANES)
            sums = kept_ref[:, columns] + read_codes(arrived_ref, place)
            own_ref[:, columns] = sums[:rows]
            for index, code_ref in enumerate(code_refs):
                values = sums[(index + 1) * rows : (index + 2) * rows]
                tiles[index] = write_codes(code_ref, place, values, tiles[index])
        for tile, code_ref in zip(tiles, code_refs):
            code_ref[:, width:] = tile.astype(jnp.int32).astype(jnp.int16)

    codes = jax.ShapeDtypeStruct((rows, width + LANES), jnp.int16)
    return pl.pallas_call(
        body,
        out_shape=[jax.ShapeDtypeStruct((rows, width), jnp.float32)] + [codes] * (blocks - 1),
        compiler_params=pltpu.CompilerParams(vmem_limit_bytes=8 * MIB),
    )(kept, arrived)


def add_codes(own, arrived):
    def body(own_ref, *refs):
        for place in range(own.shape[1] // LANES):
            columns = slice(place * LANES, (place + 1) * LANES)
            sums = own_ref[:, columns]
            for code_ref in refs[:-1]:
                sums = sums + read_codes(code_ref, place)
            refs[-1][:, columns] = sums.astype(jnp.bfloat16)

    return pl.pallas_call(
        body,
        out_shape=jax.ShapeDtypeStruct(own.shape, jnp.bfloat16),
        compiler_params=pltpu.CompilerParams(vmem_limit_bytes=8 * MIB),
    )(own, *arrived)


def coded_scatter(kept, arrived):
    blocks = lax.axis_size("wide") // 2
    own, *codes = fold(kept, arrived, blocks)
    offsets = offsets_of("wide")[1:blocks]
    return add_codes(own, [swap(code, "wide", o) for code, o in zip(codes, offsets)])


def wide_scatter(kept, sent):
    rows = 2 * kept.shape[0] // lax.axis_size("wide")
    kept = kept + swap(sent.astype(jnp.float16), "wide", 1).astype(jnp.float32)
    total = kept[:rows]
    for place, offset in enumerate(offsets_of("wide")[: kept.shape[0] // rows]):
        if offset:
            block = kept[place * rows : (place + 1) * rows].astype(jnp.float16)
            total = total + swap(block, "wide", offset).astype(jnp.float32)
    return total


def narrow_scatter(kept, sent):
    for stride, kind in zip(strides_of("narrow"), NARROW_KINDS):
        if stride > 1:
            half = kept.shape[0] // 2
            kept, sent = kept[:half], kept[half:]
        kept = kept + swap(sent.astype(kind), "narrow", stride).astype(jnp.float32)
    return kept


def gather(block, axis, paired=False):
    strides = strides_of(axis)[::-1]
    for stride in strides[:-1]:
        held = stand_in(block) if paired else block
        block = jnp.concatenate([held, swap(block, axis, stride)], axis=0)
    return [block, swap(block, axis, strides[-1])]


def gather_direct(block, axis):
    offsets = offsets_of(axis)
    held = [block] + [swap(block, axis, o) for o in offsets[1 : len(offsets) // 2]]
    return [stand_in(block)] + held[1:] + [swap(piece, axis, 1) for piece in held]


def exchange(blocks, axis):
    blocks = list(blocks)
    for stride in strides_of(axis)[::-1]:
        marked = [i for i in range(len(blocks)) if i & stride]
        arrived = swap(jnp.stack([blocks[i] for i in marked]), axis, stride)
        for place, i in enumerate(marked):
            blocks[i] = arrived[place]
    return blocks


def by_rank(blocks, flags):
    for bit, flag in enumerate(flags):
        other = 1 << bit
        blocks = [jnp.where(flag, blocks[i ^ other], block) for i, block in enumerate(blocks)]
    return blocks


def shards(
    hidden_in,
    attn_gain,
    w_query,
    w_key,
    w_value,
    w_out,
    ffn_gain,
    w_gate,
    w_up,
    w_down,
    key_cache,
    value_cache,
    cache_len,
    bank_row,
):
    wide_count = lax.axis_size("wide")
    narrow_count = lax.axis_size("narrow")
    me_wide = lax.axis_index("wide")
    me_narrow = lax.axis_index("narrow")
    flags = [(me_narrow & stride) != 0 for stride in strides_of("narrow")]
    hidden_in, me_wide, me_narrow, flags = lax.optimization_barrier(
        (hidden_in, me_wide, me_narrow, flags)
    )
    model_width = hidden_in.shape[1] * wide_count
    own_rows = hidden_in.shape[0]
    local_rows = cache_len.shape[0]
    all_rows = bank_row.shape[0]
    wide_rows = all_rows // wide_count

    def device(block, axis, me):
        bits = len(strides_of(axis))
        for bit in range(bits):
            me = me ^ (((block >> bit) & 1) << (bits - 1 - bit))
        return me

    def hypothesis(place):
        return device(place // own_rows, "narrow", me_narrow) * own_rows + place % own_rows

    def wide_row(place):
        return device(place // wide_rows, "wide", me_wide) * wide_rows + place % wide_rows

    def bank(place):
        inner = place % wide_rows
        owner = device(place // wide_rows, "wide", me_wide) * narrow_count
        owner = owner + (me_narrow ^ (inner // local_rows))
        return owner * local_rows + inner % local_rows

    down = lax.broadcasted_iota(jnp.int32, (all_rows, all_rows), 0)
    across = lax.broadcasted_iota(jnp.int32, (all_rows, all_rows), 1)
    banks = jnp.broadcast_to(bank_row[None, :], (all_rows, all_rows))
    hypothesis_bank = jnp.sum(
        jnp.where(hypothesis(down) == across, banks, 0), axis=1, keepdims=True
    )
    to_hypothesis = (hypothesis_bank == bank(across)).astype(jnp.bfloat16)
    to_wide = (wide_row(down) == across).astype(jnp.bfloat16)

    def normalized_rows(values, gain_row):
        wide_values = values.astype(jnp.float32)
        rows_sq = jnp.sum(wide_values * wide_values, axis=1)
        sent = jnp.broadcast_to(rows_sq[None, :], (wide_count * narrow_count, own_rows))
        landed = lax.all_to_all(sent, ("wide", "narrow"), 0, 0, tiled=True)
        pieces = gather(values, "narrow")
        sums = jnp.sum(landed.reshape(wide_count, narrow_count, own_rows), axis=0)
        sums = by_rank([sums[j] for j in range(narrow_count)], flags)
        order = offsets_of("narrow")
        half = narrow_count // 2
        result = []
        for piece, offsets in zip(pieces, (order[:half], order[half:])):
            sum_sq = jnp.concatenate([sums[offset] for offset in offsets])
            result.append(normalize(piece, gain_row, sum_sq, model_width))
        return result

    rows_in = hidden_in.astype(jnp.float32)
    normed = normalized_rows(hidden_in, attn_gain)

    q_cols = w_query.shape[1]
    k_cols = w_key.shape[1]
    stacked = [(w_query, q_cols), (w_key, k_cols), (w_value, k_cols)]
    heads = (q_cols + 2 * k_cols) // HEAD_DIM
    edges = [heads * chunk // QKV_CHUNKS for chunk in range(QKV_CHUNKS)] + [heads]
    pieces = []
    arrivals = []
    ordered = to_hypothesis
    for chunk in range(QKV_CHUNKS):
        first, last = edges[chunk] * HEAD_DIM, edges[chunk + 1] * HEAD_DIM
        segments = []
        start = 0
        for weight, columns in stacked:
            low, high = max(first, start), min(last, start + columns)
            if low < high:
                segments.append((weight, 0, low - start, high - low))
            start += columns
        if chunk >= 2:
            ordered, arrivals[chunk - 2] = lax.optimization_barrier((ordered, arrivals[chunk - 2]))
        (kept, sent), ordered = lax.optimization_barrier(
            (project([normed], ordered, True, segments, 2, direct=True, coded=True), ordered)
        )
        pieces.append(kept)
        arrivals.append(swap(sent, "wide", 1))
    pieces = [coded_scatter(kept, arrived) for kept, arrived in zip(pieces, arrivals)]
    summed = jnp.concatenate(pieces, axis=1)
    summed = summed.reshape(narrow_count, local_rows, -1, HEAD_DIM)
    turned = jnp.stack(exchange([summed[j] for j in range(narrow_count)], "narrow"))
    q_heads = q_cols // HEAD_DIM
    context = attend(
        turned[:, :, :q_heads],
        turned[:, :, q_heads:].astype(jnp.float32),
        key_cache,
        value_cache,
        cache_len,
        me_narrow,
    )
    context = context.reshape(narrow_count, local_rows, -1)
    by_heads = exchange([context[j] for j in range(narrow_count)], "narrow")

    depth = w_out.shape[0] // CONTEXT_CHUNKS
    groups = []
    for chunk in range(CONTEXT_CHUNKS):
        columns = slice(chunk * depth, (chunk + 1) * depth)
        block = jnp.concatenate([piece[:, columns] for piece in by_heads], axis=0)
        groups.append(gather_direct(block, "wide"))
    total = project(groups, to_hypothesis, False, [(w_out, 0, 0, w_out.shape[1])], 2)
    attn_out = narrow_scatter(*total)
    resid = (rows_in + attn_out).astype(jnp.bfloat16)
    resid_wide = resid.astype(jnp.float32)
    normed_two = normalized_rows(resid, ffn_gain)

    f_total = w_gate.shape[1]
    f_edge = int(f_total * FFN_SPLIT) // LANES * LANES
    total = None
    for first, last in ((0, f_edge), (f_edge, f_total)):
        f_cols = last - first
        segments = [(w_gate, 0, first, f_cols), (w_up, 0, first, f_cols)]
        sums = wide_scatter(*project([normed_two], to_wide, False, segments, 2, direct=True))
        act = (jax.nn.silu(sums[:, :f_cols]) * sums[:, f_cols:]).astype(jnp.bfloat16)
        total = project(
            [gather(act, "wide", paired=True)],
            to_wide,
            True,
            [(w_down, first, 0, w_down.shape[1])],
            2 if last == f_total else 1,
            total if total is None else total[0],
        )
    ffn_out = narrow_scatter(*total)
    return (resid_wide + ffn_out).astype(jnp.bfloat16)


def solution(mesh):
    return jax.shard_map(
        shards,
        mesh=mesh,
        in_specs=(
            P("narrow", "wide"),
            P("wide"),
            P("wide", "narrow"),
            P("wide", "narrow"),
            P("wide", "narrow"),
            P("narrow", "wide"),
            P("wide"),
            P("wide", "narrow"),
            P("wide", "narrow"),
            P("narrow", "wide"),
            P(("wide", "narrow"), None, None),
            P(("wide", "narrow"), None, None),
            P(("wide", "narrow")),
            P(),
        ),
        out_specs=P("narrow", "wide"),
        check_vma=False,
    )
```

```python
import math

import jax
import jax.numpy as jnp
from jax import lax
from jax.experimental import pallas as pl
from jax.experimental.pallas import tpu as pltpu
from jax.sharding import PartitionSpec as P

HEAD_DIM = 128


NORM_EPSILON = 1e-05
ROPE_BASE = 500000.0


def product(left, right):
    return jnp.dot(left, right, preferred_element_type=jnp.float32)


def normalize(values_in, gain_row, sum_sq, model_width):
    mean_sq = sum_sq / model_width
    scaled = values_in.astype(jnp.float32) * lax.rsqrt(mean_sq + NORM_EPSILON)[:, None]
    return (scaled * gain_row[None, :]).astype(jnp.bfloat16)


def rotate(head_rows, lengths):
    head_size = head_rows.shape[-1]
    half_size = head_size // 2
    inverse_freq = jnp.exp(
        jnp.arange(half_size, dtype=jnp.float32) * (-2.0 * math.log(ROPE_BASE) / head_size)
    )
    angles = lengths.astype(jnp.float32)[:, None] * inverse_freq[None, :]
    cos_part = jnp.cos(angles)[:, None, :]
    sin_part = jnp.sin(angles)[:, None, :]
    front_half = head_rows[..., :half_size].astype(jnp.float32)
    back_half = head_rows[..., half_size:].astype(jnp.float32)
    turned = jnp.concatenate(
        [
            front_half * cos_part - back_half * sin_part,
            back_half * cos_part + front_half * sin_part,
        ],
        axis=-1,
    )
    return turned.astype(jnp.bfloat16)


def attend(queries, fresh_key, fresh_value, key_cache, value_cache, lengths):
    row_count, length, kv_width = key_cache.shape
    groups = kv_width // HEAD_DIM
    group_size = queries.shape[1] // kv_width
    score_scale = 1.0 / math.sqrt(HEAD_DIM)
    query_heads = queries.reshape(row_count, groups, group_size, HEAD_DIM)
    cache_keys = key_cache.reshape(row_count, length, groups, HEAD_DIM)
    cache_values = value_cache.reshape(row_count, length, groups, HEAD_DIM)
    own_key = fresh_key.reshape(row_count, groups, HEAD_DIM)
    own_value = fresh_value.reshape(row_count, groups, HEAD_DIM)
    scores = (
        jnp.einsum("rgqd,rlgd->rgql", query_heads, cache_keys, preferred_element_type=jnp.float32)
        * score_scale
    )
    own_score = (
        jnp.einsum("rgqd,rgd->rgq", query_heads, own_key, preferred_element_type=jnp.float32)
        * score_scale
    )
    valid_pos = jnp.arange(length, dtype=jnp.int32)[None, :] < lengths[:, None]
    scores = jnp.where(valid_pos[:, None, None, :], scores, -jnp.inf)
    row_max = jnp.maximum(jnp.max(scores, axis=3), own_score)
    weights = jnp.exp(scores - row_max[..., None])
    own_weight = jnp.exp(own_score - row_max)
    weight_sum = jnp.sum(weights, axis=3) + own_weight
    probs = (weights / weight_sum[..., None]).astype(jnp.bfloat16)
    own_prob = (own_weight / weight_sum).astype(jnp.bfloat16)
    context = jnp.einsum("rgql,rlgd->rgqd", probs, cache_values, preferred_element_type=jnp.float32)
    context = (
        context
        + own_prob.astype(jnp.float32)[..., None] * own_value.astype(jnp.float32)[:, :, None, :]
    )
    return context.reshape(row_count, groups * group_size * HEAD_DIM).astype(jnp.bfloat16)


QKV_CHUNKS = 3
FFN_SPLIT = 0.5
CONTEXT_CHUNKS = 2
NARROW_KINDS = [jnp.float32] + [jnp.bfloat16] * 8
TILE = 512
ROOM = 24
DIRECT_ROOM = 50
IN_FLIGHT = 9
LANES = 128
TOP_CODE = 32700.0
LOG_STEPS = 64.0
STAND_IN = 4
MIB = 1024 * 1024


def swap(block, axis, offset):
    count = lax.axis_size(axis)
    return lax.ppermute(block, axis, [(i, i ^ offset) for i in range(count)])


def strides_of(axis):
    count = lax.axis_size(axis)
    return [1 << bit for bit in range(count.bit_length() - 1)]


def offsets_of(axis):
    order = [0]
    for stride in reversed(strides_of(axis)):
        order = order + [offset ^ stride for offset in order]
    return order


def encoded(values):
    top = jnp.max(jnp.abs(values), axis=1, keepdims=True)
    steps = jnp.floor(jnp.log2(jnp.maximum(top, 1e-30)) * LOG_STEPS + 1.5)
    return jnp.round(values * (TOP_CODE * jnp.exp2(steps * (-1.0 / LOG_STEPS)))), steps


def write_codes(code_ref, place, values, steps_tile):
    codes, steps = encoded(values)
    code_ref[:, place * LANES : (place + 1) * LANES] = codes.astype(jnp.int32).astype(jnp.int16)
    lanes = lax.broadcasted_iota(jnp.int32, (values.shape[0], LANES), 1)
    return jnp.where(lanes == place, steps, steps_tile)


def read_codes(code_ref, place):
    codes = code_ref[:, place * LANES : (place + 1) * LANES]
    steps = code_ref[:, code_ref.shape[1] - LANES :].astype(jnp.int32).astype(jnp.float32)
    scale = jnp.exp2(steps[:, place : place + 1] * (1.0 / LOG_STEPS)) * (1.0 / TOP_CODE)
    return codes.astype(jnp.int32).astype(jnp.float32) * scale


def project(
    groups, order, turned, segments, split, total=None, direct=False, coded=False
):
    rows = order.shape[0]
    depth = groups[0][0].shape[1]
    tiles = []
    width = 0
    for index, (_, first_row, first, columns) in enumerate(segments):
        for start in range(first, first + columns, TILE):
            tile = min(TILE, first + columns - start)
            tiles.append((index, first_row, start, tile, width))
            width += tile
    part = rows // split
    pieces = [piece for group in groups for piece in group]
    count = len(pieces)
    each = count // len(groups)

    def body(*refs):
        piece_refs, order_ref, rest = refs[:count], refs[count], refs[count + 1 :]
        weight_refs, rest = rest[: len(segments)], rest[len(segments) :]
        if total is not None:
            total_ref, rest = rest[0], rest[1:]
        out_refs, rest = rest[:split], rest[split:]
        copies = []
        if direct:
            for place, (index, first_row, start, tile, _) in enumerate(tiles):
                source = weight_refs[index].at[pl.ds(first_row, depth), pl.ds(start, tile)]
                copies.append(pltpu.make_async_copy(source, rest[place], rest[-1].at[place]))
        for copy in copies[:IN_FLIGHT]:
            copy.start()
        lefts = []
        for group in range(len(groups)):
            group_refs = piece_refs[group * each : (group + 1) * each]
            left = lax.dot_general(
                order_ref[...],
                jnp.concatenate([ref[...] for ref in group_refs], axis=0),
                (((0 if turned else 1,), (0,)), ((), ())),
                preferred_element_type=jnp.float32,
            )
            lefts.append(left.astype(jnp.bfloat16))
        steps_tile = jnp.zeros((part, LANES), jnp.float32)
        for number, (index, first_row, start, tile, base) in enumerate(tiles):
            result = None
            for group, left in enumerate(lefts):
                if direct:
                    copies[number].wait()
                    weight = rest[number][...]
                    if number + IN_FLIGHT < len(tiles):
                        copies[number + IN_FLIGHT].start()
                else:
                    weight = weight_refs[index][
                        pl.ds(first_row + group * depth, depth), pl.ds(start, tile)
                    ]
                product = jnp.dot(left, weight, preferred_element_type=jnp.float32)
                result = product if result is None else result + product
            if total is not None:
                result = result + total_ref[:, base : base + tile]
            for place, out_ref in enumerate(out_refs[: 1 if coded else split]):
                out_ref[:, base : base + tile] = result[place * part : (place + 1) * part]
            if coded:
                for column in range(0, tile, LANES):
                    values = result[part:, column : column + LANES]
                    place = (base + column) // LANES
                    steps_tile = write_codes(out_refs[1], place, values, steps_tile)
        if coded:
            out_refs[1][:, width:] = steps_tile.astype(jnp.int32).astype(jnp.int16)

    operands = pieces + [order] + [segment[0] for segment in segments]
    if total is not None:
        operands.append(total)
    in_vmem = pl.BlockSpec(memory_space=pltpu.VMEM)
    specs = [in_vmem] * len(operands)
    out_shape = [jax.ShapeDtypeStruct((part, width), jnp.float32)] * split
    if coded:
        out_shape[1] = jax.ShapeDtypeStruct((part, width + LANES), jnp.int16)
    scratch = []
    if direct:
        for place in range(count + 1, count + 1 + len(segments)):
            specs[place] = pl.BlockSpec(memory_space=pltpu.HBM)
        scratch = [pltpu.VMEM((depth, tile[3]), jnp.bfloat16) for tile in tiles]
        scratch.append(pltpu.SemaphoreType.DMA((len(tiles),)))
    return pl.pallas_call(
        body,
        in_specs=specs,
        out_specs=[in_vmem] * split,
        scratch_shapes=scratch,
        out_shape=out_shape,
        compiler_params=pltpu.CompilerParams(vmem_limit_bytes=(DIRECT_ROOM if direct else ROOM) * MIB),
        cost_estimate=pl.CostEstimate(
            flops=2 * rows * len(groups) * depth * (width + rows),
            bytes_accessed=2 * len(groups) * depth * width + 4 * rows * width,
            transcendentals=0,
        ),
    )(*operands)


def stand_in(array):
    def body(array_ref, copy_ref):
        copy_ref[...] = array_ref[...]

    in_vmem = pl.BlockSpec(memory_space=pltpu.VMEM)
    return pl.pallas_call(
        body,
        in_specs=[in_vmem],
        out_specs=in_vmem,
        out_shape=jax.ShapeDtypeStruct(array.shape, array.dtype),
        compiler_params=pltpu.CompilerParams(vmem_limit_bytes=MIB),
        cost_estimate=pl.CostEstimate(
            flops=int(1.1e9 * STAND_IN), bytes_accessed=4096, transcendentals=0
        ),
    )(array)


def fold(kept, arrived, blocks):
    rows = kept.shape[0] // blocks
    width = kept.shape[1]

    def body(kept_ref, arrived_ref, own_ref, *code_refs):
        tiles = [jnp.zeros((rows, LANES), jnp.float32)] * (blocks - 1)
        for place in range(width // LANES):
            columns = slice(place * LANES, (place + 1) * LANES)
            sums = kept_ref[:, columns] + read_codes(arrived_ref, place)
            own_ref[:, columns] = sums[:rows]
            for index, code_ref in enumerate(code_refs):
                values = sums[(index + 1) * rows : (index + 2) * rows]
                tiles[index] = write_codes(code_ref, place, values, tiles[index])
        for tile, code_ref in zip(tiles, code_refs):
            code_ref[:, width:] = tile.astype(jnp.int32).astype(jnp.int16)

    codes = jax.ShapeDtypeStruct((rows, width + LANES), jnp.int16)
    return pl.pallas_call(
        body,
        out_shape=[jax.ShapeDtypeStruct((rows, width), jnp.float32)] + [codes] * (blocks - 1),
        compiler_params=pltpu.CompilerParams(vmem_limit_bytes=8 * MIB),
    )(kept, arrived)


def add_codes(own, arrived):
    def body(own_ref, *refs):
        for place in range(own.shape[1] // LANES):
            columns = slice(place * LANES, (place + 1) * LANES)
            sums = own_ref[:, columns]
            for code_ref in refs[:-1]:
                sums = sums + read_codes(code_ref, place)
            refs[-1][:, columns] = sums.astype(jnp.bfloat16)

    return pl.pallas_call(
        body,
        out_shape=jax.ShapeDtypeStruct(own.shape, jnp.bfloat16),
        compiler_params=pltpu.CompilerParams(vmem_limit_bytes=8 * MIB),
    )(own, *arrived)


def coded_scatter(kept, arrived):
    for stride in strides_of("wide")[1:]:
        kept, codes = fold(kept, arrived, 2)
        arrived = swap(codes, "wide", stride)
    return add_codes(kept, [arrived])


def wide_scatter(kept, sent):
    rows = 2 * kept.shape[0] // lax.axis_size("wide")
    kept = kept + swap(sent.astype(jnp.float16), "wide", 1).astype(jnp.float32)
    total = kept[:rows]
    for place, offset in enumerate(offsets_of("wide")[: kept.shape[0] // rows]):
        if offset:
            block = kept[place * rows : (place + 1) * rows].astype(jnp.float16)
            total = total + swap(block, "wide", offset).astype(jnp.float32)
    return total


def narrow_scatter(kept, sent):
    for stride, kind in zip(strides_of("narrow"), NARROW_KINDS):
        if stride > 1:
            half = kept.shape[0] // 2
            kept, sent = kept[:half], kept[half:]
        kept = kept + swap(sent.astype(kind), "narrow", stride).astype(jnp.float32)
    return kept


def gather(block, axis, paired=False):
    strides = strides_of(axis)[::-1]
    for stride in strides[:-1]:
        held = stand_in(block) if paired else block
        block = jnp.concatenate([held, swap(block, axis, stride)], axis=0)
    return [block, swap(block, axis, strides[-1])]


def gather_pieces(block, axis):
    held = [block]
    for stride in strides_of(axis)[::-1]:
        held = held + [swap(piece, axis, stride) for piece in held]
    return [stand_in(block)] + held[1:]


def exchange(blocks, axis):
    blocks = list(blocks)
    for stride in strides_of(axis)[::-1]:
        marked = [i for i in range(len(blocks)) if i & stride]
        arrived = swap(jnp.stack([blocks[i] for i in marked]), axis, stride)
        for place, i in enumerate(marked):
            blocks[i] = arrived[place]
    return blocks


def by_rank(blocks, flags):
    for bit, flag in enumerate(flags):
        other = 1 << bit
        blocks = [jnp.where(flag, blocks[i ^ other], block) for i, block in enumerate(blocks)]
    return blocks


def shards(
    hidden_in,
    attn_gain,
    w_query,
    w_key,
    w_value,
    w_out,
    ffn_gain,
    w_gate,
    w_up,
    w_down,
    key_cache,
    value_cache,
    cache_len,
    bank_row,
):
    wide_count = lax.axis_size("wide")
    narrow_count = lax.axis_size("narrow")
    me_wide = lax.axis_index("wide")
    me_narrow = lax.axis_index("narrow")
    flags = [(me_narrow & stride) != 0 for stride in strides_of("narrow")]
    hidden_in, me_wide, me_narrow, flags = lax.optimization_barrier(
        (hidden_in, me_wide, me_narrow, flags)
    )
    model_width = hidden_in.shape[1] * wide_count
    own_rows = hidden_in.shape[0]
    local_rows = cache_len.shape[0]
    all_rows = bank_row.shape[0]
    wide_rows = all_rows // wide_count

    def device(block, axis, me):
        bits = len(strides_of(axis))
        for bit in range(bits):
            me = me ^ (((block >> bit) & 1) << (bits - 1 - bit))
        return me

    def hypothesis(place):
        return device(place // own_rows, "narrow", me_narrow) * own_rows + place % own_rows

    def wide_row(place):
        return device(place // wide_rows, "wide", me_wide) * wide_rows + place % wide_rows

    def bank(place):
        inner = place % wide_rows
        owner = device(place // wide_rows, "wide", me_wide) * narrow_count
        owner = owner + (me_narrow ^ (inner // local_rows))
        return owner * local_rows + inner % local_rows

    down = lax.broadcasted_iota(jnp.int32, (all_rows, all_rows), 0)
    across = lax.broadcasted_iota(jnp.int32, (all_rows, all_rows), 1)
    banks = jnp.broadcast_to(bank_row[None, :], (all_rows, all_rows))
    hypothesis_bank = jnp.sum(
        jnp.where(hypothesis(down) == across, banks, 0), axis=1, keepdims=True
    )
    to_hypothesis = (hypothesis_bank == bank(across)).astype(jnp.bfloat16)
    to_wide = (wide_row(down) == across).astype(jnp.bfloat16)

    def normalized_rows(values, gain_row):
        wide_values = values.astype(jnp.float32)
        rows_sq = jnp.sum(wide_values * wide_values, axis=1)
        sent = jnp.broadcast_to(rows_sq[None, :], (wide_count * narrow_count, own_rows))
        landed = lax.all_to_all(sent, ("wide", "narrow"), 0, 0, tiled=True)
        pieces = gather(values, "narrow")
        sums = jnp.sum(landed.reshape(wide_count, narrow_count, own_rows), axis=0)
        sums = by_rank([sums[j] for j in range(narrow_count)], flags)
        order = offsets_of("narrow")
        half = narrow_count // 2
        result = []
        for piece, offsets in zip(pieces, (order[:half], order[half:])):
            sum_sq = jnp.concatenate([sums[offset] for offset in offsets])
            result.append(normalize(piece, gain_row, sum_sq, model_width))
        return result

    rows_in = hidden_in.astype(jnp.float32)
    normed = normalized_rows(hidden_in, attn_gain)

    q_cols = w_query.shape[1]
    k_cols = w_key.shape[1]
    stacked = [(w_query, q_cols), (w_key, k_cols), (w_value, k_cols)]
    heads = (q_cols + 2 * k_cols) // HEAD_DIM
    edges = [heads * chunk // QKV_CHUNKS for chunk in range(QKV_CHUNKS)] + [heads]
    pieces = []
    arrivals = []
    ordered = to_hypothesis
    for chunk in range(QKV_CHUNKS):
        first, last = edges[chunk] * HEAD_DIM, edges[chunk + 1] * HEAD_DIM
        segments = []
        start = 0
        for weight, columns in stacked:
            low, high = max(first, start), min(last, start + columns)
            if low < high:
                segments.append((weight, 0, low - start, high - low))
            start += columns
        if chunk >= 2:
            ordered, arrivals[chunk - 2] = lax.optimization_barrier((ordered, arrivals[chunk - 2]))
        (kept, sent), ordered = lax.optimization_barrier(
            (project([normed], ordered, True, segments, 2, direct=True, coded=True), ordered)
        )
        pieces.append(kept)
        arrivals.append(swap(sent, "wide", 1))
    pieces = [coded_scatter(kept, arrived) for kept, arrived in zip(pieces, arrivals)]
    summed = jnp.concatenate(pieces, axis=1)
    summed = summed.reshape(narrow_count, local_rows, -1, HEAD_DIM)
    turned = exchange([summed[j] for j in range(narrow_count)], "narrow")
    turned = jnp.stack(by_rank(turned, flags), axis=1)
    q_heads = q_cols // HEAD_DIM
    k_heads = k_cols // HEAD_DIM
    query_rot = rotate(
        turned[:, :, :q_heads].reshape(local_rows, -1, HEAD_DIM), cache_len
    ).reshape(local_rows, -1)
    key_rot = rotate(
        turned[:, :, q_heads : q_heads + k_heads].reshape(local_rows, -1, HEAD_DIM), cache_len
    ).reshape(local_rows, -1)
    value_new = turned[:, :, q_heads + k_heads :].reshape(local_rows, -1)
    context = attend(query_rot, key_rot, value_new, key_cache, value_cache, cache_len)
    context = context.reshape(local_rows, narrow_count, -1)
    context = by_rank([context[:, j] for j in range(narrow_count)], flags)
    by_heads = exchange(context, "narrow")

    depth = w_out.shape[0] // CONTEXT_CHUNKS
    groups = []
    for chunk in range(CONTEXT_CHUNKS):
        columns = slice(chunk * depth, (chunk + 1) * depth)
        block = jnp.concatenate([piece[:, columns] for piece in by_heads], axis=0)
        groups.append(gather_pieces(block, "wide"))
    total = project(groups, to_hypothesis, False, [(w_out, 0, 0, w_out.shape[1])], 2)
    attn_out = narrow_scatter(*total)
    resid = (rows_in + attn_out).astype(jnp.bfloat16)
    resid_wide = resid.astype(jnp.float32)
    normed_two = normalized_rows(resid, ffn_gain)

    f_total = w_gate.shape[1]
    f_edge = int(f_total * FFN_SPLIT) // LANES * LANES
    total = None
    for first, last in ((0, f_edge), (f_edge, f_total)):
        f_cols = last - first
        segments = [(w_gate, 0, first, f_cols), (w_up, 0, first, f_cols)]
        sums = wide_scatter(*project([normed_two], to_wide, False, segments, 2, direct=True))
        act = (jax.nn.silu(sums[:, :f_cols]) * sums[:, f_cols:]).astype(jnp.bfloat16)
        total = project(
            [gather(act, "wide", paired=True)],
            to_wide,
            True,
            [(w_down, first, 0, w_down.shape[1])],
            2 if last == f_total else 1,
            total if total is None else total[0],
        )
    ffn_out = narrow_scatter(*total)
    return (resid_wide + ffn_out).astype(jnp.bfloat16)


def solution(mesh):
    return jax.shard_map(
        shards,
        mesh=mesh,
        in_specs=(
            P("narrow", "wide"),
            P("wide"),
            P("wide", "narrow"),
            P("wide", "narrow"),
            P("wide", "narrow"),
            P("narrow", "wide"),
            P("wide"),
            P("wide", "narrow"),
            P("wide", "narrow"),
            P("narrow", "wide"),
            P(("wide", "narrow"), None, None),
            P(("wide", "narrow"), None, None),
            P(("wide", "narrow")),
            P(),
        ),
        out_specs=P("narrow", "wide"),
        check_vma=False,
    )
```

```python
import math

import jax
import jax.numpy as jnp
from jax import lax
from jax.experimental import pallas as pl
from jax.experimental.pallas import tpu as pltpu
from jax.sharding import PartitionSpec as P

HEAD_DIM = 128


NORM_EPSILON = 1e-05
ROPE_BASE = 500000.0


def product(left, right):
    return jnp.dot(left, right, preferred_element_type=jnp.float32)


def normalize(values_in, gain_row, sum_sq, model_width):
    mean_sq = sum_sq / model_width
    scaled = values_in.astype(jnp.float32) * lax.rsqrt(mean_sq + NORM_EPSILON)[:, None]
    return (scaled * gain_row[None, :]).astype(jnp.bfloat16)


def rotate(head_rows, lengths):
    head_size = head_rows.shape[-1]
    half_size = head_size // 2
    inverse_freq = jnp.exp(
        jnp.arange(half_size, dtype=jnp.float32) * (-2.0 * math.log(ROPE_BASE) / head_size)
    )
    angles = lengths.astype(jnp.float32)[:, None] * inverse_freq[None, :]
    cos_part = jnp.cos(angles)[:, None, :]
    sin_part = jnp.sin(angles)[:, None, :]
    front_half = head_rows[..., :half_size].astype(jnp.float32)
    back_half = head_rows[..., half_size:].astype(jnp.float32)
    turned = jnp.concatenate(
        [
            front_half * cos_part - back_half * sin_part,
            back_half * cos_part + front_half * sin_part,
        ],
        axis=-1,
    )
    return turned.astype(jnp.bfloat16)


def attend(queries, fresh_key, fresh_value, key_cache, value_cache, lengths):
    row_count, length, kv_width = key_cache.shape
    groups = kv_width // HEAD_DIM
    group_size = queries.shape[1] // kv_width
    score_scale = 1.0 / math.sqrt(HEAD_DIM)
    query_heads = queries.reshape(row_count, groups, group_size, HEAD_DIM)
    cache_keys = key_cache.reshape(row_count, length, groups, HEAD_DIM)
    cache_values = value_cache.reshape(row_count, length, groups, HEAD_DIM)
    own_key = fresh_key.reshape(row_count, groups, HEAD_DIM)
    own_value = fresh_value.reshape(row_count, groups, HEAD_DIM)
    scores = (
        jnp.einsum("rgqd,rlgd->rgql", query_heads, cache_keys, preferred_element_type=jnp.float32)
        * score_scale
    )
    own_score = (
        jnp.einsum("rgqd,rgd->rgq", query_heads, own_key, preferred_element_type=jnp.float32)
        * score_scale
    )
    valid_pos = jnp.arange(length, dtype=jnp.int32)[None, :] < lengths[:, None]
    scores = jnp.where(valid_pos[:, None, None, :], scores, -jnp.inf)
    row_max = jnp.maximum(jnp.max(scores, axis=3), own_score)
    weights = jnp.exp(scores - row_max[..., None])
    own_weight = jnp.exp(own_score - row_max)
    weight_sum = jnp.sum(weights, axis=3) + own_weight
    probs = (weights / weight_sum[..., None]).astype(jnp.bfloat16)
    own_prob = (own_weight / weight_sum).astype(jnp.bfloat16)
    context = jnp.einsum("rgql,rlgd->rgqd", probs, cache_values, preferred_element_type=jnp.float32)
    context = (
        context
        + own_prob.astype(jnp.float32)[..., None] * own_value.astype(jnp.float32)[:, :, None, :]
    )
    return context.reshape(row_count, groups * group_size * HEAD_DIM).astype(jnp.bfloat16)


QKV_CHUNKS = 3
FFN_EDGES = (0, 4, 10, 16)
CONTEXT_CHUNKS = 1
NARROW_KINDS = [jnp.float32] + [jnp.bfloat16] * 8
TILE = 512
ROOM = 24
DIRECT_ROOM = 50
IN_FLIGHT = 9
LANES = 128
TOP_CODE = 32700.0
LOG_STEPS = 64.0
STAND_IN = 4
MIB = 1024 * 1024


def swap(block, axis, offset):
    count = lax.axis_size(axis)
    return lax.ppermute(block, axis, [(i, i ^ offset) for i in range(count)])


def strides_of(axis):
    count = lax.axis_size(axis)
    return [1 << bit for bit in range(count.bit_length() - 1)]


def offsets_of(axis):
    order = [0]
    for stride in reversed(strides_of(axis)):
        order = order + [offset ^ stride for offset in order]
    return order


def encoded(values):
    top = jnp.max(jnp.abs(values), axis=1, keepdims=True)
    steps = jnp.floor(jnp.log2(jnp.maximum(top, 1e-30)) * LOG_STEPS + 1.5)
    return jnp.round(values * (TOP_CODE * jnp.exp2(steps * (-1.0 / LOG_STEPS)))), steps


def write_codes(code_ref, place, values, steps_tile):
    codes, steps = encoded(values)
    code_ref[:, place * LANES : (place + 1) * LANES] = codes.astype(jnp.int32).astype(jnp.int16)
    lanes = lax.broadcasted_iota(jnp.int32, (values.shape[0], LANES), 1)
    return jnp.where(lanes == place, steps, steps_tile)


def read_codes(code_ref, place):
    codes = code_ref[:, place * LANES : (place + 1) * LANES]
    steps = code_ref[:, code_ref.shape[1] - LANES :].astype(jnp.int32).astype(jnp.float32)
    scale = jnp.exp2(steps[:, place : place + 1] * (1.0 / LOG_STEPS)) * (1.0 / TOP_CODE)
    return codes.astype(jnp.int32).astype(jnp.float32) * scale


def project(
    groups, order, turned, segments, split, total=None, direct=False, coded=False
):
    rows = order.shape[0]
    depth = groups[0][0].shape[1]
    tiles = []
    width = 0
    for index, (_, first_row, first, columns) in enumerate(segments):
        for start in range(first, first + columns, TILE):
            tile = min(TILE, first + columns - start)
            tiles.append((index, first_row, start, tile, width))
            width += tile
    part = rows // split
    pieces = [piece for group in groups for piece in group]
    count = len(pieces)
    each = count // len(groups)

    def body(*refs):
        piece_refs, order_ref, rest = refs[:count], refs[count], refs[count + 1 :]
        weight_refs, rest = rest[: len(segments)], rest[len(segments) :]
        if total is not None:
            total_ref, rest = rest[0], rest[1:]
        out_refs, rest = rest[:split], rest[split:]
        copies = []
        if direct:
            for place, (index, first_row, start, tile, _) in enumerate(tiles):
                source = weight_refs[index].at[pl.ds(first_row, depth), pl.ds(start, tile)]
                copies.append(pltpu.make_async_copy(source, rest[place], rest[-1].at[place]))
        for copy in copies[:IN_FLIGHT]:
            copy.start()
        lefts = []
        for group in range(len(groups)):
            group_refs = piece_refs[group * each : (group + 1) * each]
            left = lax.dot_general(
                order_ref[...],
                jnp.concatenate([ref[...] for ref in group_refs], axis=0),
                (((0 if turned else 1,), (0,)), ((), ())),
                preferred_element_type=jnp.float32,
            )
            lefts.append(left.astype(jnp.bfloat16))
        steps_tile = jnp.zeros((part, LANES), jnp.float32)
        for number, (index, first_row, start, tile, base) in enumerate(tiles):
            result = None
            for group, left in enumerate(lefts):
                if direct:
                    copies[number].wait()
                    weight = rest[number][...]
                    if number + IN_FLIGHT < len(tiles):
                        copies[number + IN_FLIGHT].start()
                else:
                    weight = weight_refs[index][
                        pl.ds(first_row + group * depth, depth), pl.ds(start, tile)
                    ]
                product = jnp.dot(left, weight, preferred_element_type=jnp.float32)
                result = product if result is None else result + product
            if total is not None:
                result = result + total_ref[:, base : base + tile]
            for place, out_ref in enumerate(out_refs[: 1 if coded else split]):
                out_ref[:, base : base + tile] = result[place * part : (place + 1) * part]
            if coded:
                for column in range(0, tile, LANES):
                    values = result[part:, column : column + LANES]
                    place = (base + column) // LANES
                    steps_tile = write_codes(out_refs[1], place, values, steps_tile)
        if coded:
            out_refs[1][:, width:] = steps_tile.astype(jnp.int32).astype(jnp.int16)

    operands = pieces + [order] + [segment[0] for segment in segments]
    if total is not None:
        operands.append(total)
    in_vmem = pl.BlockSpec(memory_space=pltpu.VMEM)
    specs = [in_vmem] * len(operands)
    out_shape = [jax.ShapeDtypeStruct((part, width), jnp.float32)] * split
    if coded:
        out_shape[1] = jax.ShapeDtypeStruct((part, width + LANES), jnp.int16)
    scratch = []
    if direct:
        for place in range(count + 1, count + 1 + len(segments)):
            specs[place] = pl.BlockSpec(memory_space=pltpu.HBM)
        scratch = [pltpu.VMEM((depth, tile[3]), jnp.bfloat16) for tile in tiles]
        scratch.append(pltpu.SemaphoreType.DMA((len(tiles),)))
    return pl.pallas_call(
        body,
        in_specs=specs,
        out_specs=[in_vmem] * split,
        scratch_shapes=scratch,
        out_shape=out_shape,
        compiler_params=pltpu.CompilerParams(vmem_limit_bytes=(DIRECT_ROOM if direct else ROOM) * MIB),
        cost_estimate=pl.CostEstimate(
            flops=2 * rows * len(groups) * depth * (width + rows),
            bytes_accessed=2 * len(groups) * depth * width + 4 * rows * width,
            transcendentals=0,
        ),
    )(*operands)


def stand_in(array):
    def body(array_ref, copy_ref):
        copy_ref[...] = array_ref[...]

    in_vmem = pl.BlockSpec(memory_space=pltpu.VMEM)
    return pl.pallas_call(
        body,
        in_specs=[in_vmem],
        out_specs=in_vmem,
        out_shape=jax.ShapeDtypeStruct(array.shape, array.dtype),
        compiler_params=pltpu.CompilerParams(vmem_limit_bytes=MIB),
        cost_estimate=pl.CostEstimate(
            flops=int(1.1e9 * STAND_IN), bytes_accessed=4096, transcendentals=0
        ),
    )(array)


def fold(kept, arrived, blocks):
    rows = kept.shape[0] // blocks
    width = kept.shape[1]

    def body(kept_ref, arrived_ref, own_ref, *code_refs):
        tiles = [jnp.zeros((rows, LANES), jnp.float32)] * (blocks - 1)
        for place in range(width // LANES):
            columns = slice(place * LANES, (place + 1) * LANES)
            sums = kept_ref[:, columns] + read_codes(arrived_ref, place)
            own_ref[:, columns] = sums[:rows]
            for index, code_ref in enumerate(code_refs):
                values = sums[(index + 1) * rows : (index + 2) * rows]
                tiles[index] = write_codes(code_ref, place, values, tiles[index])
        for tile, code_ref in zip(tiles, code_refs):
            code_ref[:, width:] = tile.astype(jnp.int32).astype(jnp.int16)

    codes = jax.ShapeDtypeStruct((rows, width + LANES), jnp.int16)
    return pl.pallas_call(
        body,
        out_shape=[jax.ShapeDtypeStruct((rows, width), jnp.float32)] + [codes] * (blocks - 1),
        compiler_params=pltpu.CompilerParams(vmem_limit_bytes=8 * MIB),
    )(kept, arrived)


def add_codes(own, arrived):
    def body(own_ref, *refs):
        for place in range(own.shape[1] // LANES):
            columns = slice(place * LANES, (place + 1) * LANES)
            sums = own_ref[:, columns]
            for code_ref in refs[:-1]:
                sums = sums + read_codes(code_ref, place)
            refs[-1][:, columns] = sums.astype(jnp.bfloat16)

    return pl.pallas_call(
        body,
        out_shape=jax.ShapeDtypeStruct(own.shape, jnp.bfloat16),
        compiler_params=pltpu.CompilerParams(vmem_limit_bytes=8 * MIB),
    )(own, *arrived)


def coded_scatter(kept, arrived):
    for stride in strides_of("wide")[1:]:
        kept, codes = fold(kept, arrived, 2)
        arrived = swap(codes, "wide", stride)
    return add_codes(kept, [arrived])


def wide_scatter(kept, arrived):
    rows = 2 * kept.shape[0] // lax.axis_size("wide")
    kept = kept + arrived.astype(jnp.float32)
    total = kept[:rows]
    for place, offset in enumerate(offsets_of("wide")[: kept.shape[0] // rows]):
        if offset:
            block = kept[place * rows : (place + 1) * rows].astype(jnp.float16)
            total = total + swap(block, "wide", offset).astype(jnp.float32)
    return total


def narrow_scatter(kept, sent):
    for stride, kind in zip(strides_of("narrow"), NARROW_KINDS):
        if stride > 1:
            half = kept.shape[0] // 2
            kept, sent = kept[:half], kept[half:]
        kept = kept + swap(sent.astype(kind), "narrow", stride).astype(jnp.float32)
    return kept


def gather(block, axis, paired=False):
    strides = strides_of(axis)[::-1]
    for stride in strides[:-1]:
        held = stand_in(block) if paired else block
        block = jnp.concatenate([held, swap(block, axis, stride)], axis=0)
    return [block, swap(block, axis, strides[-1])]


def gather_pieces(block, axis):
    held = [block]
    for stride in strides_of(axis)[::-1]:
        held = held + [swap(piece, axis, stride) for piece in held]
    return [stand_in(stand_in(block))] + held[1:]


def exchange(blocks, axis):
    blocks = list(blocks)
    for stride in strides_of(axis)[::-1]:
        marked = [i for i in range(len(blocks)) if i & stride]
        arrived = swap(jnp.stack([blocks[i] for i in marked]), axis, stride)
        for place, i in enumerate(marked):
            blocks[i] = arrived[place]
    return blocks


def by_rank(blocks, flags):
    for bit, flag in enumerate(flags):
        other = 1 << bit
        blocks = [jnp.where(flag, blocks[i ^ other], block) for i, block in enumerate(blocks)]
    return blocks


def shards(
    hidden_in,
    attn_gain,
    w_query,
    w_key,
    w_value,
    w_out,
    ffn_gain,
    w_gate,
    w_up,
    w_down,
    key_cache,
    value_cache,
    cache_len,
    bank_row,
):
    wide_count = lax.axis_size("wide")
    narrow_count = lax.axis_size("narrow")
    me_wide = lax.axis_index("wide")
    me_narrow = lax.axis_index("narrow")
    flags = [(me_narrow & stride) != 0 for stride in strides_of("narrow")]
    hidden_in, me_wide, me_narrow, flags = lax.optimization_barrier(
        (hidden_in, me_wide, me_narrow, flags)
    )
    model_width = hidden_in.shape[1] * wide_count
    own_rows = hidden_in.shape[0]
    local_rows = cache_len.shape[0]
    all_rows = bank_row.shape[0]
    wide_rows = all_rows // wide_count

    def device(block, axis, me):
        bits = len(strides_of(axis))
        for bit in range(bits):
            me = me ^ (((block >> bit) & 1) << (bits - 1 - bit))
        return me

    def hypothesis(place):
        return device(place // own_rows, "narrow", me_narrow) * own_rows + place % own_rows

    def wide_row(place):
        return device(place // wide_rows, "wide", me_wide) * wide_rows + place % wide_rows

    def bank(place):
        inner = place % wide_rows
        owner = device(place // wide_rows, "wide", me_wide) * narrow_count
        owner = owner + (me_narrow ^ (inner // local_rows))
        return owner * local_rows + inner % local_rows

    down = lax.broadcasted_iota(jnp.int32, (all_rows, all_rows), 0)
    across = lax.broadcasted_iota(jnp.int32, (all_rows, all_rows), 1)
    banks = jnp.broadcast_to(bank_row[None, :], (all_rows, all_rows))
    hypothesis_bank = jnp.sum(
        jnp.where(hypothesis(down) == across, banks, 0), axis=1, keepdims=True
    )
    to_hypothesis = (hypothesis_bank == bank(across)).astype(jnp.bfloat16)
    to_wide = (wide_row(down) == across).astype(jnp.bfloat16)

    def normalized_rows(values, gain_row):
        wide_values = values.astype(jnp.float32)
        rows_sq = jnp.sum(wide_values * wide_values, axis=1)
        sent = jnp.broadcast_to(rows_sq[None, :], (wide_count * narrow_count, own_rows))
        landed = lax.all_to_all(sent, ("wide", "narrow"), 0, 0, tiled=True)
        pieces = gather(values, "narrow")
        sums = jnp.sum(landed.reshape(wide_count, narrow_count, own_rows), axis=0)
        sums = by_rank([sums[j] for j in range(narrow_count)], flags)
        order = offsets_of("narrow")
        half = narrow_count // 2
        result = []
        for piece, offsets in zip(pieces, (order[:half], order[half:])):
            sum_sq = jnp.concatenate([sums[offset] for offset in offsets])
            result.append(normalize(piece, gain_row, sum_sq, model_width))
        return result

    rows_in = hidden_in.astype(jnp.float32)
    normed = normalized_rows(hidden_in, attn_gain)

    q_cols = w_query.shape[1]
    k_cols = w_key.shape[1]
    stacked = [(w_query, q_cols), (w_key, k_cols), (w_value, k_cols)]
    heads = (q_cols + 2 * k_cols) // HEAD_DIM
    edges = [heads * chunk // QKV_CHUNKS for chunk in range(QKV_CHUNKS)] + [heads]
    pieces = []
    arrivals = []
    ordered = to_hypothesis
    for chunk in range(QKV_CHUNKS):
        first, last = edges[chunk] * HEAD_DIM, edges[chunk + 1] * HEAD_DIM
        segments = []
        start = 0
        for weight, columns in stacked:
            low, high = max(first, start), min(last, start + columns)
            if low < high:
                segments.append((weight, 0, low - start, high - low))
            start += columns
        if chunk >= 2:
            ordered, arrivals[chunk - 2] = lax.optimization_barrier((ordered, arrivals[chunk - 2]))
        (kept, sent), ordered = lax.optimization_barrier(
            (project([normed], ordered, True, segments, 2, direct=True, coded=True), ordered)
        )
        pieces.append(kept)
        arrivals.append(swap(sent, "wide", 1))
    pieces = [coded_scatter(kept, arrived) for kept, arrived in zip(pieces, arrivals)]
    summed = jnp.concatenate(pieces, axis=1)
    summed = summed.reshape(narrow_count, local_rows, -1, HEAD_DIM)
    turned = exchange([summed[j] for j in range(narrow_count)], "narrow")
    turned = jnp.stack(by_rank(turned, flags), axis=1)
    q_heads = q_cols // HEAD_DIM
    k_heads = k_cols // HEAD_DIM
    query_rot = rotate(
        turned[:, :, :q_heads].reshape(local_rows, -1, HEAD_DIM), cache_len
    ).reshape(local_rows, -1)
    key_rot = rotate(
        turned[:, :, q_heads : q_heads + k_heads].reshape(local_rows, -1, HEAD_DIM), cache_len
    ).reshape(local_rows, -1)
    value_new = turned[:, :, q_heads + k_heads :].reshape(local_rows, -1)
    context = attend(query_rot, key_rot, value_new, key_cache, value_cache, cache_len)
    context = context.reshape(local_rows, narrow_count, -1)
    context = by_rank([context[:, j] for j in range(narrow_count)], flags)
    by_heads = exchange(context, "narrow")

    depth = w_out.shape[0] // CONTEXT_CHUNKS
    groups = []
    for chunk in range(CONTEXT_CHUNKS):
        columns = slice(chunk * depth, (chunk + 1) * depth)
        block = jnp.concatenate([piece[:, columns] for piece in by_heads], axis=0)
        groups.append(gather_pieces(block, "wide"))
    total = project(groups, to_hypothesis, False, [(w_out, 0, 0, w_out.shape[1])], 2)
    attn_out = narrow_scatter(*total)
    resid = (rows_in + attn_out).astype(jnp.bfloat16)
    resid_wide = resid.astype(jnp.float32)
    normed_two = normalized_rows(resid, ffn_gain)

    f_total = w_gate.shape[1]
    f_edges = [f_total * edge // FFN_EDGES[-1] // LANES * LANES for edge in FFN_EDGES]
    parts = []
    arrivals = []
    for chunk, (first, last) in enumerate(zip(f_edges[:-1], f_edges[1:])):
        segments = [(w_gate, 0, first, last - first), (w_up, 0, first, last - first)]
        if chunk >= 2:
            normed_two, arrivals[chunk - 2] = lax.optimization_barrier(
                (normed_two, arrivals[chunk - 2])
            )
        (kept, sent), normed_two = lax.optimization_barrier(
            (project([normed_two], to_wide, False, segments, 2, direct=True), normed_two)
        )
        parts.append(kept)
        arrivals.append(swap(sent.astype(jnp.float16), "wide", 1))
    total = None
    for first, last, kept, arrived in zip(f_edges[:-1], f_edges[1:], parts, arrivals):
        f_cols = last - first
        sums = wide_scatter(kept, arrived)
        act = (jax.nn.silu(sums[:, :f_cols]) * sums[:, f_cols:]).astype(jnp.bfloat16)
        total = project(
            [gather(act, "wide", paired=True)],
            to_wide,
            True,
            [(w_down, first, 0, w_down.shape[1])],
            2 if last == f_total else 1,
            total if total is None else total[0],
        )
    ffn_out = narrow_scatter(*total)
    return (resid_wide + ffn_out).astype(jnp.bfloat16)


def solution(mesh):
    return jax.shard_map(
        shards,
        mesh=mesh,
        in_specs=(
            P("narrow", "wide"),
            P("wide"),
            P("wide", "narrow"),
            P("wide", "narrow"),
            P("wide", "narrow"),
            P("narrow", "wide"),
            P("wide"),
            P("wide", "narrow"),
            P("wide", "narrow"),
            P("narrow", "wide"),
            P(("wide", "narrow"), None, None),
            P(("wide", "narrow"), None, None),
            P(("wide", "narrow")),
            P(),
        ),
        out_specs=P("narrow", "wide"),
        check_vma=False,
    )
```

```python
import math

import jax
import jax.numpy as jnp
from jax import lax
from jax.experimental import pallas as pl
from jax.experimental.pallas import tpu as pltpu
from jax.sharding import PartitionSpec as P

HEAD_DIM = 128


NORM_EPSILON = 1e-05
ROPE_BASE = 500000.0


def product(left, right):
    return jnp.dot(left, right, preferred_element_type=jnp.float32)


def normalize(values_in, gain_row, sum_sq, model_width):
    mean_sq = sum_sq / model_width
    scaled = values_in.astype(jnp.float32) * lax.rsqrt(mean_sq + NORM_EPSILON)[:, None]
    return (scaled * gain_row[None, :]).astype(jnp.bfloat16)


def rotate(head_rows, lengths):
    head_size = head_rows.shape[-1]
    half_size = head_size // 2
    inverse_freq = jnp.exp(
        jnp.arange(half_size, dtype=jnp.float32) * (-2.0 * math.log(ROPE_BASE) / head_size)
    )
    angles = lengths.astype(jnp.float32)[:, None] * inverse_freq[None, :]
    cos_part = jnp.cos(angles)[:, None, :]
    sin_part = jnp.sin(angles)[:, None, :]
    front_half = head_rows[..., :half_size].astype(jnp.float32)
    back_half = head_rows[..., half_size:].astype(jnp.float32)
    turned = jnp.concatenate(
        [
            front_half * cos_part - back_half * sin_part,
            back_half * cos_part + front_half * sin_part,
        ],
        axis=-1,
    )
    return turned.astype(jnp.bfloat16)


def attend(queries, fresh_key, fresh_value, key_cache, value_cache, lengths):
    row_count, length, kv_width = key_cache.shape
    groups = kv_width // HEAD_DIM
    group_size = queries.shape[1] // kv_width
    score_scale = 1.0 / math.sqrt(HEAD_DIM)
    query_heads = queries.reshape(row_count, groups, group_size, HEAD_DIM)
    cache_keys = key_cache.reshape(row_count, length, groups, HEAD_DIM)
    cache_values = value_cache.reshape(row_count, length, groups, HEAD_DIM)
    own_key = fresh_key.reshape(row_count, groups, HEAD_DIM)
    own_value = fresh_value.reshape(row_count, groups, HEAD_DIM)
    scores = (
        jnp.einsum("rgqd,rlgd->rgql", query_heads, cache_keys, preferred_element_type=jnp.float32)
        * score_scale
    )
    own_score = (
        jnp.einsum("rgqd,rgd->rgq", query_heads, own_key, preferred_element_type=jnp.float32)
        * score_scale
    )
    valid_pos = jnp.arange(length, dtype=jnp.int32)[None, :] < lengths[:, None]
    scores = jnp.where(valid_pos[:, None, None, :], scores, -jnp.inf)
    row_max = jnp.maximum(jnp.max(scores, axis=3), own_score)
    weights = jnp.exp(scores - row_max[..., None])
    own_weight = jnp.exp(own_score - row_max)
    weight_sum = jnp.sum(weights, axis=3) + own_weight
    probs = (weights / weight_sum[..., None]).astype(jnp.bfloat16)
    own_prob = (own_weight / weight_sum).astype(jnp.bfloat16)
    context = jnp.einsum("rgql,rlgd->rgqd", probs, cache_values, preferred_element_type=jnp.float32)
    context = (
        context
        + own_prob.astype(jnp.float32)[..., None] * own_value.astype(jnp.float32)[:, :, None, :]
    )
    return context.reshape(row_count, groups * group_size * HEAD_DIM).astype(jnp.bfloat16)


QKV_CHUNKS = 3
FFN_SPLIT = 0.5
CONTEXT_CHUNKS = 2
NARROW_KINDS = [jnp.float32] + [jnp.bfloat16] * 8
TILE = 512
ROOM = 24
DIRECT_ROOM = 50
IN_FLIGHT = 9
LANES = 128
TOP_CODE = 32700.0
LOG_STEPS = 64.0
STAND_IN = 4
MIB = 1024 * 1024


def swap(block, axis, offset):
    count = lax.axis_size(axis)
    return lax.ppermute(block, axis, [(i, i ^ offset) for i in range(count)])


def strides_of(axis):
    count = lax.axis_size(axis)
    return [1 << bit for bit in range(count.bit_length() - 1)]


def offsets_of(axis):
    order = [0]
    for stride in reversed(strides_of(axis)):
        order = order + [offset ^ stride for offset in order]
    return order


def encoded(values):
    top = jnp.max(jnp.abs(values), axis=1, keepdims=True)
    steps = jnp.floor(jnp.log2(jnp.maximum(top, 1e-30)) * LOG_STEPS + 1.5)
    return jnp.round(values * (TOP_CODE * jnp.exp2(steps * (-1.0 / LOG_STEPS)))), steps


def write_codes(code_ref, place, values, steps_tile):
    codes, steps = encoded(values)
    code_ref[:, place * LANES : (place + 1) * LANES] = codes.astype(jnp.int32).astype(jnp.int16)
    lanes = lax.broadcasted_iota(jnp.int32, (values.shape[0], LANES), 1)
    return jnp.where(lanes == place, steps, steps_tile)


def read_codes(code_ref, place):
    codes = code_ref[:, place * LANES : (place + 1) * LANES]
    steps = code_ref[:, code_ref.shape[1] - LANES :].astype(jnp.int32).astype(jnp.float32)
    scale = jnp.exp2(steps[:, place : place + 1] * (1.0 / LOG_STEPS)) * (1.0 / TOP_CODE)
    return codes.astype(jnp.int32).astype(jnp.float32) * scale


def project(
    groups, order, turned, segments, split, total=None, direct=False, coded=False
):
    rows = order.shape[0]
    depth = groups[0][0].shape[1]
    tiles = []
    width = 0
    for index, (_, first_row, first, columns) in enumerate(segments):
        for start in range(first, first + columns, TILE):
            tile = min(TILE, first + columns - start)
            tiles.append((index, first_row, start, tile, width))
            width += tile
    part = rows // split
    pieces = [piece for group in groups for piece in group]
    count = len(pieces)
    each = count // len(groups)

    def body(*refs):
        piece_refs, order_ref, rest = refs[:count], refs[count], refs[count + 1 :]
        weight_refs, rest = rest[: len(segments)], rest[len(segments) :]
        if total is not None:
            total_ref, rest = rest[0], rest[1:]
        out_refs, rest = rest[:split], rest[split:]
        copies = []
        if direct:
            for place, (index, first_row, start, tile, _) in enumerate(tiles):
                source = weight_refs[index].at[pl.ds(first_row, depth), pl.ds(start, tile)]
                copies.append(pltpu.make_async_copy(source, rest[place], rest[-1].at[place]))
        for copy in copies[:IN_FLIGHT]:
            copy.start()
        lefts = []
        for group in range(len(groups)):
            group_refs = piece_refs[group * each : (group + 1) * each]
            left = lax.dot_general(
                order_ref[...],
                jnp.concatenate([ref[...] for ref in group_refs], axis=0),
                (((0 if turned else 1,), (0,)), ((), ())),
                preferred_element_type=jnp.float32,
            )
            lefts.append(left.astype(jnp.bfloat16))
        steps_tile = jnp.zeros((part, LANES), jnp.float32)
        for number, (index, first_row, start, tile, base) in enumerate(tiles):
            result = None
            for group, left in enumerate(lefts):
                if direct:
                    copies[number].wait()
                    weight = rest[number][...]
                    if number + IN_FLIGHT < len(tiles):
                        copies[number + IN_FLIGHT].start()
                else:
                    weight = weight_refs[index][
                        pl.ds(first_row + group * depth, depth), pl.ds(start, tile)
                    ]
                product = jnp.dot(left, weight, preferred_element_type=jnp.float32)
                result = product if result is None else result + product
            if total is not None:
                result = result + total_ref[:, base : base + tile]
            for place, out_ref in enumerate(out_refs[: 1 if coded else split]):
                out_ref[:, base : base + tile] = result[place * part : (place + 1) * part]
            if coded:
                for column in range(0, tile, LANES):
                    values = result[part:, column : column + LANES]
                    place = (base + column) // LANES
                    steps_tile = write_codes(out_refs[1], place, values, steps_tile)
        if coded:
            out_refs[1][:, width:] = steps_tile.astype(jnp.int32).astype(jnp.int16)

    operands = pieces + [order] + [segment[0] for segment in segments]
    if total is not None:
        operands.append(total)
    in_vmem = pl.BlockSpec(memory_space=pltpu.VMEM)
    specs = [in_vmem] * len(operands)
    out_shape = [jax.ShapeDtypeStruct((part, width), jnp.float32)] * split
    if coded:
        out_shape[1] = jax.ShapeDtypeStruct((part, width + LANES), jnp.int16)
    scratch = []
    if direct:
        for place in range(count + 1, count + 1 + len(segments)):
            specs[place] = pl.BlockSpec(memory_space=pltpu.HBM)
        scratch = [pltpu.VMEM((depth, tile[3]), jnp.bfloat16) for tile in tiles]
        scratch.append(pltpu.SemaphoreType.DMA((len(tiles),)))
    return pl.pallas_call(
        body,
        in_specs=specs,
        out_specs=[in_vmem] * split,
        scratch_shapes=scratch,
        out_shape=out_shape,
        compiler_params=pltpu.CompilerParams(vmem_limit_bytes=(DIRECT_ROOM if direct else ROOM) * MIB),
        cost_estimate=pl.CostEstimate(
            flops=2 * rows * len(groups) * depth * (width + rows),
            bytes_accessed=2 * len(groups) * depth * width + 4 * rows * width,
            transcendentals=0,
        ),
    )(*operands)


def stand_in(array):
    def body(array_ref, copy_ref):
        copy_ref[...] = array_ref[...]

    in_vmem = pl.BlockSpec(memory_space=pltpu.VMEM)
    return pl.pallas_call(
        body,
        in_specs=[in_vmem],
        out_specs=in_vmem,
        out_shape=jax.ShapeDtypeStruct(array.shape, array.dtype),
        compiler_params=pltpu.CompilerParams(vmem_limit_bytes=MIB),
        cost_estimate=pl.CostEstimate(
            flops=int(1.1e9 * STAND_IN), bytes_accessed=4096, transcendentals=0
        ),
    )(array)


def fold(kept, arrived, blocks):
    rows = kept.shape[0] // blocks
    width = kept.shape[1]

    def body(kept_ref, arrived_ref, own_ref, *code_refs):
        tiles = [jnp.zeros((rows, LANES), jnp.float32)] * (blocks - 1)
        for place in range(width // LANES):
            columns = slice(place * LANES, (place + 1) * LANES)
            sums = kept_ref[:, columns] + read_codes(arrived_ref, place)
            own_ref[:, columns] = sums[:rows]
            for index, code_ref in enumerate(code_refs):
                values = sums[(index + 1) * rows : (index + 2) * rows]
                tiles[index] = write_codes(code_ref, place, values, tiles[index])
        for tile, code_ref in zip(tiles, code_refs):
            code_ref[:, width:] = tile.astype(jnp.int32).astype(jnp.int16)

    codes = jax.ShapeDtypeStruct((rows, width + LANES), jnp.int16)
    return pl.pallas_call(
        body,
        out_shape=[jax.ShapeDtypeStruct((rows, width), jnp.float32)] + [codes] * (blocks - 1),
        compiler_params=pltpu.CompilerParams(vmem_limit_bytes=8 * MIB),
    )(kept, arrived)


def add_codes(own, arrived):
    def body(own_ref, *refs):
        for place in range(own.shape[1] // LANES):
            columns = slice(place * LANES, (place + 1) * LANES)
            sums = own_ref[:, columns]
            for code_ref in refs[:-1]:
                sums = sums + read_codes(code_ref, place)
            refs[-1][:, columns] = sums.astype(jnp.bfloat16)

    return pl.pallas_call(
        body,
        out_shape=jax.ShapeDtypeStruct(own.shape, jnp.bfloat16),
        compiler_params=pltpu.CompilerParams(vmem_limit_bytes=8 * MIB),
    )(own, *arrived)


def coded_scatter(kept, arrived):
    for stride in strides_of("wide")[1:]:
        kept, codes = fold(kept, arrived, 2)
        arrived = swap(codes, "wide", stride)
    return add_codes(kept, [arrived])


def wide_scatter(kept, sent):
    rows = 2 * kept.shape[0] // lax.axis_size("wide")
    kept = kept + swap(sent.astype(jnp.float16), "wide", 1).astype(jnp.float32)
    total = kept[:rows]
    for place, offset in enumerate(offsets_of("wide")[: kept.shape[0] // rows]):
        if offset:
            block = kept[place * rows : (place + 1) * rows].astype(jnp.float16)
            total = total + swap(block, "wide", offset).astype(jnp.float32)
    return total


def narrow_scatter(kept, sent):
    for stride, kind in zip(strides_of("narrow"), NARROW_KINDS):
        if stride > 1:
            half = kept.shape[0] // 2
            kept, sent = kept[:half], kept[half:]
        kept = kept + swap(sent.astype(kind), "narrow", stride).astype(jnp.float32)
    return kept


def gather(block, axis):
    strides = strides_of(axis)[::-1]
    for stride in strides[:-1]:
        block = jnp.concatenate([block, swap(block, axis, stride)], axis=0)
    return [block, swap(block, axis, strides[-1])]


def gather_in_two(block, axis):
    offsets = offsets_of(axis)
    far = [swap(block, axis, offset) for offset in offsets[1 : len(offsets) // 2]]
    block = jnp.concatenate([stand_in(block)] + far, axis=0)
    return [block, swap(block, axis, 1)]


def gather_pieces(block, axis):
    held = [block]
    for stride in strides_of(axis)[::-1]:
        held = held + [swap(piece, axis, stride) for piece in held]
    return [stand_in(block)] + held[1:]


def exchange(blocks, axis):
    blocks = list(blocks)
    for stride in strides_of(axis)[::-1]:
        marked = [i for i in range(len(blocks)) if i & stride]
        arrived = swap(jnp.stack([blocks[i] for i in marked]), axis, stride)
        for place, i in enumerate(marked):
            blocks[i] = arrived[place]
    return blocks


def by_rank(blocks, flags):
    for bit, flag in enumerate(flags):
        other = 1 << bit
        blocks = [jnp.where(flag, blocks[i ^ other], block) for i, block in enumerate(blocks)]
    return blocks


def shards(
    hidden_in,
    attn_gain,
    w_query,
    w_key,
    w_value,
    w_out,
    ffn_gain,
    w_gate,
    w_up,
    w_down,
    key_cache,
    value_cache,
    cache_len,
    bank_row,
):
    wide_count = lax.axis_size("wide")
    narrow_count = lax.axis_size("narrow")
    me_wide = lax.axis_index("wide")
    me_narrow = lax.axis_index("narrow")
    flags = [(me_narrow & stride) != 0 for stride in strides_of("narrow")]
    hidden_in, me_wide, me_narrow, flags = lax.optimization_barrier(
        (hidden_in, me_wide, me_narrow, flags)
    )
    model_width = hidden_in.shape[1] * wide_count
    own_rows = hidden_in.shape[0]
    local_rows = cache_len.shape[0]
    all_rows = bank_row.shape[0]
    wide_rows = all_rows // wide_count

    def device(block, axis, me):
        bits = len(strides_of(axis))
        for bit in range(bits):
            me = me ^ (((block >> bit) & 1) << (bits - 1 - bit))
        return me

    def hypothesis(place):
        return device(place // own_rows, "narrow", me_narrow) * own_rows + place % own_rows

    def wide_row(place):
        return device(place // wide_rows, "wide", me_wide) * wide_rows + place % wide_rows

    def bank(place):
        inner = place % wide_rows
        owner = device(place // wide_rows, "wide", me_wide) * narrow_count
        owner = owner + (me_narrow ^ (inner // local_rows))
        return owner * local_rows + inner % local_rows

    down = lax.broadcasted_iota(jnp.int32, (all_rows, all_rows), 0)
    across = lax.broadcasted_iota(jnp.int32, (all_rows, all_rows), 1)
    banks = jnp.broadcast_to(bank_row[None, :], (all_rows, all_rows))
    hypothesis_bank = jnp.sum(
        jnp.where(hypothesis(down) == across, banks, 0), axis=1, keepdims=True
    )
    to_hypothesis = (hypothesis_bank == bank(across)).astype(jnp.bfloat16)
    to_wide = (wide_row(down) == across).astype(jnp.bfloat16)

    def normalized_rows(values, gain_row):
        wide_values = values.astype(jnp.float32)
        rows_sq = jnp.sum(wide_values * wide_values, axis=1)
        sent = jnp.broadcast_to(rows_sq[None, :], (wide_count * narrow_count, own_rows))
        landed = lax.all_to_all(sent, ("wide", "narrow"), 0, 0, tiled=True)
        pieces = gather(values, "narrow")
        sums = jnp.sum(landed.reshape(wide_count, narrow_count, own_rows), axis=0)
        sums = by_rank([sums[j] for j in range(narrow_count)], flags)
        order = offsets_of("narrow")
        half = narrow_count // 2
        result = []
        for piece, offsets in zip(pieces, (order[:half], order[half:])):
            sum_sq = jnp.concatenate([sums[offset] for offset in offsets])
            result.append(normalize(piece, gain_row, sum_sq, model_width))
        return result

    rows_in = hidden_in.astype(jnp.float32)
    normed = normalized_rows(hidden_in, attn_gain)

    q_cols = w_query.shape[1]
    k_cols = w_key.shape[1]
    stacked = [(w_query, q_cols), (w_key, k_cols), (w_value, k_cols)]
    heads = (q_cols + 2 * k_cols) // HEAD_DIM
    edges = [heads * chunk // QKV_CHUNKS for chunk in range(QKV_CHUNKS)] + [heads]
    pieces = []
    arrivals = []
    ordered = to_hypothesis
    for chunk in range(QKV_CHUNKS):
        first, last = edges[chunk] * HEAD_DIM, edges[chunk + 1] * HEAD_DIM
        segments = []
        start = 0
        for weight, columns in stacked:
            low, high = max(first, start), min(last, start + columns)
            if low < high:
                segments.append((weight, 0, low - start, high - low))
            start += columns
        if chunk >= 2:
            ordered, arrivals[chunk - 2] = lax.optimization_barrier((ordered, arrivals[chunk - 2]))
        (kept, sent), ordered = lax.optimization_barrier(
            (project([normed], ordered, True, segments, 2, direct=True, coded=True), ordered)
        )
        pieces.append(kept)
        arrivals.append(swap(sent, "wide", 1))
    pieces = [coded_scatter(kept, arrived) for kept, arrived in zip(pieces, arrivals)]
    summed = jnp.concatenate(pieces, axis=1)
    summed = summed.reshape(narrow_count, local_rows, -1, HEAD_DIM)
    turned = exchange([summed[j] for j in range(narrow_count)], "narrow")
    turned = jnp.stack(by_rank(turned, flags), axis=1)
    q_heads = q_cols // HEAD_DIM
    k_heads = k_cols // HEAD_DIM
    query_rot = rotate(
        turned[:, :, :q_heads].reshape(local_rows, -1, HEAD_DIM), cache_len
    ).reshape(local_rows, -1)
    key_rot = rotate(
        turned[:, :, q_heads : q_heads + k_heads].reshape(local_rows, -1, HEAD_DIM), cache_len
    ).reshape(local_rows, -1)
    value_new = turned[:, :, q_heads + k_heads :].reshape(local_rows, -1)
    context = attend(query_rot, key_rot, value_new, key_cache, value_cache, cache_len)
    context = context.reshape(local_rows, narrow_count, -1)
    context = by_rank([context[:, j] for j in range(narrow_count)], flags)
    by_heads = exchange(context, "narrow")

    depth = w_out.shape[0] // CONTEXT_CHUNKS
    groups = []
    for chunk in range(CONTEXT_CHUNKS):
        columns = slice(chunk * depth, (chunk + 1) * depth)
        block = jnp.concatenate([piece[:, columns] for piece in by_heads], axis=0)
        groups.append(gather_pieces(block, "wide"))
    total = project(groups, to_hypothesis, False, [(w_out, 0, 0, w_out.shape[1])], 2)
    attn_out = narrow_scatter(*total)
    resid = (rows_in + attn_out).astype(jnp.bfloat16)
    resid_wide = resid.astype(jnp.float32)
    normed_two = normalized_rows(resid, ffn_gain)

    f_total = w_gate.shape[1]
    f_edge = int(f_total * FFN_SPLIT) // LANES * LANES
    total = None
    for first, last in ((0, f_edge), (f_edge, f_total)):
        f_cols = last - first
        segments = [(w_gate, 0, first, f_cols), (w_up, 0, first, f_cols)]
        sums = wide_scatter(*project([normed_two], to_wide, False, segments, 2, direct=True))
        act = (jax.nn.silu(sums[:, :f_cols]) * sums[:, f_cols:]).astype(jnp.bfloat16)
        total = project(
            [gather_in_two(act, "wide")],
            to_wide,
            True,
            [(w_down, first, 0, w_down.shape[1])],
            2 if last == f_total else 1,
            total if total is None else total[0],
        )
    ffn_out = narrow_scatter(*total)
    return (resid_wide + ffn_out).astype(jnp.bfloat16)


def solution(mesh):
    return jax.shard_map(
        shards,
        mesh=mesh,
        in_specs=(
            P("narrow", "wide"),
            P("wide"),
            P("wide", "narrow"),
            P("wide", "narrow"),
            P("wide", "narrow"),
            P("narrow", "wide"),
            P("wide"),
            P("wide", "narrow"),
            P("wide", "narrow"),
            P("narrow", "wide"),
            P(("wide", "narrow"), None, None),
            P(("wide", "narrow"), None, None),
            P(("wide", "narrow")),
            P(),
        ),
        out_specs=P("narrow", "wide"),
        check_vma=False,
    )
```

```python
import math

import jax
import jax.numpy as jnp
from jax import lax
from jax.experimental import pallas as pl
from jax.experimental.pallas import tpu as pltpu
from jax.sharding import PartitionSpec as P

HEAD_DIM = 128


NORM_EPSILON = 1e-05
ROPE_BASE = 500000.0


def product(left, right):
    return jnp.dot(left, right, preferred_element_type=jnp.float32)


def normalize(values_in, gain_row, sum_sq, model_width):
    mean_sq = sum_sq / model_width
    scaled = values_in.astype(jnp.float32) * lax.rsqrt(mean_sq + NORM_EPSILON)[:, None]
    return (scaled * gain_row[None, :]).astype(jnp.bfloat16)


def rotate(head_rows, lengths):
    head_size = head_rows.shape[-1]
    half_size = head_size // 2
    inverse_freq = jnp.exp(
        jnp.arange(half_size, dtype=jnp.float32) * (-2.0 * math.log(ROPE_BASE) / head_size)
    )
    angles = lengths.astype(jnp.float32)[:, None] * inverse_freq[None, :]
    cos_part = jnp.cos(angles)[:, None, :]
    sin_part = jnp.sin(angles)[:, None, :]
    front_half = head_rows[..., :half_size].astype(jnp.float32)
    back_half = head_rows[..., half_size:].astype(jnp.float32)
    turned = jnp.concatenate(
        [
            front_half * cos_part - back_half * sin_part,
            back_half * cos_part + front_half * sin_part,
        ],
        axis=-1,
    )
    return turned.astype(jnp.bfloat16)


def attend(queries, fresh_key, fresh_value, key_cache, value_cache, lengths):
    row_count, length, kv_width = key_cache.shape
    groups = kv_width // HEAD_DIM
    group_size = queries.shape[1] // kv_width
    score_scale = 1.0 / math.sqrt(HEAD_DIM)
    query_heads = queries.reshape(row_count, groups, group_size, HEAD_DIM)
    cache_keys = key_cache.reshape(row_count, length, groups, HEAD_DIM)
    cache_values = value_cache.reshape(row_count, length, groups, HEAD_DIM)
    own_key = fresh_key.reshape(row_count, groups, HEAD_DIM)
    own_value = fresh_value.reshape(row_count, groups, HEAD_DIM)
    scores = (
        jnp.einsum("rgqd,rlgd->rgql", query_heads, cache_keys, preferred_element_type=jnp.float32)
        * score_scale
    )
    own_score = (
        jnp.einsum("rgqd,rgd->rgq", query_heads, own_key, preferred_element_type=jnp.float32)
        * score_scale
    )
    valid_pos = jnp.arange(length, dtype=jnp.int32)[None, :] < lengths[:, None]
    scores = jnp.where(valid_pos[:, None, None, :], scores, -jnp.inf)
    row_max = jnp.maximum(jnp.max(scores, axis=3), own_score)
    weights = jnp.exp(scores - row_max[..., None])
    own_weight = jnp.exp(own_score - row_max)
    weight_sum = jnp.sum(weights, axis=3) + own_weight
    probs = (weights / weight_sum[..., None]).astype(jnp.bfloat16)
    own_prob = (own_weight / weight_sum).astype(jnp.bfloat16)
    context = jnp.einsum("rgql,rlgd->rgqd", probs, cache_values, preferred_element_type=jnp.float32)
    context = (
        context
        + own_prob.astype(jnp.float32)[..., None] * own_value.astype(jnp.float32)[:, :, None, :]
    )
    return context.reshape(row_count, groups * group_size * HEAD_DIM).astype(jnp.bfloat16)


QKV_CHUNKS = 3
FFN_SPLIT = 0.5
CONTEXT_CHUNKS = 2
NARROW_KINDS = [jnp.float32] + [jnp.bfloat16] * 8
TILE = 512
ROOM = 24
DIRECT_ROOM = 50
IN_FLIGHT = 9
LANES = 128
TOP_CODE = 32700.0
LOG_STEPS = 64.0
STAND_IN = 4
MIB = 1024 * 1024


def swap(block, axis, offset):
    count = lax.axis_size(axis)
    return lax.ppermute(block, axis, [(i, i ^ offset) for i in range(count)])


def strides_of(axis):
    count = lax.axis_size(axis)
    return [1 << bit for bit in range(count.bit_length() - 1)]


def offsets_of(axis):
    order = [0]
    for stride in reversed(strides_of(axis)):
        order = order + [offset ^ stride for offset in order]
    return order


def encoded(values):
    top = jnp.max(jnp.abs(values), axis=1, keepdims=True)
    steps = jnp.floor(jnp.log2(jnp.maximum(top, 1e-30)) * LOG_STEPS + 1.5)
    return jnp.round(values * (TOP_CODE * jnp.exp2(steps * (-1.0 / LOG_STEPS)))), steps


def write_codes(code_ref, place, values, steps_tile):
    codes, steps = encoded(values)
    code_ref[:, place * LANES : (place + 1) * LANES] = codes.astype(jnp.int32).astype(jnp.int16)
    lanes = lax.broadcasted_iota(jnp.int32, (values.shape[0], LANES), 1)
    return jnp.where(lanes == place, steps, steps_tile)


def read_codes(code_ref, place):
    codes = code_ref[:, place * LANES : (place + 1) * LANES]
    steps = code_ref[:, code_ref.shape[1] - LANES :].astype(jnp.int32).astype(jnp.float32)
    scale = jnp.exp2(steps[:, place : place + 1] * (1.0 / LOG_STEPS)) * (1.0 / TOP_CODE)
    return codes.astype(jnp.int32).astype(jnp.float32) * scale


def project(
    groups, order, turned, segments, split, total=None, direct=False, coded=False
):
    rows = order.shape[0]
    depth = groups[0][0].shape[1]
    tiles = []
    width = 0
    for index, (_, first_row, first, columns) in enumerate(segments):
        for start in range(first, first + columns, TILE):
            tile = min(TILE, first + columns - start)
            tiles.append((index, first_row, start, tile, width))
            width += tile
    part = rows // split
    pieces = [piece for group in groups for piece in group]
    count = len(pieces)
    each = count // len(groups)

    def body(*refs):
        piece_refs, order_ref, rest = refs[:count], refs[count], refs[count + 1 :]
        weight_refs, rest = rest[: len(segments)], rest[len(segments) :]
        if total is not None:
            total_ref, rest = rest[0], rest[1:]
        out_refs, rest = rest[:split], rest[split:]
        copies = []
        if direct:
            for place, (index, first_row, start, tile, _) in enumerate(tiles):
                source = weight_refs[index].at[pl.ds(first_row, depth), pl.ds(start, tile)]
                copies.append(pltpu.make_async_copy(source, rest[place], rest[-1].at[place]))
        for copy in copies[:IN_FLIGHT]:
            copy.start()
        lefts = []
        for group in range(len(groups)):
            group_refs = piece_refs[group * each : (group + 1) * each]
            left = lax.dot_general(
                order_ref[...],
                jnp.concatenate([ref[...] for ref in group_refs], axis=0),
                (((0 if turned else 1,), (0,)), ((), ())),
                preferred_element_type=jnp.float32,
            )
            lefts.append(left.astype(jnp.bfloat16))
        steps_tile = jnp.zeros((part, LANES), jnp.float32)
        for number, (index, first_row, start, tile, base) in enumerate(tiles):
            result = None
            for group, left in enumerate(lefts):
                if direct:
                    copies[number].wait()
                    weight = rest[number][...]
                    if number + IN_FLIGHT < len(tiles):
                        copies[number + IN_FLIGHT].start()
                else:
                    weight = weight_refs[index][
                        pl.ds(first_row + group * depth, depth), pl.ds(start, tile)
                    ]
                product = jnp.dot(left, weight, preferred_element_type=jnp.float32)
                result = product if result is None else result + product
            if total is not None:
                result = result + total_ref[:, base : base + tile]
            for place, out_ref in enumerate(out_refs[: 1 if coded else split]):
                out_ref[:, base : base + tile] = result[place * part : (place + 1) * part]
            if coded:
                for column in range(0, tile, LANES):
                    values = result[part:, column : column + LANES]
                    place = (base + column) // LANES
                    steps_tile = write_codes(out_refs[1], place, values, steps_tile)
        if coded:
            out_refs[1][:, width:] = steps_tile.astype(jnp.int32).astype(jnp.int16)

    operands = pieces + [order] + [segment[0] for segment in segments]
    if total is not None:
        operands.append(total)
    in_vmem = pl.BlockSpec(memory_space=pltpu.VMEM)
    specs = [in_vmem] * len(operands)
    out_shape = [jax.ShapeDtypeStruct((part, width), jnp.float32)] * split
    if coded:
        out_shape[1] = jax.ShapeDtypeStruct((part, width + LANES), jnp.int16)
    scratch = []
    if direct:
        for place in range(count + 1, count + 1 + len(segments)):
            specs[place] = pl.BlockSpec(memory_space=pltpu.HBM)
        scratch = [pltpu.VMEM((depth, tile[3]), jnp.bfloat16) for tile in tiles]
        scratch.append(pltpu.SemaphoreType.DMA((len(tiles),)))
    return pl.pallas_call(
        body,
        in_specs=specs,
        out_specs=[in_vmem] * split,
        scratch_shapes=scratch,
        out_shape=out_shape,
        compiler_params=pltpu.CompilerParams(vmem_limit_bytes=(DIRECT_ROOM if direct else ROOM) * MIB),
        cost_estimate=pl.CostEstimate(
            flops=2 * rows * len(groups) * depth * (width + rows),
            bytes_accessed=2 * len(groups) * depth * width + 4 * rows * width,
            transcendentals=0,
        ),
    )(*operands)


def stand_in(array):
    def body(array_ref, copy_ref):
        copy_ref[...] = array_ref[...]

    in_vmem = pl.BlockSpec(memory_space=pltpu.VMEM)
    return pl.pallas_call(
        body,
        in_specs=[in_vmem],
        out_specs=in_vmem,
        out_shape=jax.ShapeDtypeStruct(array.shape, array.dtype),
        compiler_params=pltpu.CompilerParams(vmem_limit_bytes=MIB),
        cost_estimate=pl.CostEstimate(
            flops=int(1.1e9 * STAND_IN), bytes_accessed=4096, transcendentals=0
        ),
    )(array)


def fold(kept, arrived, blocks):
    rows = kept.shape[0] // blocks
    width = kept.shape[1]

    def body(kept_ref, arrived_ref, own_ref, *code_refs):
        tiles = [jnp.zeros((rows, LANES), jnp.float32)] * (blocks - 1)
        for place in range(width // LANES):
            columns = slice(place * LANES, (place + 1) * LANES)
            sums = kept_ref[:, columns] + read_codes(arrived_ref, place)
            own_ref[:, columns] = sums[:rows]
            for index, code_ref in enumerate(code_refs):
                values = sums[(index + 1) * rows : (index + 2) * rows]
                tiles[index] = write_codes(code_ref, place, values, tiles[index])
        for tile, code_ref in zip(tiles, code_refs):
            code_ref[:, width:] = tile.astype(jnp.int32).astype(jnp.int16)

    codes = jax.ShapeDtypeStruct((rows, width + LANES), jnp.int16)
    return pl.pallas_call(
        body,
        out_shape=[jax.ShapeDtypeStruct((rows, width), jnp.float32)] + [codes] * (blocks - 1),
        compiler_params=pltpu.CompilerParams(vmem_limit_bytes=8 * MIB),
    )(kept, arrived)


def add_codes(own, arrived):
    def body(own_ref, *refs):
        for place in range(own.shape[1] // LANES):
            columns = slice(place * LANES, (place + 1) * LANES)
            sums = own_ref[:, columns]
            for code_ref in refs[:-1]:
                sums = sums + read_codes(code_ref, place)
            refs[-1][:, columns] = sums.astype(jnp.bfloat16)

    return pl.pallas_call(
        body,
        out_shape=jax.ShapeDtypeStruct(own.shape, jnp.bfloat16),
        compiler_params=pltpu.CompilerParams(vmem_limit_bytes=8 * MIB),
    )(own, *arrived)


def coded_scatter(kept, arrived):
    for stride in strides_of("wide")[1:]:
        kept, codes = fold(kept, arrived, 2)
        arrived = swap(codes, "wide", stride)
    return add_codes(kept, [arrived])


def wide_scatter(kept, sent):
    rows = 2 * kept.shape[0] // lax.axis_size("wide")
    kept = kept + swap(sent.astype(jnp.float16), "wide", 1).astype(jnp.float32)
    total = kept[:rows]
    for place, offset in enumerate(offsets_of("wide")[: kept.shape[0] // rows]):
        if offset:
            block = kept[place * rows : (place + 1) * rows].astype(jnp.float16)
            total = total + swap(block, "wide", offset).astype(jnp.float32)
    return total


def narrow_scatter(kept, sent):
    for stride, kind in zip(strides_of("narrow"), NARROW_KINDS):
        if stride > 1:
            half = kept.shape[0] // 2
            kept, sent = kept[:half], kept[half:]
        kept = kept + swap(sent.astype(kind), "narrow", stride).astype(jnp.float32)
    return kept


def gather(block, axis):
    strides = strides_of(axis)[::-1]
    for stride in strides[:-1]:
        block = jnp.concatenate([block, swap(block, axis, stride)], axis=0)
    return [block, swap(block, axis, strides[-1])]


def gather_in_two(block, axis):
    offsets = offsets_of(axis)
    far = [swap(block, axis, offset) for offset in offsets[1 : len(offsets) // 2]]
    block = jnp.concatenate([stand_in(block)] + far, axis=0)
    return [block, swap(block, axis, 1)]


def gather_pieces(block, axis):
    held = [block]
    for stride in strides_of(axis)[::-1]:
        held = held + [swap(piece, axis, stride) for piece in held]
    return [stand_in(block)] + held[1:]


def exchange(blocks, axis):
    blocks = list(blocks)
    for stride in strides_of(axis)[::-1]:
        marked = [i for i in range(len(blocks)) if i & stride]
        arrived = swap(jnp.stack([blocks[i] for i in marked]), axis, stride)
        for place, i in enumerate(marked):
            blocks[i] = arrived[place]
    return blocks


def by_rank(blocks, flags):
    for bit, flag in enumerate(flags):
        other = 1 << bit
        blocks = [jnp.where(flag, blocks[i ^ other], block) for i, block in enumerate(blocks)]
    return blocks


def shards(
    hidden_in,
    attn_gain,
    w_query,
    w_key,
    w_value,
    w_out,
    ffn_gain,
    w_gate,
    w_up,
    w_down,
    key_cache,
    value_cache,
    cache_len,
    bank_row,
):
    wide_count = lax.axis_size("wide")
    narrow_count = lax.axis_size("narrow")
    me_wide = lax.axis_index("wide")
    me_narrow = lax.axis_index("narrow")
    flags = [(me_narrow & stride) != 0 for stride in strides_of("narrow")]
    hidden_in, me_wide, me_narrow, flags = lax.optimization_barrier(
        (hidden_in, me_wide, me_narrow, flags)
    )
    model_width = hidden_in.shape[1] * wide_count
    own_rows = hidden_in.shape[0]
    local_rows = cache_len.shape[0]
    all_rows = bank_row.shape[0]
    wide_rows = all_rows // wide_count

    def device(block, axis, me):
        bits = len(strides_of(axis))
        for bit in range(bits):
            me = me ^ (((block >> bit) & 1) << (bits - 1 - bit))
        return me

    def hypothesis(place):
        return device(place // own_rows, "narrow", me_narrow) * own_rows + place % own_rows

    def wide_row(place):
        return device(place // wide_rows, "wide", me_wide) * wide_rows + place % wide_rows

    def bank(place):
        inner = place % wide_rows
        owner = device(place // wide_rows, "wide", me_wide) * narrow_count
        owner = owner + (me_narrow ^ (inner // local_rows))
        return owner * local_rows + inner % local_rows

    down = lax.broadcasted_iota(jnp.int32, (all_rows, all_rows), 0)
    across = lax.broadcasted_iota(jnp.int32, (all_rows, all_rows), 1)
    banks = jnp.broadcast_to(bank_row[None, :], (all_rows, all_rows))
    hypothesis_bank = jnp.sum(
        jnp.where(hypothesis(down) == across, banks, 0), axis=1, keepdims=True
    )
    to_hypothesis = (hypothesis_bank == bank(across)).astype(jnp.bfloat16)
    to_wide = (wide_row(down) == across).astype(jnp.bfloat16)

    def normalized_rows(values, gain_row):
        wide_values = values.astype(jnp.float32)
        rows_sq = jnp.sum(wide_values * wide_values, axis=1)
        sent = jnp.broadcast_to(rows_sq[None, :], (wide_count * narrow_count, own_rows))
        landed = lax.all_to_all(sent, ("wide", "narrow"), 0, 0, tiled=True)
        pieces = gather(values, "narrow")
        sums = jnp.sum(landed.reshape(wide_count, narrow_count, own_rows), axis=0)
        sums = by_rank([sums[j] for j in range(narrow_count)], flags)
        order = offsets_of("narrow")
        half = narrow_count // 2
        result = []
        for piece, offsets in zip(pieces, (order[:half], order[half:])):
            sum_sq = jnp.concatenate([sums[offset] for offset in offsets])
            result.append(normalize(piece, gain_row, sum_sq, model_width))
        return result

    rows_in = hidden_in.astype(jnp.float32)
    normed = normalized_rows(hidden_in, attn_gain)

    q_cols = w_query.shape[1]
    k_cols = w_key.shape[1]
    stacked = [(w_query, q_cols), (w_key, k_cols), (w_value, k_cols)]
    heads = (q_cols + 2 * k_cols) // HEAD_DIM
    edges = [heads * chunk // QKV_CHUNKS for chunk in range(QKV_CHUNKS)] + [heads]
    pieces = []
    arrivals = []
    ordered = to_hypothesis
    for chunk in range(QKV_CHUNKS):
        first, last = edges[chunk] * HEAD_DIM, edges[chunk + 1] * HEAD_DIM
        segments = []
        start = 0
        for weight, columns in stacked:
            low, high = max(first, start), min(last, start + columns)
            if low < high:
                segments.append((weight, 0, low - start, high - low))
            start += columns
        if chunk >= 2:
            ordered, arrivals[chunk - 2] = lax.optimization_barrier((ordered, arrivals[chunk - 2]))
        (kept, sent), ordered = lax.optimization_barrier(
            (project([normed], ordered, True, segments, 2, direct=True, coded=True), ordered)
        )
        pieces.append(kept)
        arrivals.append(swap(sent, "wide", 1))
    pieces = [coded_scatter(kept, arrived) for kept, arrived in zip(pieces, arrivals)]
    summed = jnp.concatenate(pieces, axis=1)
    summed = summed.reshape(narrow_count, local_rows, -1, HEAD_DIM)
    turned = exchange([summed[j] for j in range(narrow_count)], "narrow")
    turned = jnp.stack(by_rank(turned, flags), axis=1)
    q_heads = q_cols // HEAD_DIM
    k_heads = k_cols // HEAD_DIM
    query_rot = rotate(
        turned[:, :, :q_heads].reshape(local_rows, -1, HEAD_DIM), cache_len
    ).reshape(local_rows, -1)
    key_rot = rotate(
        turned[:, :, q_heads : q_heads + k_heads].reshape(local_rows, -1, HEAD_DIM), cache_len
    ).reshape(local_rows, -1)
    value_new = turned[:, :, q_heads + k_heads :].reshape(local_rows, -1)
    context = attend(query_rot, key_rot, value_new, key_cache, value_cache, cache_len)
    context = context.reshape(local_rows, narrow_count, -1)
    context = by_rank([context[:, j] for j in range(narrow_count)], flags)
    by_heads = exchange(context, "narrow")

    depth = w_out.shape[0] // CONTEXT_CHUNKS
    groups = []
    for chunk in range(CONTEXT_CHUNKS):
        columns = slice(chunk * depth, (chunk + 1) * depth)
        block = jnp.concatenate([piece[:, columns] for piece in by_heads], axis=0)
        groups.append(gather_pieces(block, "wide"))
    half = w_out.shape[1] // 2
    halves = [
        project(groups, to_hypothesis, False, [(w_out, 0, first, half)], 2)
        for first in (0, half)
    ]
    attn_out = jnp.concatenate([narrow_scatter(*sums) for sums in halves], axis=1)
    resid = (rows_in + attn_out).astype(jnp.bfloat16)
    resid_wide = resid.astype(jnp.float32)
    normed_two = normalized_rows(resid, ffn_gain)

    f_total = w_gate.shape[1]
    f_edge = int(f_total * FFN_SPLIT) // LANES * LANES
    total = None
    for first, last in ((0, f_edge), (f_edge, f_total)):
        f_cols = last - first
        segments = [(w_gate, 0, first, f_cols), (w_up, 0, first, f_cols)]
        sums = wide_scatter(*project([normed_two], to_wide, False, segments, 2, direct=True))
        act = (jax.nn.silu(sums[:, :f_cols]) * sums[:, f_cols:]).astype(jnp.bfloat16)
        total = project(
            [gather_in_two(act, "wide")],
            to_wide,
            True,
            [(w_down, first, 0, w_down.shape[1])],
            2 if last == f_total else 1,
            total if total is None else total[0],
        )
    ffn_out = narrow_scatter(*total)
    return (resid_wide + ffn_out).astype(jnp.bfloat16)


def solution(mesh):
    return jax.shard_map(
        shards,
        mesh=mesh,
        in_specs=(
            P("narrow", "wide"),
            P("wide"),
            P("wide", "narrow"),
            P("wide", "narrow"),
            P("wide", "narrow"),
            P("narrow", "wide"),
            P("wide"),
            P("wide", "narrow"),
            P("wide", "narrow"),
            P("narrow", "wide"),
            P(("wide", "narrow"), None, None),
            P(("wide", "narrow"), None, None),
            P(("wide", "narrow")),
            P(),
        ),
        out_specs=P("narrow", "wide"),
        check_vma=False,
    )
```

```python
import math

import jax
import jax.numpy as jnp
from jax import lax
from jax.experimental import pallas as pl
from jax.experimental.pallas import tpu as pltpu
from jax.sharding import PartitionSpec as P

HEAD_DIM = 128


NORM_EPSILON = 1e-05
ROPE_BASE = 500000.0


def product(left, right):
    return jnp.dot(left, right, preferred_element_type=jnp.float32)


def normalize(values_in, gain_row, sum_sq, model_width):
    mean_sq = sum_sq / model_width
    scaled = values_in.astype(jnp.float32) * lax.rsqrt(mean_sq + NORM_EPSILON)[:, None]
    return (scaled * gain_row[None, :]).astype(jnp.bfloat16)


def rotate(head_rows, lengths):
    head_size = head_rows.shape[-1]
    half_size = head_size // 2
    inverse_freq = jnp.exp(
        jnp.arange(half_size, dtype=jnp.float32) * (-2.0 * math.log(ROPE_BASE) / head_size)
    )
    angles = lengths.astype(jnp.float32)[:, None] * inverse_freq[None, :]
    cos_part = jnp.cos(angles)[:, None, :]
    sin_part = jnp.sin(angles)[:, None, :]
    front_half = head_rows[..., :half_size].astype(jnp.float32)
    back_half = head_rows[..., half_size:].astype(jnp.float32)
    turned = jnp.concatenate(
        [
            front_half * cos_part - back_half * sin_part,
            back_half * cos_part + front_half * sin_part,
        ],
        axis=-1,
    )
    return turned.astype(jnp.bfloat16)


def attend(queries, fresh_key, fresh_value, key_cache, value_cache, lengths):
    row_count, length, kv_width = key_cache.shape
    groups = kv_width // HEAD_DIM
    group_size = queries.shape[1] // kv_width
    score_scale = 1.0 / math.sqrt(HEAD_DIM)
    query_heads = queries.reshape(row_count, groups, group_size, HEAD_DIM)
    cache_keys = key_cache.reshape(row_count, length, groups, HEAD_DIM)
    cache_values = value_cache.reshape(row_count, length, groups, HEAD_DIM)
    own_key = fresh_key.reshape(row_count, groups, HEAD_DIM)
    own_value = fresh_value.reshape(row_count, groups, HEAD_DIM)
    scores = (
        jnp.einsum("rgqd,rlgd->rgql", query_heads, cache_keys, preferred_element_type=jnp.float32)
        * score_scale
    )
    own_score = (
        jnp.einsum("rgqd,rgd->rgq", query_heads, own_key, preferred_element_type=jnp.float32)
        * score_scale
    )
    valid_pos = jnp.arange(length, dtype=jnp.int32)[None, :] < lengths[:, None]
    scores = jnp.where(valid_pos[:, None, None, :], scores, -jnp.inf)
    row_max = jnp.maximum(jnp.max(scores, axis=3), own_score)
    weights = jnp.exp(scores - row_max[..., None])
    own_weight = jnp.exp(own_score - row_max)
    weight_sum = jnp.sum(weights, axis=3) + own_weight
    probs = (weights / weight_sum[..., None]).astype(jnp.bfloat16)
    own_prob = (own_weight / weight_sum).astype(jnp.bfloat16)
    context = jnp.einsum("rgql,rlgd->rgqd", probs, cache_values, preferred_element_type=jnp.float32)
    context = (
        context
        + own_prob.astype(jnp.float32)[..., None] * own_value.astype(jnp.float32)[:, :, None, :]
    )
    return context.reshape(row_count, groups * group_size * HEAD_DIM).astype(jnp.bfloat16)


QKV_CHUNKS = 3
FFN_SPLIT = 0.5
CONTEXT_CHUNKS = 2
NARROW_KINDS = [jnp.float32] + [jnp.bfloat16] * 8
TILE = 512
ROOM = 24
DIRECT_ROOM = 50
IN_FLIGHT = 9
LANES = 128
TOP_CODE = 32700.0
LOG_STEPS = 64.0
STAND_IN = 4
MIB = 1024 * 1024


def swap(block, axis, offset):
    count = lax.axis_size(axis)
    return lax.ppermute(block, axis, [(i, i ^ offset) for i in range(count)])


def strides_of(axis):
    count = lax.axis_size(axis)
    return [1 << bit for bit in range(count.bit_length() - 1)]


def offsets_of(axis):
    order = [0]
    for stride in reversed(strides_of(axis)):
        order = order + [offset ^ stride for offset in order]
    return order


def encoded(values):
    top = jnp.max(jnp.abs(values), axis=1, keepdims=True)
    steps = jnp.floor(jnp.log2(jnp.maximum(top, 1e-30)) * LOG_STEPS + 1.5)
    return jnp.round(values * (TOP_CODE * jnp.exp2(steps * (-1.0 / LOG_STEPS)))), steps


def write_codes(code_ref, place, values, steps_tile):
    codes, steps = encoded(values)
    code_ref[:, place * LANES : (place + 1) * LANES] = codes.astype(jnp.int32).astype(jnp.int16)
    lanes = lax.broadcasted_iota(jnp.int32, (values.shape[0], LANES), 1)
    return jnp.where(lanes == place, steps, steps_tile)


def read_codes(code_ref, place):
    codes = code_ref[:, place * LANES : (place + 1) * LANES]
    steps = code_ref[:, code_ref.shape[1] - LANES :].astype(jnp.int32).astype(jnp.float32)
    scale = jnp.exp2(steps[:, place : place + 1] * (1.0 / LOG_STEPS)) * (1.0 / TOP_CODE)
    return codes.astype(jnp.int32).astype(jnp.float32) * scale


def project(
    groups, order, turned, segments, split, total=None, direct=False, coded=False
):
    rows = order.shape[0]
    depth = groups[0][0].shape[1]
    tiles = []
    width = 0
    for index, (_, first_row, first, columns) in enumerate(segments):
        for start in range(first, first + columns, TILE):
            tile = min(TILE, first + columns - start)
            tiles.append((index, first_row, start, tile, width))
            width += tile
    part = rows // split
    pieces = [piece for group in groups for piece in group]
    count = len(pieces)
    each = count // len(groups)

    def body(*refs):
        piece_refs, order_ref, rest = refs[:count], refs[count], refs[count + 1 :]
        weight_refs, rest = rest[: len(segments)], rest[len(segments) :]
        if total is not None:
            total_ref, rest = rest[0], rest[1:]
        out_refs, rest = rest[:split], rest[split:]
        copies = []
        if direct:
            for place, (index, first_row, start, tile, _) in enumerate(tiles):
                source = weight_refs[index].at[pl.ds(first_row, depth), pl.ds(start, tile)]
                copies.append(pltpu.make_async_copy(source, rest[place], rest[-1].at[place]))
        for copy in copies[:IN_FLIGHT]:
            copy.start()
        lefts = []
        for group in range(len(groups)):
            group_refs = piece_refs[group * each : (group + 1) * each]
            left = lax.dot_general(
                order_ref[...],
                jnp.concatenate([ref[...] for ref in group_refs], axis=0),
                (((0 if turned else 1,), (0,)), ((), ())),
                preferred_element_type=jnp.float32,
            )
            lefts.append(left.astype(jnp.bfloat16))
        steps_tile = jnp.zeros((part, LANES), jnp.float32)
        for number, (index, first_row, start, tile, base) in enumerate(tiles):
            result = None
            for group, left in enumerate(lefts):
                if direct:
                    copies[number].wait()
                    weight = rest[number][...]
                    if number + IN_FLIGHT < len(tiles):
                        copies[number + IN_FLIGHT].start()
                else:
                    weight = weight_refs[index][
                        pl.ds(first_row + group * depth, depth), pl.ds(start, tile)
                    ]
                product = jnp.dot(left, weight, preferred_element_type=jnp.float32)
                result = product if result is None else result + product
            if total is not None:
                result = result + total_ref[:, base : base + tile]
            for place, out_ref in enumerate(out_refs[: 1 if coded else split]):
                out_ref[:, base : base + tile] = result[place * part : (place + 1) * part]
            if coded:
                for column in range(0, tile, LANES):
                    values = result[part:, column : column + LANES]
                    place = (base + column) // LANES
                    steps_tile = write_codes(out_refs[1], place, values, steps_tile)
        if coded:
            out_refs[1][:, width:] = steps_tile.astype(jnp.int32).astype(jnp.int16)

    operands = pieces + [order] + [segment[0] for segment in segments]
    if total is not None:
        operands.append(total)
    in_vmem = pl.BlockSpec(memory_space=pltpu.VMEM)
    specs = [in_vmem] * len(operands)
    out_shape = [jax.ShapeDtypeStruct((part, width), jnp.float32)] * split
    if coded:
        out_shape[1] = jax.ShapeDtypeStruct((part, width + LANES), jnp.int16)
    scratch = []
    if direct:
        for place in range(count + 1, count + 1 + len(segments)):
            specs[place] = pl.BlockSpec(memory_space=pltpu.HBM)
        scratch = [pltpu.VMEM((depth, tile[3]), jnp.bfloat16) for tile in tiles]
        scratch.append(pltpu.SemaphoreType.DMA((len(tiles),)))
    return pl.pallas_call(
        body,
        in_specs=specs,
        out_specs=[in_vmem] * split,
        scratch_shapes=scratch,
        out_shape=out_shape,
        compiler_params=pltpu.CompilerParams(vmem_limit_bytes=(DIRECT_ROOM if direct else ROOM) * MIB),
        cost_estimate=pl.CostEstimate(
            flops=2 * rows * len(groups) * depth * (width + rows),
            bytes_accessed=2 * len(groups) * depth * width + 4 * rows * width,
            transcendentals=0,
        ),
    )(*operands)


def stand_in(array):
    def body(array_ref, copy_ref):
        copy_ref[...] = array_ref[...]

    in_vmem = pl.BlockSpec(memory_space=pltpu.VMEM)
    return pl.pallas_call(
        body,
        in_specs=[in_vmem],
        out_specs=in_vmem,
        out_shape=jax.ShapeDtypeStruct(array.shape, array.dtype),
        compiler_params=pltpu.CompilerParams(vmem_limit_bytes=MIB),
        cost_estimate=pl.CostEstimate(
            flops=int(1.1e9 * STAND_IN), bytes_accessed=4096, transcendentals=0
        ),
    )(array)


def fold(kept, arrived, blocks):
    rows = kept.shape[0] // blocks
    width = kept.shape[1]

    def body(kept_ref, arrived_ref, own_ref, *code_refs):
        tiles = [jnp.zeros((rows, LANES), jnp.float32)] * (blocks - 1)
        for place in range(width // LANES):
            columns = slice(place * LANES, (place + 1) * LANES)
            sums = kept_ref[:, columns] + read_codes(arrived_ref, place)
            own_ref[:, columns] = sums[:rows]
            for index, code_ref in enumerate(code_refs):
                values = sums[(index + 1) * rows : (index + 2) * rows]
                tiles[index] = write_codes(code_ref, place, values, tiles[index])
        for tile, code_ref in zip(tiles, code_refs):
            code_ref[:, width:] = tile.astype(jnp.int32).astype(jnp.int16)

    codes = jax.ShapeDtypeStruct((rows, width + LANES), jnp.int16)
    return pl.pallas_call(
        body,
        out_shape=[jax.ShapeDtypeStruct((rows, width), jnp.float32)] + [codes] * (blocks - 1),
        compiler_params=pltpu.CompilerParams(vmem_limit_bytes=8 * MIB),
    )(kept, arrived)


def add_codes(own, arrived):
    def body(own_ref, *refs):
        for place in range(own.shape[1] // LANES):
            columns = slice(place * LANES, (place + 1) * LANES)
            sums = own_ref[:, columns]
            for code_ref in refs[:-1]:
                sums = sums + read_codes(code_ref, place)
            refs[-1][:, columns] = sums.astype(jnp.bfloat16)

    return pl.pallas_call(
        body,
        out_shape=jax.ShapeDtypeStruct(own.shape, jnp.bfloat16),
        compiler_params=pltpu.CompilerParams(vmem_limit_bytes=8 * MIB),
    )(own, *arrived)


def coded_scatter(kept, arrived):
    for stride in strides_of("wide")[1:]:
        kept, codes = fold(kept, arrived, 2)
        arrived = swap(codes, "wide", stride)
    return add_codes(kept, [arrived])


def wide_scatter(kept, sent):
    rows = 2 * kept.shape[0] // lax.axis_size("wide")
    kept = kept + swap(sent.astype(jnp.float16), "wide", 1).astype(jnp.float32)
    total = kept[:rows]
    for place, offset in enumerate(offsets_of("wide")[: kept.shape[0] // rows]):
        if offset:
            block = kept[place * rows : (place + 1) * rows].astype(jnp.float16)
            total = total + swap(block, "wide", offset).astype(jnp.float32)
    return total


def narrow_scatter(kept, sent):
    for stride, kind in zip(strides_of("narrow"), NARROW_KINDS):
        if stride > 1:
            half = kept.shape[0] // 2
            kept, sent = kept[:half], kept[half:]
        kept = kept + swap(sent.astype(kind), "narrow", stride).astype(jnp.float32)
    return kept


def gather(block, axis):
    strides = strides_of(axis)[::-1]
    for stride in strides[:-1]:
        block = jnp.concatenate([block, swap(block, axis, stride)], axis=0)
    return [block, swap(block, axis, strides[-1])]


def gather_in_two(block, axis):
    offsets = offsets_of(axis)
    far = [swap(block, axis, offset) for offset in offsets[1 : len(offsets) // 2]]
    block = jnp.concatenate([stand_in(block)] + far, axis=0)
    return [block, swap(block, axis, 1)]


def gather_pieces(block, axis):
    held = [block]
    for stride in strides_of(axis)[::-1]:
        held = held + [swap(piece, axis, stride) for piece in held]
    return [stand_in(block)] + held[1:]


def exchange(blocks, axis):
    blocks = list(blocks)
    for stride in strides_of(axis)[::-1]:
        marked = [i for i in range(len(blocks)) if i & stride]
        arrived = swap(jnp.stack([blocks[i] for i in marked]), axis, stride)
        for place, i in enumerate(marked):
            blocks[i] = arrived[place]
    return blocks


def by_rank(blocks, flags):
    for bit, flag in enumerate(flags):
        other = 1 << bit
        blocks = [jnp.where(flag, blocks[i ^ other], block) for i, block in enumerate(blocks)]
    return blocks


def shards(
    hidden_in,
    attn_gain,
    w_query,
    w_key,
    w_value,
    w_out,
    ffn_gain,
    w_gate,
    w_up,
    w_down,
    key_cache,
    value_cache,
    cache_len,
    bank_row,
):
    wide_count = lax.axis_size("wide")
    narrow_count = lax.axis_size("narrow")
    me_wide = lax.axis_index("wide")
    me_narrow = lax.axis_index("narrow")
    flags = [(me_narrow & stride) != 0 for stride in strides_of("narrow")]
    hidden_in, me_wide, me_narrow, flags = lax.optimization_barrier(
        (hidden_in, me_wide, me_narrow, flags)
    )
    model_width = hidden_in.shape[1] * wide_count
    own_rows = hidden_in.shape[0]
    local_rows = cache_len.shape[0]
    all_rows = bank_row.shape[0]
    wide_rows = all_rows // wide_count

    def device(block, axis, me):
        bits = len(strides_of(axis))
        for bit in range(bits):
            me = me ^ (((block >> bit) & 1) << (bits - 1 - bit))
        return me

    def hypothesis(place):
        return device(place // own_rows, "narrow", me_narrow) * own_rows + place % own_rows

    def wide_row(place):
        return device(place // wide_rows, "wide", me_wide) * wide_rows + place % wide_rows

    def bank(place):
        inner = place % wide_rows
        owner = device(place // wide_rows, "wide", me_wide) * narrow_count
        owner = owner + (me_narrow ^ (inner // local_rows))
        return owner * local_rows + inner % local_rows

    down = lax.broadcasted_iota(jnp.int32, (all_rows, all_rows), 0)
    across = lax.broadcasted_iota(jnp.int32, (all_rows, all_rows), 1)
    banks = jnp.broadcast_to(bank_row[None, :], (all_rows, all_rows))
    hypothesis_bank = jnp.sum(
        jnp.where(hypothesis(down) == across, banks, 0), axis=1, keepdims=True
    )
    to_hypothesis = (hypothesis_bank == bank(across)).astype(jnp.bfloat16)
    to_wide = (wide_row(down) == across).astype(jnp.bfloat16)

    def normalized_rows(values, gain_row):
        wide_values = values.astype(jnp.float32)
        rows_sq = jnp.sum(wide_values * wide_values, axis=1)
        sent = jnp.broadcast_to(rows_sq[None, :], (wide_count * narrow_count, own_rows))
        landed = lax.all_to_all(sent, ("wide", "narrow"), 0, 0, tiled=True)
        pieces = gather(values, "narrow")
        sums = jnp.sum(landed.reshape(wide_count, narrow_count, own_rows), axis=0)
        sums = by_rank([sums[j] for j in range(narrow_count)], flags)
        order = offsets_of("narrow")
        half = narrow_count // 2
        result = []
        for piece, offsets in zip(pieces, (order[:half], order[half:])):
            sum_sq = jnp.concatenate([sums[offset] for offset in offsets])
            result.append(normalize(piece, gain_row, sum_sq, model_width))
        return result

    rows_in = hidden_in.astype(jnp.float32)
    normed = normalized_rows(hidden_in, attn_gain)

    q_cols = w_query.shape[1]
    k_cols = w_key.shape[1]
    stacked = [(w_query, q_cols), (w_key, k_cols), (w_value, k_cols)]
    heads = (q_cols + 2 * k_cols) // HEAD_DIM
    edges = [heads * chunk // QKV_CHUNKS for chunk in range(QKV_CHUNKS)] + [heads]
    pieces = []
    arrivals = []
    ordered = to_hypothesis
    for chunk in range(QKV_CHUNKS):
        first, last = edges[chunk] * HEAD_DIM, edges[chunk + 1] * HEAD_DIM
        segments = []
        start = 0
        for weight, columns in stacked:
            low, high = max(first, start), min(last, start + columns)
            if low < high:
                segments.append((weight, 0, low - start, high - low))
            start += columns
        if chunk >= 2:
            ordered, arrivals[chunk - 2] = lax.optimization_barrier((ordered, arrivals[chunk - 2]))
        (kept, sent), ordered = lax.optimization_barrier(
            (project([normed], ordered, True, segments, 2, direct=True, coded=True), ordered)
        )
        pieces.append(kept)
        arrivals.append(swap(sent, "wide", 1))
    pieces = [coded_scatter(kept, arrived) for kept, arrived in zip(pieces, arrivals)]
    summed = jnp.concatenate(pieces, axis=1)
    summed = summed.reshape(narrow_count, local_rows, -1, HEAD_DIM)
    turned = exchange([summed[j] for j in range(narrow_count)], "narrow")
    turned = jnp.stack(by_rank(turned, flags), axis=1)
    q_heads = q_cols // HEAD_DIM
    k_heads = k_cols // HEAD_DIM
    query_rot = rotate(
        turned[:, :, :q_heads].reshape(local_rows, -1, HEAD_DIM), cache_len
    ).reshape(local_rows, -1)
    key_rot = rotate(
        turned[:, :, q_heads : q_heads + k_heads].reshape(local_rows, -1, HEAD_DIM), cache_len
    ).reshape(local_rows, -1)
    value_new = turned[:, :, q_heads + k_heads :].reshape(local_rows, -1)
    context = attend(query_rot, key_rot, value_new, key_cache, value_cache, cache_len)
    context = context.reshape(local_rows, narrow_count, -1)
    context = by_rank([context[:, j] for j in range(narrow_count)], flags)
    by_heads = exchange(context, "narrow")

    depth = w_out.shape[0] // CONTEXT_CHUNKS
    groups = []
    for chunk in range(CONTEXT_CHUNKS):
        columns = slice(chunk * depth, (chunk + 1) * depth)
        block = jnp.concatenate([piece[:, columns] for piece in by_heads], axis=0)
        groups.append(gather_pieces(block, "wide"))
    half = w_out.shape[1] // 2
    halves = [
        project(groups, to_hypothesis, False, [(w_out, 0, first, half)], 2)
        for first in (0, half)
    ]
    attn_out = jnp.concatenate([narrow_scatter(*sums) for sums in halves], axis=1)
    resid = (rows_in + attn_out).astype(jnp.bfloat16)
    resid_wide = resid.astype(jnp.float32)
    normed_two = normalized_rows(resid, ffn_gain)

    f_total = w_gate.shape[1]
    f_edge = int(f_total * FFN_SPLIT) // LANES * LANES
    total = [None, None]
    for first, last in ((0, f_edge), (f_edge, f_total)):
        f_cols = last - first
        segments = [(w_gate, 0, first, f_cols), (w_up, 0, first, f_cols)]
        sums = wide_scatter(*project([normed_two], to_wide, False, segments, 2, direct=True))
        act = (jax.nn.silu(sums[:, :f_cols]) * sums[:, f_cols:]).astype(jnp.bfloat16)
        gathered = gather_in_two(act, "wide")
        half = w_down.shape[1] // 2
        total = [
            project(
                [gathered],
                to_wide,
                True,
                [(w_down, first, place * half, half)],
                2 if last == f_total else 1,
                earlier if earlier is None else earlier[0],
            )
            for place, earlier in enumerate(total)
        ]
    ffn_out = jnp.concatenate([narrow_scatter(*sums) for sums in total], axis=1)
    return (resid_wide + ffn_out).astype(jnp.bfloat16)


def solution(mesh):
    return jax.shard_map(
        shards,
        mesh=mesh,
        in_specs=(
            P("narrow", "wide"),
            P("wide"),
            P("wide", "narrow"),
            P("wide", "narrow"),
            P("wide", "narrow"),
            P("narrow", "wide"),
            P("wide"),
            P("wide", "narrow"),
            P("wide", "narrow"),
            P("narrow", "wide"),
            P(("wide", "narrow"), None, None),
            P(("wide", "narrow"), None, None),
            P(("wide", "narrow")),
            P(),
        ),
        out_specs=P("narrow", "wide"),
        check_vma=False,
    )
```
